32 devices in a mesh: ctx: 16 (over z, y, core), fsdp: 2 (over x).
Axes of the slice: x: 2, y: 2, z: 4, core: 2. Of those that a mesh axis runs over, the one named last changes fastest.
Arguments:
- tokens: bfloat16 [2048, 16384], P(('ctx', 'fsdp')), may hold values from -64 to 64
- queries: bfloat16 [2048, 2048], P(('ctx', 'fsdp')), may hold values from -192 to 192, as said below
- key_weight: bfloat16 [16384, 128], P('fsdp'), may hold values from -0.046875 to 0.046875
- value_weight: bfloat16 [16384, 128], P('fsdp'), may hold values from -0.046875 to 0.046875
Outputs:
- kv_cache: bfloat16 [2048, 256], P(('ctx', 'fsdp'))
- attended: bfloat16 [2048, 2048], P(('ctx', 'fsdp'))
The draws below stay inside these ranges and needn't reach their ends.
Inputs may be any that keep to these rules, and one draw needn't show every extreme that they name: `queries`: query projections of the same tokens, 16 heads of 128 features each.
All inputs are finite; a program needn't handle non-finite values.
Results may differ from the reference program's by a relative error of at most 0.011.
Values may be sent and summed in bfloat16 or wider, within the bound.
No kernel may reach another device: no remote copies, remote signals or barrier semaphores. Data moves between devices by JAX's collectives and lax.ppermute only.
A program may use at most 64 MiB of HBM per device.

```python
import math
import jax
import jax.numpy as jnp
from jax import lax

D = 16384
HS = 128
QH = 16
TOKENS = 2048


def spread_scales(key, shape, lowest, highest):
    return jnp.exp(jax.random.uniform(key, shape, jnp.float32, math.log(lowest), math.log(highest)))


def draw_tokens(key, part):
    key = jax.random.fold_in(key, 11)
    base_key, row_key, column_key = jax.random.split(key, 3)
    base_value = jnp.clip(jax.random.normal(base_key, (TOKENS, D), jnp.float32), -6.0, 6.0)
    row_scale = spread_scales(row_key, (TOKENS, 1), 0.9, 1.1)
    column_scale = spread_scales(column_key, (1, D), 0.3, 3.0)
    return (base_value * row_scale * column_scale).astype(jnp.bfloat16)


def draw_queries(key, part):
    key = jax.random.fold_in(key, 23)
    base_key, scale_key = jax.random.split(key, 2)
    base_value = jnp.clip(jax.random.normal(base_key, (TOKENS, QH, HS), jnp.float32), -6.0, 6.0)
    head_scale = spread_scales(scale_key, (TOKENS, QH, 1), 1.0, 3.0)
    return (base_value * head_scale).reshape(TOKENS, QH * HS).astype(jnp.bfloat16)


def steps_of(key, dims, pieces, smallest, high):
    loudness = 1.0
    for position, parts in pieces:
        heights = jax.random.uniform(jax.random.fold_in(jax.random.fold_in(key, 6), position), (parts,), jnp.float32, smallest / len(pieces), high / len(pieces))
        loudness = loudness * jnp.repeat(jnp.exp(heights), dims[position] // parts).reshape((-1,) + (1,) * (len(dims) - 1 - position))
    return loudness


def scatter_about(own_key, shape, spread, reach, shards=(), held_as=jnp.bfloat16):
    loudness = steps_of(own_key, shape, shards, -0.22, 0.18) if shards else 1.0
    array = jax.random.normal(own_key, shape, jnp.float32) * spread * loudness
    return jnp.minimum(jnp.maximum(array, -reach), reach).astype(held_as)


def setup_inputs(seed: int = 0) -> dict:
    key_list = jax.random.split(jax.random.key(seed), 5)
    tokens = draw_tokens(jax.random.fold_in(key_list[4], 71), 0)
    queries = draw_queries(jax.random.fold_in(key_list[4], 71), 0)
    key_weight = scatter_about(key_list[2], (D, HS), D ** -0.5, 0.046875, ((0, 2),))
    value_weight = scatter_about(key_list[3], (D, HS), D ** -0.5, 0.046875, ((0, 2),))
    return {"tokens": tokens, "queries": queries, "key_weight": key_weight, "value_weight": value_weight}


rope_base = 500000.0


def rotate(vectors, cosine, sine_table):
    middle = vectors.shape[-1] // 2
    leading = vectors[..., :middle]
    back_half = vectors[..., middle:]
    return jnp.concatenate([leading * cosine - back_half * sine_table, back_half * cosine + leading * sine_table], axis=-1)


def tables(positions, head_size):
    middle = head_size // 2
    frequency = rope_base ** (-jnp.arange(middle, dtype=jnp.float32) * 2.0 / head_size)
    angles = positions.astype(jnp.float32)[:, None] * frequency[None, :]
    return jnp.cos(angles), jnp.sin(angles)


def reference(tokens, queries, key_weight, value_weight):
    total_rows = tokens.shape[0]
    head_count = queries.shape[1] // HS
    score_scale = HS ** -0.5
    key_raw = jnp.dot(tokens, key_weight, preferred_element_type=jnp.float32)
    value_raw = jnp.dot(tokens, value_weight, preferred_element_type=jnp.float32)
    positions = jnp.arange(total_rows, dtype=jnp.int32)
    cosine, sine_table = tables(positions, HS)
    keys_rot = rotate(key_raw, cosine, sine_table).astype(jnp.bfloat16)
    values_cast = value_raw.astype(jnp.bfloat16)
    kv_cache = jnp.concatenate([keys_rot, values_cast], axis=1)
    rotated = rotate(queries.astype(jnp.float32).reshape(total_rows, head_count, HS), cosine[:, None, :], sine_table[:, None, :]).astype(jnp.bfloat16)
    block_rows = math.gcd(total_rows, 256)

    def one_block(block_number):
        row_start = block_number * block_rows
        query_flat = lax.dynamic_slice_in_dim(rotated, row_start, block_rows, 0).reshape(block_rows * head_count, HS)
        query_pos = row_start + jnp.arange(block_rows * head_count, dtype=jnp.int32) // head_count
        scores = lax.dot_general(query_flat, keys_rot, (((1,), (1,)), ((), ())), preferred_element_type=jnp.float32) * score_scale
        allowed = positions[None, :] <= query_pos[:, None]
        peak = jnp.max(jnp.where(allowed, scores, -jnp.inf), axis=1, keepdims=True)
        weights = jnp.where(allowed, jnp.exp(scores - peak), 0.0)
        denominator = jnp.sum(weights, axis=1, keepdims=True)
        mixed = jnp.dot(weights.astype(jnp.bfloat16), values_cast, preferred_element_type=jnp.float32) / denominator
        return mixed.reshape(block_rows, head_count * HS).astype(jnp.bfloat16)

    attended = lax.map(one_block, jnp.arange(total_rows // block_rows, dtype=jnp.int32))
    return kv_cache, attended.reshape(total_rows, head_count * HS)
```

```python
from functools import partial
import math

import jax
import jax.numpy as jnp
from jax import lax
from jax.experimental import pallas as pl
from jax.experimental.pallas import tpu as pltpu
from jax.sharding import PartitionSpec as P

rope_base = 500000.0
floor_value = -1e30


def rotate(vectors, cosine, sine_table):
    middle = vectors.shape[-1] // 2
    leading = vectors[..., :middle]
    back_half = vectors[..., middle:]
    return jnp.concatenate(
        [leading * cosine - back_half * sine_table, back_half * cosine + leading * sine_table],
        axis=-1,
    )


def tables(positions, head_size):
    middle = head_size // 2
    frequency = rope_base ** (-jnp.arange(middle, dtype=jnp.float32) * 2.0 / head_size)
    angles = positions.astype(jnp.float32)[:, None] * frequency[None, :]
    return (jnp.cos(angles), jnp.sin(angles))


def attention_kernel(
    place_ref, query_ref, *refs, masks, rows, group_rows, head_size, heads, heads_at_once
):
    pieces, out_ref = refs[:-1], refs[-1]
    place = place_ref[0]
    shift = place_ref[1]
    factor = head_size ** (-0.5) * math.log2(math.e)
    chunk = rows * heads_at_once
    contract_last = (((1,), (1,)), ((), ()))
    query_pos = shift + lax.rem(
        lax.broadcasted_iota(jnp.int32, (chunk, group_rows), 0), jnp.int32(rows)
    )
    key_pos = lax.broadcasted_iota(jnp.int32, (chunk, group_rows), 1)
    diagonal = key_pos <= query_pos

    for part in range(heads // heads_at_once):
        query = query_ref[part * chunk : (part + 1) * chunk, :]
        scores = []
        values = []
        for piece, piece_masks in zip(pieces, masks):
            raw = (
                lax.dot_general(
                    query,
                    piece[:, :head_size],
                    contract_last,
                    preferred_element_type=jnp.float32,
                )
                * factor
            )
            for slot, mask in enumerate(piece_masks):
                block = raw[:, slot * group_rows : (slot + 1) * group_rows]
                if mask == 0:
                    block = jnp.where(diagonal, block, floor_value)
                else:
                    bias = jnp.where((place ^ mask) < place, 0.0, floor_value).astype(jnp.float32)
                    block = block + bias
                scores.append(block)
                values.append(piece[slot * group_rows : (slot + 1) * group_rows, head_size:])
        peak = scores[0]
        for block in scores[1:]:
            peak = jnp.maximum(peak, block)
        peak = jnp.max(peak, axis=1, keepdims=True)
        weights = [jnp.exp2(block - peak) for block in scores]
        total = weights[0]
        for block in weights[1:]:
            total = total + block
        denominator = jnp.sum(total, axis=1, keepdims=True)
        numerator = jnp.dot(
            jnp.concatenate([block.astype(jnp.bfloat16) for block in weights], axis=1),
            jnp.concatenate(values, axis=0),
            preferred_element_type=jnp.float32,
        )
        result = (numerator / denominator).astype(out_ref.dtype)
        for head in range(heads_at_once):
            column = (part * heads_at_once + head) * head_size
            out_ref[:, column : column + head_size] = result[head * rows : (head + 1) * rows, :]


def attend(place, query_flat, pieces, masks, rows, group_rows, head_size):
    heads = query_flat.shape[0] // rows
    heads_at_once = math.gcd(heads, 4)
    keys = sum(piece.shape[0] for piece in pieces)
    whole = pl.BlockSpec(memory_space=pltpu.VMEM)
    return pl.pallas_call(
        partial(
            attention_kernel,
            masks=masks,
            rows=rows,
            group_rows=group_rows,
            head_size=head_size,
            heads=heads,
            heads_at_once=heads_at_once,
        ),
        out_shape=jax.ShapeDtypeStruct((rows, heads * head_size), jnp.bfloat16),
        in_specs=[pl.BlockSpec(memory_space=pltpu.SMEM), whole] + [whole] * len(pieces),
        out_specs=whole,
        compiler_params=pltpu.CompilerParams(vmem_limit_bytes=48 * 1024 * 1024),
        cost_estimate=pl.CostEstimate(
            flops=4 * heads * rows * keys * head_size,
            bytes_accessed=4 * heads * rows * head_size + 4 * keys * head_size,
            transcendentals=heads * rows * keys,
        ),
        name="attend",
    )(place, query_flat, *pieces)


def make_local(contexts, shards):
    def local(tokens, queries, key_weight, value_weight):
        rows = tokens.shape[0]
        depth, head_size = key_weight.shape
        heads = queries.shape[1] // head_size
        group_rows = shards * rows
        context = lax.axis_index("ctx")
        shard = lax.axis_index("fsdp")

        received = [None] * shards
        for step in range(1, shards):
            target = lax.rem(shard + step, shards)
            columns = lax.dynamic_slice_in_dim(tokens, target * depth, depth, 1)
            received[step] = lax.ppermute(
                columns, "fsdp", [(i, (i + step) % shards) for i in range(shards)]
            )
        received[0] = lax.dynamic_slice_in_dim(tokens, shard * depth, depth, 1)

        positions = context * group_rows + jnp.arange(group_rows, dtype=jnp.int32)
        cosine, sine_table = tables(positions, head_size)
        own_cosine = lax.dynamic_slice_in_dim(cosine, shard * rows, rows, 0)
        own_sine = lax.dynamic_slice_in_dim(sine_table, shard * rows, rows, 0)
        by_head = queries.astype(jnp.float32).reshape(rows, heads, head_size).transpose(1, 0, 2)
        query_flat = (
            rotate(by_head, own_cosine[None], own_sine[None])
            .astype(jnp.bfloat16)
            .reshape(heads * rows, head_size)
        )

        products = []
        for columns in received:
            products.append(
                jnp.concatenate(
                    [
                        jnp.dot(columns, key_weight, preferred_element_type=jnp.float32),
                        jnp.dot(columns, value_weight, preferred_element_type=jnp.float32),
                    ],
                    axis=1,
                )
            )
        if shards == 2:
            ordered = [
                jnp.where(shard == 0, products[0], products[1]),
                jnp.where(shard == 0, products[1], products[0]),
            ]
            partial_sums = jnp.concatenate(ordered, axis=0)
        else:
            partial_sums = jnp.zeros((group_rows, 2 * head_size), jnp.float32)
            for step in range(shards):
                source = lax.rem(shard + shards - step, shards)
                partial_sums = lax.dynamic_update_slice_in_dim(
                    partial_sums, products[step], source * rows, 0
                )
        reach = 1
        while reach < shards:
            partial_sums = partial_sums + lax.ppermute(
                partial_sums, "fsdp", [(i, i ^ reach) for i in range(shards)]
            )
            reach *= 2

        keys_rot = rotate(partial_sums[:, :head_size], cosine, sine_table).astype(jnp.bfloat16)
        group = jnp.concatenate([keys_rot, partial_sums[:, head_size:].astype(jnp.bfloat16)], axis=1)
        kv_cache = lax.dynamic_slice_in_dim(group, shard * rows, rows, 0)

        pieces, masks = [group], [[0]]
        reach = contexts // 2
        order = []
        while reach > 1:
            order.append(reach)
            reach //= 2
        if contexts > 1:
            order.append(1)
        for bit in order:
            known = jnp.concatenate(pieces, axis=0) if len(pieces) > 1 else pieces[0]
            known_masks = [mask for piece_masks in masks for mask in piece_masks]
            pieces.append(lax.ppermute(known, "ctx", [(i, i ^ bit) for i in range(contexts)]))
            masks.append([mask ^ bit for mask in known_masks])

        place = jnp.stack([context, shard * rows]).astype(jnp.int32)
        attended = attend(place, query_flat, pieces, masks, rows, group_rows, head_size)
        return (kv_cache, attended)

    return local


def solution(mesh):
    placed = (P(("ctx", "fsdp"), None), P(("ctx", "fsdp"), None), P("fsdp", None), P("fsdp", None))
    return jax.shard_map(
        make_local(mesh.shape["ctx"], mesh.shape["fsdp"]),
        mesh=mesh,
        in_specs=placed,
        out_specs=(P(("ctx", "fsdp"), None), P(("ctx", "fsdp"), None)),
        check_vma=False,
    )
```

```python
from functools import partial
import math

import jax
import jax.numpy as jnp
from jax import lax
from jax.experimental import pallas as pl
from jax.experimental.pallas import tpu as pltpu
from jax.sharding import PartitionSpec as P

rope_base = 500000.0
floor_value = -1e30


def rotate(vectors, cosine, sine_table):
    middle = vectors.shape[-1] // 2
    leading = vectors[..., :middle]
    back_half = vectors[..., middle:]
    return jnp.concatenate(
        [leading * cosine - back_half * sine_table, back_half * cosine + leading * sine_table],
        axis=-1,
    )


def tables(positions, head_size):
    middle = head_size // 2
    frequency = rope_base ** (-jnp.arange(middle, dtype=jnp.float32) * 2.0 / head_size)
    angles = positions.astype(jnp.float32)[:, None] * frequency[None, :]
    return (jnp.cos(angles), jnp.sin(angles))


def attention_kernel(
    span_ref, place_ref, query_ref, *refs, count, carry, final, rows, own, head_size, stride
):
    pieces, refs = refs[:count], refs[count:]
    if carry:
        old_peak, old_total, old_sum = refs[:3]
        refs = refs[3:]
    start = span_ref[0]
    first = span_ref[1]
    factor = head_size ** (-0.5) * math.log2(math.e)
    flat = query_ref.shape[0]
    keys = jnp.concatenate([piece[:, :head_size] for piece in pieces], axis=0)
    values = jnp.concatenate([piece[:, head_size:] for piece in pieces], axis=0)
    width = keys.shape[0]
    edge = min(width, -(-own // 128) * 128)
    query_pos = first + lax.rem(
        lax.broadcasted_iota(jnp.int32, (stride, edge), 0), jnp.int32(rows)
    )
    diagonal = place_ref[:, :edge] <= query_pos
    bias = jnp.where(place_ref[...] < start, 0.0, floor_value).astype(jnp.float32)

    def one(part):
        place = pl.ds(pl.multiple_of(part * stride, stride), stride)
        scores = (
            lax.dot_general(
                query_ref[place, :],
                keys,
                (((1,), (1,)), ((), ())),
                preferred_element_type=jnp.float32,
            )
            * factor
        )
        masked = jnp.where(diagonal, scores[:, :edge], floor_value)
        if edge < width:
            masked = jnp.concatenate([masked, scores[:, edge:] + bias[:, edge:]], axis=1)
        peak = jnp.max(masked, axis=1, keepdims=True)
        if carry:
            peak = jnp.maximum(peak, old_peak[place, :])
        weights = jnp.exp2(masked - peak)
        total = jnp.sum(weights, axis=1, keepdims=True)
        numerator = jnp.dot(
            weights.astype(jnp.bfloat16), values, preferred_element_type=jnp.float32
        )
        if carry:
            shrink = jnp.exp2(old_peak[place, :] - peak)
            total = total + shrink * old_total[place, :]
            numerator = numerator + shrink * old_sum[place, :]
        if final:
            out_ref, scratch = refs
            scratch[place, :] = (numerator / total).astype(jnp.bfloat16)
        else:
            peak_ref, total_ref, sum_ref = refs
            peak_ref[place, :] = peak
            total_ref[place, :] = total
            sum_ref[place, :] = numerator

    if width <= 2048:
        for part in range(flat // stride):
            one(part)
    else:

        @pl.loop(0, flat // stride)
        def each(part):
            one(part)

    if final:
        out_ref, scratch = refs
        for head in range(flat // rows):
            out_ref[:, head * head_size : (head + 1) * head_size] = scratch[
                head * rows : (head + 1) * rows, :
            ]


def attend(span, place, query_flat, pieces, state, final, rows):
    flat, head_size = query_flat.shape
    width = sum(piece.shape[0] for piece in pieces)
    stride = math.gcd(flat, 256 if width <= 2048 else rows)
    whole = pl.BlockSpec(memory_space=pltpu.VMEM)
    if final:
        shapes = jax.ShapeDtypeStruct((rows, flat // rows * head_size), jnp.bfloat16)
        out_specs, scratch = whole, [pltpu.VMEM((flat, head_size), jnp.bfloat16)]
    else:
        shapes = [
            jax.ShapeDtypeStruct((flat, 1), jnp.float32),
            jax.ShapeDtypeStruct((flat, 1), jnp.float32),
            jax.ShapeDtypeStruct((flat, head_size), jnp.float32),
        ]
        out_specs, scratch = [whole] * 3, []
    return pl.pallas_call(
        partial(
            attention_kernel,
            count=len(pieces),
            carry=state is not None,
            final=final,
            rows=rows,
            own=pieces[0].shape[0],
            head_size=head_size,
            stride=stride,
        ),
        out_shape=shapes,
        in_specs=[pl.BlockSpec(memory_space=pltpu.SMEM)]
        + [whole] * (2 + len(pieces) + (0 if state is None else 3)),
        out_specs=out_specs,
        scratch_shapes=scratch,
        compiler_params=pltpu.CompilerParams(vmem_limit_bytes=40 * 1024 * 1024),
        cost_estimate=pl.CostEstimate(
            flops=4 * flat * width * head_size,
            bytes_accessed=4 * flat * head_size + 4 * width * head_size,
            transcendentals=flat * width,
        ),
        name="attend_last" if final else "attend_part",
    )(span, place, query_flat, *pieces, *(() if state is None else state))


def stages_of(contexts):
    bits = []
    bit = contexts // 2
    while bit >= 1:
        bits.append(bit)
        bit //= 2
    core = bits[-1:]
    rest = bits[:-1]
    stages = [rest[i : i + 2] for i in range(0, len(rest), 2)] + ([core] if core else [])
    return stages


def spread(block, contexts):
    pieces, masks = [block], [[0]]
    for stage in stages_of(contexts):
        known = jnp.concatenate(pieces, axis=0) if len(pieces) > 1 else pieces[0]
        known_masks = [mask for piece_masks in masks for mask in piece_masks]
        moves = [0]
        for bit in stage:
            moves = moves + [move ^ bit for move in moves]
        for move in moves[1:]:
            pieces.append(lax.ppermute(known, "ctx", [(i, i ^ move) for i in range(contexts)]))
            masks.append([mask ^ move for mask in known_masks])
    return pieces, masks


def make_local(contexts, shards, parts):
    def local(tokens, queries, key_weight, value_weight):
        rows = tokens.shape[0]
        depth, head_size = key_weight.shape
        heads = queries.shape[1] // head_size
        group_rows = shards * rows
        part_rows = rows // parts
        context = lax.axis_index("ctx")
        shard = lax.axis_index("fsdp")

        received = []
        for part in range(parts):
            top = part * part_rows
            arrived = []
            for step in range(1, shards):
                target = lax.rem(shard + step, shards)
                columns = lax.dynamic_slice(
                    tokens, (jnp.int32(top), target * depth), (part_rows, depth)
                )
                arrived.append(
                    lax.ppermute(
                        columns, "fsdp", [(i, (i + step) % shards) for i in range(shards)]
                    )
                )
            received.append(arrived)
        own_columns = lax.dynamic_slice_in_dim(tokens, shard * depth, depth, 1)

        def project(columns):
            return jnp.concatenate(
                [
                    jnp.dot(columns, key_weight, preferred_element_type=jnp.float32),
                    jnp.dot(columns, value_weight, preferred_element_type=jnp.float32),
                ],
                axis=1,
            )

        own_product = project(own_columns)

        start = context * group_rows
        positions = start + jnp.arange(group_rows, dtype=jnp.int32)
        cosine, sine_table = tables(positions, head_size)
        own_cosine = lax.dynamic_slice_in_dim(cosine, shard * rows, rows, 0)
        own_sine = lax.dynamic_slice_in_dim(sine_table, shard * rows, rows, 0)
        by_head = queries.astype(jnp.float32).reshape(rows, heads, head_size).transpose(1, 0, 2)
        query_flat = (
            rotate(by_head, own_cosine[None], own_sine[None])
            .astype(jnp.bfloat16)
            .reshape(heads * rows, head_size)
        )
        span = jnp.stack([start, start + shard * rows]).astype(jnp.int32)

        def rows_of(table, top):
            return table.reshape(shards, rows, -1)[:, top : top + part_rows].reshape(
                shards * part_rows, -1
            )

        state = None
        cache_parts = []
        for part in range(parts):
            top = part * part_rows
            products = [own_product[top : top + part_rows]] + [
                project(columns) for columns in received[part]
            ]
            if shards == 2:
                partial_sums = jnp.concatenate(
                    [
                        jnp.where(shard == 0, products[0], products[1]),
                        jnp.where(shard == 0, products[1], products[0]),
                    ],
                    axis=0,
                )
            else:
                partial_sums = jnp.zeros((shards * part_rows, 2 * head_size), jnp.float32)
                for step in range(shards):
                    source = lax.rem(shard + shards - step, shards)
                    partial_sums = lax.dynamic_update_slice_in_dim(
                        partial_sums, products[step], source * part_rows, 0
                    )
            reach = 1
            while reach < shards:
                partial_sums = partial_sums + lax.ppermute(
                    partial_sums, "fsdp", [(i, i ^ reach) for i in range(shards)]
                )
                reach *= 2
            keys_rot = rotate(
                partial_sums[:, :head_size], rows_of(cosine, top), rows_of(sine_table, top)
            ).astype(jnp.bfloat16)
            block = jnp.concatenate(
                [keys_rot, partial_sums[:, head_size:].astype(jnp.bfloat16)], axis=1
            )
            cache_parts.append(lax.dynamic_slice_in_dim(block, shard * part_rows, part_rows, 0))
            pieces, masks = spread(block, contexts)
            local_pos = rows_of(jnp.arange(group_rows, dtype=jnp.int32)[:, None], top)[:, 0]
            order = jnp.array([mask for piece_masks in masks for mask in piece_masks], jnp.int32)
            place = ((context ^ order)[:, None] * group_rows + local_pos[None, :]).reshape(1, -1)
            last = part == parts - 1
            state = attend(span, place, query_flat, pieces, state, last, rows)
        kv_cache = jnp.concatenate(cache_parts, axis=0)
        return (kv_cache, state)

    return local


def solution(mesh):
    placed = (P(("ctx", "fsdp"), None), P(("ctx", "fsdp"), None), P("fsdp", None), P("fsdp", None))
    return jax.shard_map(
        make_local(mesh.shape["ctx"], mesh.shape["fsdp"], 2),
        mesh=mesh,
        in_specs=placed,
        out_specs=(P(("ctx", "fsdp"), None), P(("ctx", "fsdp"), None)),
        check_vma=False,
    )
```

```python
from functools import partial
import math

import jax
import jax.numpy as jnp
from jax import lax
from jax.experimental import pallas as pl
from jax.experimental.pallas import tpu as pltpu
from jax.sharding import PartitionSpec as P

rope_base = 500000.0
floor_value = -1e30


def rotate(vectors, cosine, sine_table):
    middle = vectors.shape[-1] // 2
    leading = vectors[..., :middle]
    back_half = vectors[..., middle:]
    return jnp.concatenate(
        [leading * cosine - back_half * sine_table, back_half * cosine + leading * sine_table],
        axis=-1,
    )


def tables(positions, head_size):
    middle = head_size // 2
    frequency = rope_base ** (-jnp.arange(middle, dtype=jnp.float32) * 2.0 / head_size)
    angles = positions.astype(jnp.float32)[:, None] * frequency[None, :]
    return (jnp.cos(angles), jnp.sin(angles))


def attention_kernel(
    span_ref, place_ref, query_ref, *refs, count, carry, final, rows, own, head_size, stride
):
    pieces, refs = refs[:count], refs[count:]
    if carry:
        old_peak, old_total, old_sum = refs[:3]
        refs = refs[3:]
    start = span_ref[0]
    first = span_ref[1]
    factor = head_size ** (-0.5) * math.log2(math.e)
    flat = query_ref.shape[0]
    keys = jnp.concatenate([piece[:, :head_size] for piece in pieces], axis=0)
    values = jnp.concatenate([piece[:, head_size:] for piece in pieces], axis=0)
    width = keys.shape[0]
    edge = min(width, -(-own // 128) * 128)
    query_pos = first + lax.rem(
        lax.broadcasted_iota(jnp.int32, (stride, edge), 0), jnp.int32(rows)
    )
    diagonal = place_ref[:, :edge] <= query_pos
    bias = jnp.where(place_ref[...] < start, 0.0, floor_value).astype(jnp.float32)

    def one(part):
        place = pl.ds(pl.multiple_of(part * stride, stride), stride)
        scores = (
            lax.dot_general(
                query_ref[place, :],
                keys,
                (((1,), (1,)), ((), ())),
                preferred_element_type=jnp.float32,
            )
            * factor
        )
        masked = jnp.where(diagonal, scores[:, :edge], floor_value)
        if edge < width:
            masked = jnp.concatenate([masked, scores[:, edge:] + bias[:, edge:]], axis=1)
        peak = jnp.max(masked, axis=1, keepdims=True)
        if carry:
            peak = jnp.maximum(peak, old_peak[place, :])
        weights = jnp.exp2(masked - peak)
        total = jnp.sum(weights, axis=1, keepdims=True)
        numerator = jnp.dot(
            weights.astype(jnp.bfloat16), values, preferred_element_type=jnp.float32
        )
        if carry:
            shrink = jnp.exp2(old_peak[place, :] - peak)
            total = total + shrink * old_total[place, :]
            numerator = numerator + shrink * old_sum[place, :]
        if final:
            out_ref, scratch = refs
            scratch[place, :] = (numerator / total).astype(jnp.bfloat16)
        else:
            peak_ref, total_ref, sum_ref = refs
            peak_ref[place, :] = peak
            total_ref[place, :] = total
            sum_ref[place, :] = numerator

    if width <= 2048:
        for part in range(flat // stride):
            one(part)
    else:

        @pl.loop(0, flat // stride)
        def each(part):
            one(part)

    if final:
        out_ref, scratch = refs
        for head in range(flat // rows):
            out_ref[:, head * head_size : (head + 1) * head_size] = scratch[
                head * rows : (head + 1) * rows, :
            ]


def attend(span, place, query_flat, pieces, state, final, rows):
    flat, head_size = query_flat.shape
    width = sum(piece.shape[0] for piece in pieces)
    stride = math.gcd(flat, 256 if width <= 2048 else rows)
    whole = pl.BlockSpec(memory_space=pltpu.VMEM)
    if final:
        shapes = jax.ShapeDtypeStruct((rows, flat // rows * head_size), jnp.bfloat16)
        out_specs, scratch = whole, [pltpu.VMEM((flat, head_size), jnp.bfloat16)]
    else:
        shapes = [
            jax.ShapeDtypeStruct((flat, 1), jnp.float32),
            jax.ShapeDtypeStruct((flat, 1), jnp.float32),
            jax.ShapeDtypeStruct((flat, head_size), jnp.float32),
        ]
        out_specs, scratch = [whole] * 3, []
    return pl.pallas_call(
        partial(
            attention_kernel,
            count=len(pieces),
            carry=state is not None,
            final=final,
            rows=rows,
            own=pieces[0].shape[0],
            head_size=head_size,
            stride=stride,
        ),
        out_shape=shapes,
        in_specs=[pl.BlockSpec(memory_space=pltpu.SMEM)]
        + [whole] * (2 + len(pieces) + (0 if state is None else 3)),
        out_specs=out_specs,
        scratch_shapes=scratch,
        compiler_params=pltpu.CompilerParams(vmem_limit_bytes=40 * 1024 * 1024),
        cost_estimate=pl.CostEstimate(
            flops=4 * flat * width * head_size,
            bytes_accessed=4 * flat * head_size + 4 * width * head_size,
            transcendentals=flat * width,
        ),
        name="attend_last" if final else "attend_part",
    )(span, place, query_flat, *pieces, *(() if state is None else state))


def stages_of(contexts):
    bits = []
    bit = contexts // 2
    while bit >= 1:
        bits.append(bit)
        bit //= 2
    core = bits[-1:]
    rest = bits[:-1]
    stages = [rest[i : i + 2] for i in range(0, len(rest), 2)] + ([core] if core else [])
    return stages


def after(value, *earlier):
    return lax.optimization_barrier((value, *earlier))[0]


def make_local(contexts, shards, plan):
    def local(tokens, queries, key_weight, value_weight):
        rows = tokens.shape[0]
        depth, head_size = key_weight.shape
        heads = queries.shape[1] // head_size
        group_rows = shards * rows
        context = lax.axis_index("ctx")
        shard = lax.axis_index("fsdp")
        unit = rows // sum(sum(part) for part in plan)

        def send_rows(top, count, *earlier):
            source = after(tokens, *earlier) if earlier else tokens
            arrived, sent = [], []
            for step in range(1, shards):
                target = lax.rem(shard + step, shards)
                columns = lax.dynamic_slice(
                    source, (jnp.int32(top), target * depth), (count, depth)
                )
                sent.append(columns)
                arrived.append(
                    lax.ppermute(
                        columns, "fsdp", [(i, (i + step) % shards) for i in range(shards)]
                    )
                )
            return arrived, sent

        def rows_of(table, top, count):
            return table.reshape(shards, rows, -1)[:, top : top + count].reshape(
                shards * count, -1
            )

        class Part:
            pass

        parts = []
        chunks = []
        top = 0
        for sizes in plan:
            part = Part()
            part.top = top
            part.rows = sum(sizes) * unit
            part.first = len(chunks)
            for size in sizes:
                chunks.append((top, size * unit))
                top += size * unit
            part.end = len(chunks)
            part.stage = None
            parts.append(part)
        stages = stages_of(contexts)
        ahead = parts[0].end + 1

        flying = []
        sent = ()
        for chunk in chunks[:ahead]:
            arrived, sent = send_rows(*chunk, *sent)
            flying.append(arrived)

        weight = after(jnp.concatenate([key_weight, value_weight], axis=1), *sent)
        own_columns = lax.dynamic_slice_in_dim(tokens, shard * depth, depth, 1)
        own_product = jnp.dot(own_columns, weight, preferred_element_type=jnp.float32)

        start = context * group_rows
        positions = start + jnp.arange(group_rows, dtype=jnp.int32)
        cosine, sine_table = tables(positions, head_size)
        own_cosine = lax.dynamic_slice_in_dim(cosine, shard * rows, rows, 0)
        own_sine = lax.dynamic_slice_in_dim(sine_table, shard * rows, rows, 0)
        by_head = queries.astype(jnp.float32).reshape(rows, heads, head_size).transpose(1, 0, 2)
        query_flat = (
            rotate(by_head, own_cosine[None], own_sine[None])
            .astype(jnp.bfloat16)
            .reshape(heads * rows, head_size)
        )
        span = jnp.stack([start, start + shard * rows]).astype(jnp.int32)
        own_product, cosine, sine_table, query_flat, span = lax.optimization_barrier(
            (own_product, cosine, sine_table, query_flat, span)
        )

        def exchange(part, arrived):
            columns = [
                jnp.concatenate([chunk[s] for chunk in arrived], axis=0)
                for s in range(shards - 1)
            ]
            products = [own_product[part.top : part.top + part.rows]] + [
                jnp.dot(c, weight, preferred_element_type=jnp.float32) for c in columns
            ]
            if shards == 2:
                sums = jnp.concatenate(
                    [
                        jnp.where(shard == 0, products[0], products[1]),
                        jnp.where(shard == 0, products[1], products[0]),
                    ],
                    axis=0,
                )
            else:
                sums = jnp.zeros((shards * part.rows, 2 * head_size), jnp.float32)
                for step in range(shards):
                    source = lax.rem(shard + shards - step, shards)
                    sums = lax.dynamic_update_slice_in_dim(
                        sums, products[step], source * part.rows, 0
                    )
            part.sums = after(sums)
            part.other = jnp.zeros_like(sums)
            reach = 1
            while reach < shards:
                if reach > 1:
                    part.sums = part.sums + part.other
                part.other = lax.ppermute(
                    part.sums, "fsdp", [(i, i ^ reach) for i in range(shards)]
                )
                reach *= 2
            part.stage = 0

        def held(part):
            return (part.sums, part.other) if part.stage == 0 else tuple(part.pieces)

        def advance(part, values):
            if part.stage == 0:
                sums = values[0] + values[1]
                keys_rot = rotate(
                    sums[:, :head_size],
                    rows_of(cosine, part.top, part.rows),
                    rows_of(sine_table, part.top, part.rows),
                ).astype(jnp.bfloat16)
                block = after(
                    jnp.concatenate([keys_rot, sums[:, head_size:].astype(jnp.bfloat16)], axis=1)
                )
                part.cache = lax.dynamic_slice_in_dim(block, shard * part.rows, part.rows, 0)
                part.pieces, part.masks = [block], [[0]]
            else:
                part.pieces = list(values)
            known = jnp.concatenate(part.pieces, axis=0)
            if part.stage < len(stages):
                known_masks = [mask for piece_masks in part.masks for mask in piece_masks]
                moves = [0]
                for bit in stages[part.stage]:
                    moves = moves + [move ^ bit for move in moves]
                for move in moves[1:]:
                    part.pieces.append(
                        lax.ppermute(known, "ctx", [(i, i ^ move) for i in range(contexts)])
                    )
                    part.masks.append([mask ^ move for mask in known_masks])
            part.stage += 1

        def step_all(going, extra=()):
            gated = lax.optimization_barrier((tuple(held(part) for part in going), extra))
            for part, values in zip(going, gated[0]):
                advance(part, values)
            return gated[1]

        def finish(part, state, last):
            local_pos = rows_of(
                jnp.arange(group_rows, dtype=jnp.int32)[:, None], part.top, part.rows
            )[:, 0]
            order = jnp.array([mask for masks in part.masks for mask in masks], jnp.int32)
            place = ((context ^ order)[:, None] * group_rows + local_pos[None, :]).reshape(1, -1)
            return attend(span, place, query_flat, part.pieces, state, last, rows)

        for index, part in enumerate(parts):
            going = [p for p in parts[:index] if p.stage <= len(stages)]
            arrived = flying[part.first : part.end]
            arrived = list(lax.optimization_barrier((arrived, own_product))[0])
            exchange(part, arrived)
            for chunk in chunks[len(flying) : part.end + 2]:
                flying.append(send_rows(*chunk, part.sums)[0])
            if index + 1 < len(parts):
                nearest = flying[parts[index + 1].first]
                nearest = step_all(going + [part], tuple(nearest))
                flying[parts[index + 1].first] = list(nearest)
        state = None
        going = list(parts)
        while going:
            step_all(going)
            ready = [part for part in going if part.stage > len(stages)]
            going = [part for part in going if part.stage <= len(stages)]
            for part in ready:
                state = finish(part, state, part is parts[-1])
        kv_cache = jnp.concatenate([part.cache for part in parts], axis=0)
        return (kv_cache, state)

    return local


def solution(mesh):
    placed = (P(("ctx", "fsdp"), None), P(("ctx", "fsdp"), None), P("fsdp", None), P("fsdp", None))
    return jax.shard_map(
        make_local(mesh.shape["ctx"], mesh.shape["fsdp"], ((1, 5), (1, 1))),
        mesh=mesh,
        in_specs=placed,
        out_specs=(P(("ctx", "fsdp"), None), P(("ctx", "fsdp"), None)),
        check_vma=False,
    )
```

```python
from functools import partial
import math

import jax
import jax.numpy as jnp
from jax import lax
from jax.experimental import pallas as pl
from jax.experimental.pallas import tpu as pltpu
from jax.sharding import PartitionSpec as P

rope_base = 500000.0
floor_value = -1e30


def rotate(vectors, cosine, sine_table):
    middle = vectors.shape[-1] // 2
    leading = vectors[..., :middle]
    back_half = vectors[..., middle:]
    return jnp.concatenate(
        [leading * cosine - back_half * sine_table, back_half * cosine + leading * sine_table],
        axis=-1,
    )


def tables(positions, head_size):
    middle = head_size // 2
    frequency = rope_base ** (-jnp.arange(middle, dtype=jnp.float32) * 2.0 / head_size)
    angles = positions.astype(jnp.float32)[:, None] * frequency[None, :]
    return (jnp.cos(angles), jnp.sin(angles))


def attention_kernel(
    span_ref, place_ref, query_ref, *refs, count, carry, final, rows, edge, head_size, stride
):
    pieces, refs = refs[:count], refs[count:]
    if carry:
        old_peak, old_total, old_sum = refs[:3]
        refs = refs[3:]
    start = span_ref[0]
    first = span_ref[1]
    factor = head_size ** (-0.5) * math.log2(math.e)
    flat = query_ref.shape[0]
    keys = jnp.concatenate([piece[:, :head_size] for piece in pieces], axis=0)
    values = jnp.concatenate([piece[:, head_size:] for piece in pieces], axis=0)
    width = keys.shape[0]
    if edge:
        query_pos = first + lax.rem(
            lax.broadcasted_iota(jnp.int32, (stride, edge), 0), jnp.int32(rows)
        )
        diagonal = place_ref[:, :edge] <= query_pos
    bias = jnp.where(place_ref[...] < start, 0.0, floor_value).astype(jnp.float32)

    def one(part):
        place = pl.ds(pl.multiple_of(part * stride, stride), stride)
        scores = (
            lax.dot_general(
                query_ref[place, :],
                keys,
                (((1,), (1,)), ((), ())),
                preferred_element_type=jnp.float32,
            )
            * factor
        )
        masked = []
        if edge:
            masked.append(jnp.where(diagonal, scores[:, :edge], floor_value))
        if edge < width:
            masked.append(scores[:, edge:] + bias[:, edge:])
        masked = jnp.concatenate(masked, axis=1) if len(masked) > 1 else masked[0]
        peak = jnp.max(masked, axis=1, keepdims=True)
        if carry:
            peak = jnp.maximum(peak, old_peak[place, :])
        weights = jnp.exp2(masked - peak)
        total = jnp.sum(weights, axis=1, keepdims=True)
        numerator = jnp.dot(
            weights.astype(jnp.bfloat16), values, preferred_element_type=jnp.float32
        )
        if carry:
            shrink = jnp.exp2(old_peak[place, :] - peak)
            total = total + shrink * old_total[place, :]
            numerator = numerator + shrink * old_sum[place, :]
        if final:
            out_ref, scratch = refs
            scratch[place, :] = (numerator / total).astype(jnp.bfloat16)
        else:
            peak_ref, total_ref, sum_ref = refs
            peak_ref[place, :] = peak
            total_ref[place, :] = total
            sum_ref[place, :] = numerator

    if width <= 2048:
        for part in range(flat // stride):
            one(part)
    else:

        @pl.loop(0, flat // stride)
        def each(part):
            one(part)

    if final:
        out_ref, scratch = refs
        for head in range(flat // rows):
            out_ref[:, head * head_size : (head + 1) * head_size] = scratch[
                head * rows : (head + 1) * rows, :
            ]


def attend(span, place, query_flat, pieces, edge, state, final, rows):
    flat, head_size = query_flat.shape
    width = sum(piece.shape[0] for piece in pieces)
    stride = math.gcd(flat, 256 if width <= 2048 else rows)
    whole = pl.BlockSpec(memory_space=pltpu.VMEM)
    if final:
        shapes = jax.ShapeDtypeStruct((rows, flat // rows * head_size), jnp.bfloat16)
        out_specs, scratch = whole, [pltpu.VMEM((flat, head_size), jnp.bfloat16)]
    else:
        shapes = [
            jax.ShapeDtypeStruct((flat, 1), jnp.float32),
            jax.ShapeDtypeStruct((flat, 1), jnp.float32),
            jax.ShapeDtypeStruct((flat, head_size), jnp.float32),
        ]
        out_specs, scratch = [whole] * 3, []
    return pl.pallas_call(
        partial(
            attention_kernel,
            count=len(pieces),
            carry=state is not None,
            final=final,
            rows=rows,
            edge=edge,
            head_size=head_size,
            stride=stride,
        ),
        out_shape=shapes,
        in_specs=[pl.BlockSpec(memory_space=pltpu.SMEM)]
        + [whole] * (2 + len(pieces) + (0 if state is None else 3)),
        out_specs=out_specs,
        scratch_shapes=scratch,
        compiler_params=pltpu.CompilerParams(vmem_limit_bytes=24 * 1024 * 1024),
        cost_estimate=pl.CostEstimate(
            flops=4 * flat * width * head_size,
            bytes_accessed=4 * flat * head_size + 4 * width * head_size,
            transcendentals=flat * width,
        ),
        name="attend_last" if final else "attend_part",
    )(span, place, query_flat, *pieces, *(() if state is None else state))


def stages_of(contexts):
    bits = []
    bit = contexts // 2
    while bit >= 1:
        bits.append(bit)
        bit //= 2
    core = bits[-1:]
    rest = bits[:-1]
    stages = [rest[i : i + 2] for i in range(0, len(rest), 2)] + ([core] if core else [])
    return stages


def after(value, *earlier):
    return lax.optimization_barrier((value, *earlier))[0]


def make_local(contexts, shards, plan):
    def local(tokens, queries, key_weight, value_weight):
        rows = tokens.shape[0]
        depth, head_size = key_weight.shape
        heads = queries.shape[1] // head_size
        group_rows = shards * rows
        context = lax.axis_index("ctx")
        shard = lax.axis_index("fsdp")
        unit = rows // sum(sum(part) for part in plan)

        def send_rows(top, count, *earlier):
            source = after(tokens, *earlier) if earlier else tokens
            arrived, sent = [], []
            for step in range(1, shards):
                target = lax.rem(shard + step, shards)
                columns = lax.dynamic_slice(
                    source, (jnp.int32(top), target * depth), (count, depth)
                )
                sent.append(columns)
                arrived.append(
                    lax.ppermute(
                        columns, "fsdp", [(i, (i + step) % shards) for i in range(shards)]
                    )
                )
            return arrived, sent

        def rows_of(table, top, count):
            return table.reshape(shards, rows, -1)[:, top : top + count].reshape(
                shards * count, -1
            )

        class Part:
            pass

        parts = []
        chunks = []
        top = 0
        for sizes in plan:
            part = Part()
            part.top = top
            part.rows = sum(sizes) * unit
            part.first = len(chunks)
            for size in sizes:
                chunks.append((top, size * unit))
                top += size * unit
            part.end = len(chunks)
            part.stage = None
            parts.append(part)
        stages = stages_of(contexts)
        ahead = parts[0].end + 1

        flying = []
        sent = ()
        for chunk in chunks[:ahead]:
            arrived, sent = send_rows(*chunk, *sent)
            flying.append(arrived)

        weight = after(jnp.concatenate([key_weight, value_weight], axis=1), *sent)
        own_columns = lax.dynamic_slice_in_dim(tokens, shard * depth, depth, 1)
        own_product = jnp.dot(own_columns, weight, preferred_element_type=jnp.float32)

        start = context * group_rows
        positions = start + jnp.arange(group_rows, dtype=jnp.int32)
        cosine, sine_table = tables(positions, head_size)
        own_cosine = lax.dynamic_slice_in_dim(cosine, shard * rows, rows, 0)
        own_sine = lax.dynamic_slice_in_dim(sine_table, shard * rows, rows, 0)
        by_head = queries.astype(jnp.float32).reshape(rows, heads, head_size).transpose(1, 0, 2)
        query_flat = (
            rotate(by_head, own_cosine[None], own_sine[None])
            .astype(jnp.bfloat16)
            .reshape(heads * rows, head_size)
        )
        span = jnp.stack([start, start + shard * rows]).astype(jnp.int32)
        own_product, cosine, sine_table, query_flat, span = lax.optimization_barrier(
            (own_product, cosine, sine_table, query_flat, span)
        )

        def exchange(part, arrived):
            columns = [
                jnp.concatenate([chunk[s] for chunk in arrived], axis=0)
                for s in range(shards - 1)
            ]
            products = [own_product[part.top : part.top + part.rows]] + [
                jnp.dot(c, weight, preferred_element_type=jnp.float32) for c in columns
            ]
            if shards == 2:
                sums = jnp.concatenate(
                    [
                        jnp.where(shard == 0, products[0], products[1]),
                        jnp.where(shard == 0, products[1], products[0]),
                    ],
                    axis=0,
                )
            else:
                sums = jnp.zeros((shards * part.rows, 2 * head_size), jnp.float32)
                for step in range(shards):
                    source = lax.rem(shard + shards - step, shards)
                    sums = lax.dynamic_update_slice_in_dim(
                        sums, products[step], source * part.rows, 0
                    )
            part.sums = after(sums)
            part.other = jnp.zeros_like(sums)
            reach = 1
            while reach < shards:
                if reach > 1:
                    part.sums = part.sums + part.other
                part.other = lax.ppermute(
                    part.sums, "fsdp", [(i, i ^ reach) for i in range(shards)]
                )
                reach *= 2
            part.stage = 0

        def held(part):
            return (part.sums, part.other) if part.stage == 0 else tuple(part.pieces)

        def advance(part, values):
            if part.stage == 0:
                sums = values[0] + values[1]
                keys_rot = rotate(
                    sums[:, :head_size],
                    rows_of(cosine, part.top, part.rows),
                    rows_of(sine_table, part.top, part.rows),
                ).astype(jnp.bfloat16)
                block = after(
                    jnp.concatenate([keys_rot, sums[:, head_size:].astype(jnp.bfloat16)], axis=1)
                )
                part.cache = lax.dynamic_slice_in_dim(block, shard * part.rows, part.rows, 0)
                part.pieces, part.places = [block], [context[None]]
                part.edge = block.shape[0]
            else:
                part.pieces = list(values)
            if part.stage < len(stages):
                known = jnp.concatenate(part.pieces, axis=0)
                places = jnp.concatenate(part.places)
                bits = stages[part.stage]
                if len(bits) == 1:
                    pairs = [(i, i ^ bits[0]) for i in range(contexts)]
                    part.pieces.append(lax.ppermute(known, "ctx", pairs))
                    part.places.append(places ^ bits[0])
                else:
                    low = min(bits)
                    count = (sum(bits) // low) + 1
                    groups = [
                        [base + low * turn for turn in range(count)]
                        for base in range(contexts)
                        if base & sum(bits) == 0
                    ]
                    copies = jnp.broadcast_to(known[None], (count,) + known.shape)
                    gathered = lax.all_to_all(copies, "ctx", 0, 0, axis_index_groups=groups)
                    part.pieces = [gathered.reshape(-1, known.shape[1])]
                    turns = low * jnp.arange(count, dtype=jnp.int32)
                    kept = places & ~jnp.int32(sum(bits))
                    part.places = [(turns[:, None] | kept[None, :]).reshape(-1)]
                    part.edge = part.pieces[0].shape[0]
            part.stage += 1

        def step_all(going, extra=()):
            gated = lax.optimization_barrier((tuple(held(part) for part in going), extra))
            for part, values in zip(going, gated[0]):
                advance(part, values)
            return gated[1]

        def finish(part, state, last):
            local_pos = rows_of(
                jnp.arange(group_rows, dtype=jnp.int32)[:, None], part.top, part.rows
            )[:, 0]

            def one(pieces, places, edge, state, last):
                place = (
                    jnp.concatenate(places)[:, None] * group_rows + local_pos[None, :]
                ).reshape(1, -1)
                return attend(span, place, query_flat, pieces, edge, state, last, rows)

            if last:
                state = one(part.pieces[:-1], part.places[:-1], part.edge, state, False)
                return one(part.pieces[-1:], part.places[-1:], 0, state, True)
            return one(part.pieces, part.places, part.edge, state, False)

        for index, part in enumerate(parts):
            going = [p for p in parts[:index] if p.stage < len(stages)]
            arrived = flying[part.first : part.end]
            arrived = list(lax.optimization_barrier((arrived, own_product))[0])
            exchange(part, arrived)
            for chunk in chunks[len(flying) : part.end + 2]:
                flying.append(send_rows(*chunk, part.sums)[0])
            if index + 1 < len(parts):
                nearest = flying[parts[index + 1].first]
                nearest = step_all(going + [part], tuple(nearest))
                flying[parts[index + 1].first] = list(nearest)
        state = None
        going = list(parts)
        while going:
            step_all(going)
            ready = [part for part in going if part.stage >= len(stages)]
            going = [part for part in going if part.stage < len(stages)]
            for part in ready:
                state = finish(part, state, part is parts[-1])
        kv_cache = jnp.concatenate([part.cache for part in parts], axis=0)
        return (kv_cache, state)

    return local


def solution(mesh):
    placed = (P(("ctx", "fsdp"), None), P(("ctx", "fsdp"), None), P("fsdp", None), P("fsdp", None))
    return jax.shard_map(
        make_local(mesh.shape["ctx"], mesh.shape["fsdp"], ((1, 7),)),
        mesh=mesh,
        in_specs=placed,
        out_specs=(P(("ctx", "fsdp"), None), P(("ctx", "fsdp"), None)),
        check_vma=False,
    )
```

```python
from functools import partial
import math

import jax
import jax.numpy as jnp
from jax import lax
from jax.experimental import pallas as pl
from jax.experimental.pallas import tpu as pltpu
from jax.sharding import PartitionSpec as P

rope_base = 500000.0
floor_value = -1e30


def rotate(vectors, cosine, sine_table):
    middle = vectors.shape[-1] // 2
    leading = vectors[..., :middle]
    back_half = vectors[..., middle:]
    return jnp.concatenate(
        [leading * cosine - back_half * sine_table, back_half * cosine + leading * sine_table],
        axis=-1,
    )


def tables(positions, head_size):
    middle = head_size // 2
    frequency = rope_base ** (-jnp.arange(middle, dtype=jnp.float32) * 2.0 / head_size)
    angles = positions.astype(jnp.float32)[:, None] * frequency[None, :]
    return (jnp.cos(angles), jnp.sin(angles))


def attention_kernel(
    span_ref, place_ref, query_ref, *refs, count, carry, final, rows, own, head_size, stride
):
    pieces, refs = refs[:count], refs[count:]
    if carry:
        old_peak, old_total, old_sum = refs[:3]
        refs = refs[3:]
    start = span_ref[0]
    first = span_ref[1]
    factor = head_size ** (-0.5) * math.log2(math.e)
    flat = query_ref.shape[0]
    keys = jnp.concatenate([piece[:, :head_size] for piece in pieces], axis=0)
    values = jnp.concatenate([piece[:, head_size:] for piece in pieces], axis=0)
    width = keys.shape[0]
    edge = min(width, -(-own // 128) * 128)
    query_pos = first + lax.rem(
        lax.broadcasted_iota(jnp.int32, (stride, edge), 0), jnp.int32(rows)
    )
    diagonal = place_ref[:, :edge] <= query_pos
    bias = jnp.where(place_ref[...] < start, 0.0, floor_value).astype(jnp.float32)

    def one(part):
        place = pl.ds(pl.multiple_of(part * stride, stride), stride)
        scores = (
            lax.dot_general(
                query_ref[place, :],
                keys,
                (((1,), (1,)), ((), ())),
                preferred_element_type=jnp.float32,
            )
            * factor
        )
        masked = jnp.where(diagonal, scores[:, :edge], floor_value)
        if edge < width:
            masked = jnp.concatenate([masked, scores[:, edge:] + bias[:, edge:]], axis=1)
        peak = jnp.max(masked, axis=1, keepdims=True)
        if carry:
            peak = jnp.maximum(peak, old_peak[place, :])
        weights = jnp.exp2(masked - peak)
        total = jnp.sum(weights, axis=1, keepdims=True)
        numerator = jnp.dot(
            weights.astype(jnp.bfloat16), values, preferred_element_type=jnp.float32
        )
        if carry:
            shrink = jnp.exp2(old_peak[place, :] - peak)
            total = total + shrink * old_total[place, :]
            numerator = numerator + shrink * old_sum[place, :]
        if final:
            out_ref, scratch = refs
            scratch[place, :] = (numerator / total).astype(jnp.bfloat16)
        else:
            peak_ref, total_ref, sum_ref = refs
            peak_ref[place, :] = peak
            total_ref[place, :] = total
            sum_ref[place, :] = numerator

    if width <= 2048:
        for part in range(flat // stride):
            one(part)
    else:

        @pl.loop(0, flat // stride)
        def each(part):
            one(part)

    if final:
        out_ref, scratch = refs
        for head in range(flat // rows):
            out_ref[:, head * head_size : (head + 1) * head_size] = scratch[
                head * rows : (head + 1) * rows, :
            ]


def attend(span, place, query_flat, pieces, own, state, final, rows):
    flat, head_size = query_flat.shape
    width = sum(piece.shape[0] for piece in pieces)
    stride = math.gcd(flat, 256 if width <= 2048 else rows)
    whole = pl.BlockSpec(memory_space=pltpu.VMEM)
    if final:
        shapes = jax.ShapeDtypeStruct((rows, flat // rows * head_size), jnp.bfloat16)
        out_specs, scratch = whole, [pltpu.VMEM((flat, head_size), jnp.bfloat16)]
    else:
        shapes = [
            jax.ShapeDtypeStruct((flat, 1), jnp.float32),
            jax.ShapeDtypeStruct((flat, 1), jnp.float32),
            jax.ShapeDtypeStruct((flat, head_size), jnp.float32),
        ]
        out_specs, scratch = [whole] * 3, []
    return pl.pallas_call(
        partial(
            attention_kernel,
            count=len(pieces),
            carry=state is not None,
            final=final,
            rows=rows,
            own=own,
            head_size=head_size,
            stride=stride,
        ),
        out_shape=shapes,
        in_specs=[pl.BlockSpec(memory_space=pltpu.SMEM)]
        + [whole] * (2 + len(pieces) + (0 if state is None else 3)),
        out_specs=out_specs,
        scratch_shapes=scratch,
        compiler_params=pltpu.CompilerParams(vmem_limit_bytes=24 * 1024 * 1024),
        cost_estimate=pl.CostEstimate(
            flops=4 * flat * width * head_size,
            bytes_accessed=4 * flat * head_size + 4 * width * head_size,
            transcendentals=flat * width,
        ),
        name="attend_last" if final else "attend_part",
    )(span, place, query_flat, *pieces, *(() if state is None else state))


def stages_of(contexts):
    bits = []
    bit = contexts // 2
    while bit >= 1:
        bits.append(bit)
        bit //= 2
    core = bits[-1:]
    rest = bits[:-1]
    stages = [rest[i : i + 2] for i in range(0, len(rest), 2)] + ([core] if core else [])
    return stages


def after(value, *earlier):
    return lax.optimization_barrier((value, *earlier))[0]


def make_local(contexts, shards, plan):
    def local(tokens, queries, key_weight, value_weight):
        rows = tokens.shape[0]
        depth, head_size = key_weight.shape
        heads = queries.shape[1] // head_size
        group_rows = shards * rows
        context = lax.axis_index("ctx")
        shard = lax.axis_index("fsdp")
        unit = rows // sum(sum(part) for part in plan)

        def send_rows(top, count, *earlier):
            source = after(tokens, *earlier) if earlier else tokens
            arrived, sent = [], []
            for step in range(1, shards):
                target = lax.rem(shard + step, shards)
                columns = lax.dynamic_slice(
                    source, (jnp.int32(top), target * depth), (count, depth)
                )
                sent.append(columns)
                arrived.append(
                    lax.ppermute(
                        columns, "fsdp", [(i, (i + step) % shards) for i in range(shards)]
                    )
                )
            return arrived, sent

        def rows_of(table, top, count):
            return table.reshape(shards, rows, -1)[:, top : top + count].reshape(
                shards * count, -1
            )

        class Part:
            pass

        parts = []
        chunks = []
        top = 0
        for sizes in plan:
            part = Part()
            part.top = top
            part.rows = sum(sizes) * unit
            part.first = len(chunks)
            for size in sizes:
                chunks.append((top, size * unit))
                top += size * unit
            part.end = len(chunks)
            part.stage = None
            parts.append(part)
        stages = stages_of(contexts)
        ahead = parts[0].end + 1

        flying = []
        sent = ()
        for chunk in chunks[:ahead]:
            arrived, sent = send_rows(*chunk, *sent)
            flying.append(arrived)

        def project(columns):
            return [
                jnp.dot(columns, weight, preferred_element_type=jnp.float32)
                for weight in (key_weight, value_weight)
            ]

        own_columns = lax.dynamic_slice_in_dim(after(tokens, *sent), shard * depth, depth, 1)
        own_product = jnp.concatenate(project(own_columns), axis=1)

        start = context * group_rows
        positions = start + jnp.arange(group_rows, dtype=jnp.int32)
        cosine, sine_table = tables(positions, head_size)
        own_cosine = lax.dynamic_slice_in_dim(cosine, shard * rows, rows, 0)
        own_sine = lax.dynamic_slice_in_dim(sine_table, shard * rows, rows, 0)
        by_head = queries.astype(jnp.float32).reshape(rows, heads, head_size).transpose(1, 0, 2)
        query_flat = (
            rotate(by_head, own_cosine[None], own_sine[None])
            .astype(jnp.bfloat16)
            .reshape(heads * rows, head_size)
        )
        span = jnp.stack([start, start + shard * rows]).astype(jnp.int32)
        own_product, cosine, sine_table, query_flat, span = lax.optimization_barrier(
            (own_product, cosine, sine_table, query_flat, span)
        )

        def exchange(part, arrived):
            products = [own_product[part.top : part.top + part.rows]] + [
                jnp.concatenate([chunk[step] for chunk in arrived], axis=0)
                for step in range(shards - 1)
            ]
            if shards == 2:
                sums = jnp.concatenate(
                    [
                        jnp.where(shard == 0, products[0], products[1]),
                        jnp.where(shard == 0, products[1], products[0]),
                    ],
                    axis=0,
                )
            else:
                sums = jnp.zeros((shards * part.rows, 2 * head_size), jnp.float32)
                for step in range(shards):
                    source = lax.rem(shard + shards - step, shards)
                    sums = lax.dynamic_update_slice_in_dim(
                        sums, products[step], source * part.rows, 0
                    )
            part.sums = after(sums)
            part.other = jnp.zeros_like(sums)
            reach = 1
            while reach < shards:
                if reach > 1:
                    part.sums = part.sums + part.other
                part.other = lax.ppermute(
                    part.sums, "fsdp", [(i, i ^ reach) for i in range(shards)]
                )
                reach *= 2
            part.stage = 0

        def held(part):
            return (part.sums, part.other) if part.stage == 0 else tuple(part.pieces)

        def advance(part, values):
            if part.stage == 0:
                sums = values[0] + values[1]
                keys_rot = rotate(
                    sums[:, :head_size],
                    rows_of(cosine, part.top, part.rows),
                    rows_of(sine_table, part.top, part.rows),
                ).astype(jnp.bfloat16)
                block = after(
                    jnp.concatenate([keys_rot, sums[:, head_size:].astype(jnp.bfloat16)], axis=1)
                )
                part.cache = lax.dynamic_slice_in_dim(block, shard * part.rows, part.rows, 0)
                part.pieces, part.masks = [block], [[0]]
            else:
                part.pieces = list(values)
            if part.stage < len(stages):
                known = jnp.concatenate(part.pieces, axis=0)
                known_masks = [mask for piece_masks in part.masks for mask in piece_masks]
                part.pieces, part.masks = [known], [known_masks]
                moves = [0]
                for bit in stages[part.stage]:
                    moves = moves + [move ^ bit for move in moves]
                for move in moves[1:]:
                    part.pieces.append(
                        lax.ppermute(known, "ctx", [(i, i ^ move) for i in range(contexts)])
                    )
                    part.masks.append([mask ^ move for mask in known_masks])
            part.stage += 1

        def step_all(going, extra=()):
            gated = lax.optimization_barrier((tuple(held(part) for part in going), extra))
            for part, values in zip(going, gated[0]):
                advance(part, values)
            return gated[1]

        def finish(part, state, last):
            local_pos = rows_of(
                jnp.arange(group_rows, dtype=jnp.int32)[:, None], part.top, part.rows
            )[:, 0]
            order = jnp.array([mask for masks in part.masks for mask in masks], jnp.int32)
            place = ((context ^ order)[:, None] * group_rows + local_pos[None, :]).reshape(1, -1)
            return attend(span, place, query_flat, part.pieces, shards * part.rows, state, last, rows)

        for index, part in enumerate(parts):
            going = [p for p in parts[:index] if p.stage <= len(stages)]
            gate = own_product
            arrived = []
            for number in range(part.first, part.end):
                chunk, gate = lax.optimization_barrier((flying[number], gate))
                gate = [jnp.concatenate(project(columns), axis=1) for columns in chunk]
                arrived.append(gate)
            exchange(part, arrived)
            for chunk in chunks[len(flying) : part.end + 2]:
                flying.append(send_rows(*chunk, part.sums)[0])
            if index + 1 < len(parts):
                nearest = flying[parts[index + 1].first]
                nearest = step_all(going + [part], tuple(nearest))
                flying[parts[index + 1].first] = list(nearest)
        state = None
        going = list(parts)
        while going:
            step_all(going)
            ready = [part for part in going if part.stage > len(stages)]
            going = [part for part in going if part.stage <= len(stages)]
            for part in ready:
                state = finish(part, state, part is parts[-1])
        kv_cache = jnp.concatenate([part.cache for part in parts], axis=0)
        return (kv_cache, state)

    return local


def solution(mesh):
    placed = (P(("ctx", "fsdp"), None), P(("ctx", "fsdp"), None), P("fsdp", None), P("fsdp", None))
    return jax.shard_map(
        make_local(mesh.shape["ctx"], mesh.shape["fsdp"], ((1, 3), (2, 2))),
        mesh=mesh,
        in_specs=placed,
        out_specs=(P(("ctx", "fsdp"), None), P(("ctx", "fsdp"), None)),
        check_vma=False,
    )
```

```python
from functools import partial
import math

import jax
import jax.numpy as jnp
from jax import lax
from jax.experimental import pallas as pl
from jax.experimental.pallas import tpu as pltpu
from jax.sharding import PartitionSpec as P

rope_base = 500000.0
floor_value = -1e30


def rotate(vectors, cosine, sine_table):
    middle = vectors.shape[-1] // 2
    leading = vectors[..., :middle]
    back_half = vectors[..., middle:]
    return jnp.concatenate(
        [leading * cosine - back_half * sine_table, back_half * cosine + leading * sine_table],
        axis=-1,
    )


def tables(positions, head_size):
    middle = head_size // 2
    frequency = rope_base ** (-jnp.arange(middle, dtype=jnp.float32) * 2.0 / head_size)
    angles = positions.astype(jnp.float32)[:, None] * frequency[None, :]
    return (jnp.cos(angles), jnp.sin(angles))


def attention_kernel(
    span_ref, place_ref, query_ref, *refs, count, carry, final, rows, own, head_size, stride
):
    pieces, refs = refs[:count], refs[count:]
    if carry:
        old_peak, old_total, old_sum = refs[:3]
        refs = refs[3:]
    start = span_ref[0]
    first = span_ref[1]
    factor = head_size ** (-0.5) * math.log2(math.e)
    flat = query_ref.shape[0]
    keys = jnp.concatenate([piece[:, :head_size] for piece in pieces], axis=0)
    values = jnp.concatenate([piece[:, head_size:] for piece in pieces], axis=0)
    width = keys.shape[0]
    edge = min(width, -(-own // 128) * 128)
    if edge:
        query_pos = first + lax.rem(
            lax.broadcasted_iota(jnp.int32, (stride, edge), 0), jnp.int32(rows)
        )
        diagonal = place_ref[:, :edge] <= query_pos
    bias = jnp.where(place_ref[...] < start, 0.0, floor_value).astype(jnp.float32)

    def one(part):
        place = pl.ds(pl.multiple_of(part * stride, stride), stride)
        scores = (
            lax.dot_general(
                query_ref[place, :],
                keys,
                (((1,), (1,)), ((), ())),
                preferred_element_type=jnp.float32,
            )
            * factor
        )
        masked = []
        if edge:
            masked.append(jnp.where(diagonal, scores[:, :edge], floor_value))
        if edge < width:
            masked.append(scores[:, edge:] + bias[:, edge:])
        masked = jnp.concatenate(masked, axis=1) if len(masked) > 1 else masked[0]
        peak = jnp.max(masked, axis=1, keepdims=True)
        if carry:
            peak = jnp.maximum(peak, old_peak[place, :])
        weights = jnp.exp2(masked - peak)
        total = jnp.sum(weights, axis=1, keepdims=True)
        numerator = jnp.dot(
            weights.astype(jnp.bfloat16), values, preferred_element_type=jnp.float32
        )
        if carry:
            shrink = jnp.exp2(old_peak[place, :] - peak)
            total = total + shrink * old_total[place, :]
            numerator = numerator + shrink * old_sum[place, :]
        if final:
            out_ref, scratch = refs
            scratch[place, :] = (numerator / total).astype(jnp.bfloat16)
        else:
            peak_ref, total_ref, sum_ref = refs
            peak_ref[place, :] = peak
            total_ref[place, :] = total
            sum_ref[place, :] = numerator

    if width <= 2048:
        for part in range(flat // stride):
            one(part)
    else:

        @pl.loop(0, flat // stride)
        def each(part):
            one(part)

    if final:
        out_ref, scratch = refs
        for head in range(flat // rows):
            out_ref[:, head * head_size : (head + 1) * head_size] = scratch[
                head * rows : (head + 1) * rows, :
            ]


def attend(span, place, query_flat, pieces, own, state, final, rows):
    flat, head_size = query_flat.shape
    width = sum(piece.shape[0] for piece in pieces)
    stride = math.gcd(flat, 256 if width <= 2048 else rows)
    whole = pl.BlockSpec(memory_space=pltpu.VMEM)
    if final:
        shapes = jax.ShapeDtypeStruct((rows, flat // rows * head_size), jnp.bfloat16)
        out_specs, scratch = whole, [pltpu.VMEM((flat, head_size), jnp.bfloat16)]
    else:
        shapes = [
            jax.ShapeDtypeStruct((flat, 1), jnp.float32),
            jax.ShapeDtypeStruct((flat, 1), jnp.float32),
            jax.ShapeDtypeStruct((flat, head_size), jnp.float32),
        ]
        out_specs, scratch = [whole] * 3, []
    return pl.pallas_call(
        partial(
            attention_kernel,
            count=len(pieces),
            carry=state is not None,
            final=final,
            rows=rows,
            own=own,
            head_size=head_size,
            stride=stride,
        ),
        out_shape=shapes,
        in_specs=[pl.BlockSpec(memory_space=pltpu.SMEM)]
        + [whole] * (2 + len(pieces) + (0 if state is None else 3)),
        out_specs=out_specs,
        scratch_shapes=scratch,
        compiler_params=pltpu.CompilerParams(vmem_limit_bytes=24 * 1024 * 1024),
        cost_estimate=pl.CostEstimate(
            flops=4 * flat * width * head_size,
            bytes_accessed=4 * flat * head_size + 4 * width * head_size,
            transcendentals=flat * width,
        ),
        name="attend_last" if final else "attend_part",
    )(span, place, query_flat, *pieces, *(() if state is None else state))


def pick_kernel(tokens_ref, *refs, top, count, depth, shards, own):
    shard = lax.axis_index("fsdp")
    outs, sems = refs[:-1], refs[-1]
    copies = []
    for step in range(1, shards):
        start = pl.multiple_of(lax.rem(shard + step, shards) * depth, depth)
        copies.append(
            pltpu.make_async_copy(
                tokens_ref.at[pl.ds(top, count), pl.ds(start, depth)],
                outs[step - 1],
                sems.at[step - 1],
            )
        )
    if own:
        start = pl.multiple_of(shard * depth, depth)
        copies.append(
            pltpu.make_async_copy(
                tokens_ref.at[:, pl.ds(start, depth)], outs[shards - 1], sems.at[shards - 1]
            )
        )
    for copy in copies:
        copy.start()
    for copy in copies:
        copy.wait()


def pick(tokens, top, count, depth, shards, own):
    shapes = [jax.ShapeDtypeStruct((count, depth), tokens.dtype)] * (shards - 1)
    if own:
        shapes.append(jax.ShapeDtypeStruct((tokens.shape[0], depth), tokens.dtype))
    return pl.pallas_call(
        partial(pick_kernel, top=top, count=count, depth=depth, shards=shards, own=own),
        out_shape=shapes,
        in_specs=[pl.BlockSpec(memory_space=pl.ANY)],
        out_specs=[pl.BlockSpec(memory_space=pltpu.VMEM)] * len(shapes),
        scratch_shapes=[pltpu.SemaphoreType.DMA((shards,))],
        compiler_params=pltpu.CompilerParams(vmem_limit_bytes=60 * 1024 * 1024),
        name="pick_rest" if own else "pick_first",
    )(tokens)


def stages_of(contexts):
    bits = []
    bit = contexts // 2
    while bit >= 1:
        bits.append(bit)
        bit //= 2
    core = bits[-1:]
    rest = bits[:-1]
    stages = [rest[i : i + 2] for i in range(0, len(rest), 2)] + ([core] if core else [])
    return stages


def after(value, *earlier):
    return lax.optimization_barrier((value, *earlier))[0]


def make_local(contexts, shards, plan):
    def local(tokens, queries, key_weight, value_weight):
        rows = tokens.shape[0]
        depth, head_size = key_weight.shape
        heads = queries.shape[1] // head_size
        group_rows = shards * rows
        context = lax.axis_index("ctx")
        shard = lax.axis_index("fsdp")
        unit = rows // sum(sum(part) for part in plan)
        stages = stages_of(contexts)

        def send(columns):
            return [
                lax.ppermute(
                    columns[step - 1], "fsdp", [(i, (i + step) % shards) for i in range(shards)]
                )
                for step in range(1, shards)
            ]

        def rows_of(table, top, count):
            return table.reshape(shards, rows, -1)[:, top : top + count].reshape(
                shards * count, -1
            )

        class Part:
            pass

        parts = []
        chunks = []
        top = 0
        for sizes in plan:
            part = Part()
            part.top = top
            part.rows = sum(sizes) * unit
            part.first = len(chunks)
            for size in sizes:
                chunks.append((top, size * unit))
                top += size * unit
            part.end = len(chunks)
            part.stage = 0
            parts.append(part)
        early, late = parts

        first_rows = chunks[0][1]
        first_columns = pick(tokens, 0, first_rows, depth, shards, False)
        rest = pick(
            after(tokens, *first_columns), first_rows, rows - first_rows, depth, shards, True
        )
        own_columns = rest[-1]
        flying = [send(first_columns)]

        def send_rows(chunk, *earlier):
            top, count = chunk
            source = [after(columns, *earlier) if earlier else columns for columns in rest[:-1]]
            columns = [
                lax.slice_in_dim(block, top - first_rows, top - first_rows + count, axis=0)
                for block in source
            ]
            return send(columns)

        for chunk in chunks[1 : early.end + 1]:
            flying.append(send_rows(chunk))

        def project(columns):
            return jnp.concatenate(
                [
                    jnp.dot(columns, weight, preferred_element_type=jnp.float32)
                    for weight in (key_weight, value_weight)
                ],
                axis=1,
            )

        own_product = project(own_columns)

        start = context * group_rows
        positions = start + jnp.arange(group_rows, dtype=jnp.int32)
        cosine, sine_table = tables(positions, head_size)
        own_cosine = lax.dynamic_slice_in_dim(cosine, shard * rows, rows, 0)
        own_sine = lax.dynamic_slice_in_dim(sine_table, shard * rows, rows, 0)
        by_head = queries.astype(jnp.float32).reshape(rows, heads, head_size).transpose(1, 0, 2)
        query_flat = (
            rotate(by_head, own_cosine[None], own_sine[None])
            .astype(jnp.bfloat16)
            .reshape(heads * rows, head_size)
        )
        span = jnp.stack([start, start + shard * rows]).astype(jnp.int32)
        own_product, cosine, sine_table, query_flat, span = lax.optimization_barrier(
            (own_product, cosine, sine_table, query_flat, span)
        )

        def exchange(part):
            gate = own_product
            arrived = []
            for number in range(part.first, part.end):
                chunk, gate = lax.optimization_barrier((flying[number], gate))
                gate = [project(columns) for columns in chunk]
                arrived.append(gate)
            products = [own_product[part.top : part.top + part.rows]] + [
                jnp.concatenate([chunk[step] for chunk in arrived], axis=0)
                for step in range(shards - 1)
            ]
            if shards == 2:
                sums = jnp.concatenate(
                    [
                        jnp.where(shard == 0, products[0], products[1]),
                        jnp.where(shard == 0, products[1], products[0]),
                    ],
                    axis=0,
                )
            else:
                sums = jnp.zeros((shards * part.rows, 2 * head_size), jnp.float32)
                for step in range(shards):
                    source = lax.rem(shard + shards - step, shards)
                    sums = lax.dynamic_update_slice_in_dim(
                        sums, products[step], source * part.rows, 0
                    )
            part.sums = after(sums)
            part.other = jnp.zeros_like(sums)
            reach = 1
            while reach < shards:
                if reach > 1:
                    part.sums = part.sums + part.other
                part.other = lax.ppermute(
                    part.sums, "fsdp", [(i, i ^ reach) for i in range(shards)]
                )
                reach *= 2

        def combine(part, *gate):
            own, other = lax.optimization_barrier((part.sums, part.other, *gate))[:2]
            sums = own + other
            keys_rot = rotate(
                sums[:, :head_size],
                rows_of(cosine, part.top, part.rows),
                rows_of(sine_table, part.top, part.rows),
            ).astype(jnp.bfloat16)
            block = after(
                jnp.concatenate([keys_rot, sums[:, head_size:].astype(jnp.bfloat16)], axis=1)
            )
            part.cache = lax.dynamic_slice_in_dim(block, shard * part.rows, part.rows, 0)
            part.known, part.fresh, part.masks = block, [], [0]

        def advance(part, *gate):
            fresh = lax.optimization_barrier((part.known, part.fresh, *gate))
            part.known = after(jnp.concatenate([fresh[0]] + list(fresh[1]), axis=0))
            part.fresh = []
            if part.stage < len(stages):
                moves = [0]
                for bit in stages[part.stage]:
                    moves = moves + [move ^ bit for move in moves]
                part.fresh = [
                    lax.ppermute(part.known, "ctx", [(i, i ^ move) for i in range(contexts)])
                    for move in moves[1:]
                ]
                part.known_masks = part.masks
                part.masks = [mask ^ move for move in moves for mask in part.masks]
            part.stage += 1

        def absorb(part, pieces, masks, own, state, last, *gate):
            local_pos = rows_of(
                jnp.arange(group_rows, dtype=jnp.int32)[:, None], part.top, part.rows
            )[:, 0]
            order = jnp.array(masks, jnp.int32)
            place = ((context ^ order)[:, None] * group_rows + local_pos[None, :]).reshape(1, -1)
            query = after(query_flat, *gate)
            return attend(span, place, query, pieces, own, state, last, rows)

        exchange(early)
        for chunk in chunks[early.end + 1 :]:
            flying.append(send_rows(chunk, early.sums))
        combine(early, *flying[early.end])
        advance(early)
        exchange(late)
        for stage in range(len(stages)):
            if early.stage < len(stages):
                advance(early, late.sums if stage == 0 else late.known)
            if stage == 0:
                combine(late, early.known)
                advance(late)
            elif stage < len(stages) - 1:
                advance(late, early.known)
        state = absorb(
            early,
            [early.known] + list(early.fresh),
            early.masks,
            shards * early.rows,
            None,
            False,
            late.known,
        )
        advance(late, *state)
        state = absorb(
            late, [late.known], late.known_masks, shards * late.rows, state, False
        )
        fresh_masks = late.masks[len(late.known_masks) :]
        attended = absorb(late, list(late.fresh), fresh_masks, 0, state, True)
        kv_cache = jnp.concatenate([part.cache for part in parts], axis=0)
        return (kv_cache, attended)

    return local


def solution(mesh):
    placed = (P(("ctx", "fsdp"), None), P(("ctx", "fsdp"), None), P("fsdp", None), P("fsdp", None))
    return jax.shard_map(
        make_local(mesh.shape["ctx"], mesh.shape["fsdp"], ((2, 3), (2, 1))),
        mesh=mesh,
        in_specs=placed,
        out_specs=(P(("ctx", "fsdp"), None), P(("ctx", "fsdp"), None)),
        check_vma=False,
    )
```

```python
from functools import partial
import math

import jax
import jax.numpy as jnp
from jax import lax
from jax.experimental import pallas as pl
from jax.experimental.pallas import tpu as pltpu
from jax.sharding import PartitionSpec as P

rope_base = 500000.0
floor_value = -1e30


def rotate(vectors, cosine, sine_table):
    middle = vectors.shape[-1] // 2
    leading = vectors[..., :middle]
    back_half = vectors[..., middle:]
    return jnp.concatenate(
        [leading * cosine - back_half * sine_table, back_half * cosine + leading * sine_table],
        axis=-1,
    )


def tables(positions, head_size):
    middle = head_size // 2
    frequency = rope_base ** (-jnp.arange(middle, dtype=jnp.float32) * 2.0 / head_size)
    angles = positions.astype(jnp.float32)[:, None] * frequency[None, :]
    return (jnp.cos(angles), jnp.sin(angles))


def attention_kernel(
    span_ref, place_ref, query_ref, *refs, count, carry, final, rows, own, head_size, stride
):
    pieces, refs = refs[:count], refs[count:]
    if carry:
        old_peak, old_total, old_sum = refs[:3]
        refs = refs[3:]
    start = span_ref[0]
    first = span_ref[1]
    factor = head_size ** (-0.5) * math.log2(math.e)
    flat = query_ref.shape[0]
    keys = jnp.concatenate([piece[:, :head_size] for piece in pieces], axis=0)
    values = jnp.concatenate([piece[:, head_size:] for piece in pieces], axis=0)
    width = keys.shape[0]
    edge = min(width, -(-own // 128) * 128)
    if edge:
        query_pos = first + lax.rem(
            lax.broadcasted_iota(jnp.int32, (stride, edge), 0), jnp.int32(rows)
        )
        diagonal = place_ref[:, :edge] <= query_pos
    bias = jnp.where(place_ref[...] < start, 0.0, floor_value).astype(jnp.float32)

    def one(part):
        place = pl.ds(pl.multiple_of(part * stride, stride), stride)
        scores = (
            lax.dot_general(
                query_ref[place, :],
                keys,
                (((1,), (1,)), ((), ())),
                preferred_element_type=jnp.float32,
            )
            * factor
        )
        masked = []
        if edge:
            masked.append(jnp.where(diagonal, scores[:, :edge], floor_value))
        if edge < width:
            masked.append(scores[:, edge:] + bias[:, edge:])
        masked = jnp.concatenate(masked, axis=1) if len(masked) > 1 else masked[0]
        peak = jnp.max(masked, axis=1, keepdims=True)
        if carry:
            peak = jnp.maximum(peak, old_peak[place, :])
        weights = jnp.exp2(masked - peak)
        total = jnp.sum(weights, axis=1, keepdims=True)
        numerator = jnp.dot(
            weights.astype(jnp.bfloat16), values, preferred_element_type=jnp.float32
        )
        if carry:
            shrink = jnp.exp2(old_peak[place, :] - peak)
            total = total + shrink * old_total[place, :]
            numerator = numerator + shrink * old_sum[place, :]
        if final:
            out_ref, scratch = refs
            scratch[place, :] = (numerator / total).astype(jnp.bfloat16)
        else:
            peak_ref, total_ref, sum_ref = refs
            peak_ref[place, :] = peak
            total_ref[place, :] = total
            sum_ref[place, :] = numerator

    if width <= 2048:
        for part in range(flat // stride):
            one(part)
    else:

        @pl.loop(0, flat // stride)
        def each(part):
            one(part)

    if final:
        out_ref, scratch = refs
        for head in range(flat // rows):
            out_ref[:, head * head_size : (head + 1) * head_size] = scratch[
                head * rows : (head + 1) * rows, :
            ]


def attend(span, place, query_flat, pieces, own, state, final, rows):
    flat, head_size = query_flat.shape
    width = sum(piece.shape[0] for piece in pieces)
    stride = math.gcd(flat, 256 if width <= 2048 else rows)
    whole = pl.BlockSpec(memory_space=pltpu.VMEM)
    if final:
        shapes = jax.ShapeDtypeStruct((rows, flat // rows * head_size), jnp.bfloat16)
        out_specs, scratch = whole, [pltpu.VMEM((flat, head_size), jnp.bfloat16)]
    else:
        shapes = [
            jax.ShapeDtypeStruct((flat, 1), jnp.float32),
            jax.ShapeDtypeStruct((flat, 1), jnp.float32),
            jax.ShapeDtypeStruct((flat, head_size), jnp.float32),
        ]
        out_specs, scratch = [whole] * 3, []
    return pl.pallas_call(
        partial(
            attention_kernel,
            count=len(pieces),
            carry=state is not None,
            final=final,
            rows=rows,
            own=own,
            head_size=head_size,
            stride=stride,
        ),
        out_shape=shapes,
        in_specs=[pl.BlockSpec(memory_space=pltpu.SMEM)]
        + [whole] * (2 + len(pieces) + (0 if state is None else 3)),
        out_specs=out_specs,
        scratch_shapes=scratch,
        compiler_params=pltpu.CompilerParams(vmem_limit_bytes=24 * 1024 * 1024),
        cost_estimate=pl.CostEstimate(
            flops=4 * flat * width * head_size,
            bytes_accessed=4 * flat * head_size + 4 * width * head_size,
            transcendentals=flat * width,
        ),
        name="attend_last" if final else "attend_part",
    )(span, place, query_flat, *pieces, *(() if state is None else state))


def stages_of(contexts):
    bits = []
    bit = contexts // 2
    while bit >= 1:
        bits.append(bit)
        bit //= 2
    core = bits[-1:]
    rest = bits[:-1]
    stages = [rest[i : i + 2] for i in range(0, len(rest), 2)] + ([core] if core else [])
    return stages


def after(value, *earlier):
    return lax.optimization_barrier((value, *earlier))[0]


def make_local(contexts, shards, plan):
    def local(tokens, queries, key_weight, value_weight):
        rows = tokens.shape[0]
        depth, head_size = key_weight.shape
        heads = queries.shape[1] // head_size
        group_rows = shards * rows
        context = lax.axis_index("ctx")
        shard = lax.axis_index("fsdp")
        unit = rows // sum(sum(part) for part in plan)
        stages = stages_of(contexts)

        def send_rows(chunk, *earlier):
            top, count = chunk
            source = after(tokens, *earlier) if earlier else tokens
            arrived, sent = [], []
            for step in range(1, shards):
                target = lax.rem(shard + step, shards)
                columns = lax.dynamic_slice(
                    source, (jnp.int32(top), target * depth), (count, depth)
                )
                sent.append(columns)
                arrived.append(
                    lax.ppermute(
                        columns, "fsdp", [(i, (i + step) % shards) for i in range(shards)]
                    )
                )
            return arrived, sent

        def places_of(top, count):
            turns = jnp.arange(shards, dtype=jnp.int32) * rows + top
            return (turns[:, None] + jnp.arange(count, dtype=jnp.int32)[None, :]).reshape(-1)

        class Part:
            pass

        parts = []
        chunks = []
        top = 0
        for sizes in plan:
            part = Part()
            part.top = top
            part.rows = sum(sizes) * unit
            part.first = len(chunks)
            for size in sizes:
                chunks.append((top, size * unit))
                top += size * unit
            part.end = len(chunks)
            part.stage = 0
            parts.append(part)
        early, late = parts

        flying = []
        sent = ()
        for chunk in chunks[: early.end + 1]:
            arrived, sent = send_rows(chunk, *sent)
            flying.append(arrived)

        def project(columns):
            return jnp.concatenate(
                [
                    jnp.dot(columns, weight, preferred_element_type=jnp.float32)
                    for weight in (key_weight, value_weight)
                ],
                axis=1,
            )

        own_columns = lax.dynamic_slice_in_dim(after(tokens, *sent), shard * depth, depth, 1)
        own_product = project(own_columns)

        start = context * group_rows
        first = start + shard * rows
        own_cosine, own_sine = tables(first + jnp.arange(rows, dtype=jnp.int32), head_size)
        by_head = queries.astype(jnp.float32).reshape(rows, heads, head_size).transpose(1, 0, 2)
        query_flat = (
            rotate(by_head, own_cosine[None], own_sine[None])
            .astype(jnp.bfloat16)
            .reshape(heads * rows, head_size)
        )
        span = jnp.stack([start, first]).astype(jnp.int32)
        for part in parts:
            part.tables = tables(start + places_of(part.top, part.rows), head_size)
        own_product, early.tables, late.tables, query_flat, span = lax.optimization_barrier(
            (own_product, early.tables, late.tables, query_flat, span)
        )

        def exchange(part, gate):
            arrived = []
            for number in range(part.first, part.end):
                chunk, gate = lax.optimization_barrier((flying[number], gate))
                gate = [project(columns) for columns in chunk]
                arrived.append(gate)
            products = [own_product[part.top : part.top + part.rows]] + [
                jnp.concatenate([chunk[step] for chunk in arrived], axis=0)
                for step in range(shards - 1)
            ]
            if shards == 2:
                sums = jnp.concatenate(
                    [
                        jnp.where(shard == 0, products[0], products[1]),
                        jnp.where(shard == 0, products[1], products[0]),
                    ],
                    axis=0,
                )
            else:
                sums = jnp.zeros((shards * part.rows, 2 * head_size), jnp.float32)
                for step in range(shards):
                    source = lax.rem(shard + shards - step, shards)
                    sums = lax.dynamic_update_slice_in_dim(
                        sums, products[step], source * part.rows, 0
                    )
            part.sums = after(sums)
            part.other = jnp.zeros_like(sums)
            reach = 1
            while reach < shards:
                if reach > 1:
                    part.sums = part.sums + part.other
                part.other = lax.ppermute(
                    part.sums, "fsdp", [(i, i ^ reach) for i in range(shards)]
                )
                reach *= 2

        def combine(part, *gate):
            own, other = lax.optimization_barrier((part.sums, part.other, *gate))[:2]
            sums = own + other
            keys_rot = rotate(sums[:, :head_size], *part.tables).astype(jnp.bfloat16)
            block = after(
                jnp.concatenate([keys_rot, sums[:, head_size:].astype(jnp.bfloat16)], axis=1)
            )
            part.cache = lax.dynamic_slice_in_dim(block, shard * part.rows, part.rows, 0)
            part.known, part.fresh, part.masks = block, [], [0]

        def advance(part, *gate):
            fresh = lax.optimization_barrier((part.known, part.fresh, *gate))
            part.known = after(jnp.concatenate([fresh[0]] + list(fresh[1]), axis=0))
            part.fresh = []
            if part.stage < len(stages):
                moves = [0]
                for bit in stages[part.stage]:
                    moves = moves + [move ^ bit for move in moves]
                part.fresh = [
                    lax.ppermute(part.known, "ctx", [(i, i ^ move) for i in range(contexts)])
                    for move in moves[1:]
                ]
                part.known_masks = part.masks
                part.masks = [mask ^ move for move in moves for mask in part.masks]
            part.stage += 1

        def absorb(part, pieces, masks, own, state, last, *gate):
            local_pos = places_of(part.top, part.rows)
            order = jnp.array(masks, jnp.int32)
            place = ((context ^ order)[:, None] * group_rows + local_pos[None, :]).reshape(1, -1)
            query = after(query_flat, *gate)
            return attend(span, place, query, pieces, own, state, last, rows)

        exchange(early, own_product)
        for chunk in chunks[early.end + 1 :]:
            flying.append(send_rows(chunk, early.sums)[0])
        combine(early, *flying[early.end])
        advance(early)
        exchange(late, early.known)
        for stage in range(len(stages)):
            if early.stage < len(stages):
                advance(early, late.sums if stage == 0 else late.known)
            if stage == 0:
                combine(late, early.known)
                advance(late)
            elif stage < len(stages) - 1:
                advance(late, early.known)
        state = absorb(
            early,
            [early.known] + list(early.fresh),
            early.masks,
            shards * early.rows,
            None,
            False,
            late.known,
        )
        advance(late, *state)
        state = absorb(
            late, [late.known], late.known_masks, shards * late.rows, state, False
        )
        fresh_masks = late.masks[len(late.known_masks) :]
        attended = absorb(late, list(late.fresh), fresh_masks, 0, state, True)
        kv_cache = jnp.concatenate([part.cache for part in parts], axis=0)
        return (kv_cache, attended)

    return local


def solution(mesh):
    placed = (P(("ctx", "fsdp"), None), P(("ctx", "fsdp"), None), P("fsdp", None), P("fsdp", None))
    return jax.shard_map(
        make_local(mesh.shape["ctx"], mesh.shape["fsdp"], ((1, 4), (2, 1))),
        mesh=mesh,
        in_specs=placed,
        out_specs=(P(("ctx", "fsdp"), None), P(("ctx", "fsdp"), None)),
        check_vma=False,
    )
```

```python
from functools import partial
import math

import jax
import jax.numpy as jnp
from jax import lax
from jax.experimental import pallas as pl
from jax.experimental.pallas import tpu as pltpu
from jax.sharding import PartitionSpec as P

rope_base = 500000.0
floor_value = -1e30


def rotate(vectors, cosine, sine_table):
    middle = vectors.shape[-1] // 2
    leading = vectors[..., :middle]
    back_half = vectors[..., middle:]
    return jnp.concatenate(
        [leading * cosine - back_half * sine_table, back_half * cosine + leading * sine_table],
        axis=-1,
    )


def tables(positions, head_size):
    middle = head_size // 2
    frequency = rope_base ** (-jnp.arange(middle, dtype=jnp.float32) * 2.0 / head_size)
    angles = positions.astype(jnp.float32)[:, None] * frequency[None, :]
    return (jnp.cos(angles), jnp.sin(angles))


def attention_kernel(
    span_ref, place_ref, query_ref, *refs, groups, carry, final, rows, own, head_size, stride
):
    count = len(groups)
    pieces, refs = refs[:count], refs[count:]
    if carry:
        old_peak, old_total, old_sum = refs[:3]
        refs = refs[3:]
    start = span_ref[0]
    first = span_ref[1]
    factor = head_size ** (-0.5) * math.log2(math.e)
    flat = query_ref.shape[0]
    ordered = []
    for half in range(2):
        for piece, group in zip(pieces, groups):
            for top in range(0, piece.shape[0], group):
                begin = top + half * (group // 2)
                ordered.append(piece[begin : begin + group // 2, :])
    everything = jnp.concatenate(ordered, axis=0)

    def run(width):
        keys = everything[:width, :head_size]
        values = everything[:width, head_size:]
        edge = min(width, -(-own // 128) * 128)
        if edge:
            query_pos = first + lax.rem(
                lax.broadcasted_iota(jnp.int32, (stride, edge), 0), jnp.int32(rows)
            )
            diagonal = place_ref[:, :edge] <= query_pos
        bias = jnp.where(place_ref[:, :width] < start, 0.0, floor_value).astype(jnp.float32)

        def one(part):
            place = pl.ds(pl.multiple_of(part * stride, stride), stride)
            scores = (
                lax.dot_general(
                    query_ref[place, :],
                    keys,
                    (((1,), (1,)), ((), ())),
                    preferred_element_type=jnp.float32,
                )
                * factor
            )
            masked = []
            if edge:
                masked.append(jnp.where(diagonal, scores[:, :edge], floor_value))
            if edge < width:
                masked.append(scores[:, edge:] + bias[:, edge:])
            masked = jnp.concatenate(masked, axis=1) if len(masked) > 1 else masked[0]
            peak = jnp.max(masked, axis=1, keepdims=True)
            if carry:
                peak = jnp.maximum(peak, old_peak[place, :])
            weights = jnp.exp2(masked - peak)
            total = jnp.sum(weights, axis=1, keepdims=True)
            numerator = jnp.dot(
                weights.astype(jnp.bfloat16), values, preferred_element_type=jnp.float32
            )
            if carry:
                shrink = jnp.exp2(old_peak[place, :] - peak)
                total = total + shrink * old_total[place, :]
                numerator = numerator + shrink * old_sum[place, :]
            if final:
                out_ref, scratch = refs
                scratch[place, :] = (numerator / total).astype(jnp.bfloat16)
            else:
                peak_ref, total_ref, sum_ref = refs
                peak_ref[place, :] = peak
                total_ref[place, :] = total
                sum_ref[place, :] = numerator

        if flat // stride <= 4:
            for part in range(flat // stride):
                one(part)
        else:

            @pl.loop(0, flat // stride)
            def each(part):
                one(part)

    upper = span_ref[2]

    @pl.when(upper == 1)
    def all_keys():
        run(everything.shape[0])

    @pl.when(upper == 0)
    def lower_keys():
        run(everything.shape[0] // 2)

    if final:
        out_ref, scratch = refs
        for head in range(flat // rows):
            out_ref[:, head * head_size : (head + 1) * head_size] = scratch[
                head * rows : (head + 1) * rows, :
            ]


def attend(span, place, query_flat, pieces, groups, own, state, final, rows):
    flat, head_size = query_flat.shape
    width = sum(piece.shape[0] for piece in pieces)
    stride = math.gcd(flat, 1024 if width <= 2048 else rows)
    whole = pl.BlockSpec(memory_space=pltpu.VMEM)
    if final:
        shapes = jax.ShapeDtypeStruct((rows, flat // rows * head_size), jnp.bfloat16)
        out_specs, scratch = whole, [pltpu.VMEM((flat, head_size), jnp.bfloat16)]
    else:
        shapes = [
            jax.ShapeDtypeStruct((flat, 1), jnp.float32),
            jax.ShapeDtypeStruct((flat, 1), jnp.float32),
            jax.ShapeDtypeStruct((flat, head_size), jnp.float32),
        ]
        out_specs, scratch = [whole] * 3, []
    return pl.pallas_call(
        partial(
            attention_kernel,
            groups=groups,
            carry=state is not None,
            final=final,
            rows=rows,
            own=own,
            head_size=head_size,
            stride=stride,
        ),
        out_shape=shapes,
        in_specs=[pl.BlockSpec(memory_space=pltpu.SMEM)]
        + [whole] * (2 + len(pieces) + (0 if state is None else 3)),
        out_specs=out_specs,
        scratch_shapes=scratch,
        compiler_params=pltpu.CompilerParams(vmem_limit_bytes=32 * 1024 * 1024),
        cost_estimate=pl.CostEstimate(
            flops=4 * flat * width * head_size,
            bytes_accessed=4 * flat * head_size + 4 * width * head_size,
            transcendentals=flat * width,
        ),
        name="attend_last" if final else "attend_part",
    )(span, place, query_flat, *pieces, *(() if state is None else state))


def stages_of(contexts):
    bits = []
    bit = contexts // 2
    while bit >= 1:
        bits.append(bit)
        bit //= 2
    core = bits[-1:]
    rest = bits[:-1]
    stages = [rest[i : i + 2] for i in range(0, len(rest), 2)] + ([core] if core else [])
    return stages


def after(value, *earlier):
    return lax.optimization_barrier((value, *earlier))[0]


def make_local(contexts, shards, plan):
    def local(tokens, queries, key_weight, value_weight):
        rows = tokens.shape[0]
        depth, head_size = key_weight.shape
        heads = queries.shape[1] // head_size
        group_rows = shards * rows
        context = lax.axis_index("ctx")
        shard = lax.axis_index("fsdp")
        unit = rows // sum(sum(part) for part in plan)
        stages = stages_of(contexts)

        def send_rows(chunk, *earlier):
            top, count = chunk
            source = after(tokens, *earlier) if earlier else tokens
            arrived, sent = [], []
            for step in range(1, shards):
                target = lax.rem(shard + step, shards)
                columns = lax.dynamic_slice(
                    source, (jnp.int32(top), target * depth), (count, depth)
                )
                sent.append(columns)
                arrived.append(
                    lax.ppermute(
                        columns, "fsdp", [(i, (i + step) % shards) for i in range(shards)]
                    )
                )
            return arrived, sent

        def places_of(top, count):
            turns = jnp.arange(shards, dtype=jnp.int32) * rows + top
            return (turns[:, None] + jnp.arange(count, dtype=jnp.int32)[None, :]).reshape(-1)

        class Part:
            pass

        parts = []
        chunks = []
        top = 0
        for sizes in plan:
            part = Part()
            part.top = top
            part.rows = sum(sizes) * unit
            part.first = len(chunks)
            for size in sizes:
                chunks.append((top, size * unit))
                top += size * unit
            part.end = len(chunks)
            part.stage = 0
            parts.append(part)
        early, late = parts

        flying = []
        sent = ()
        for chunk in chunks[: early.end + 1]:
            arrived, sent = send_rows(chunk, *sent)
            flying.append(arrived)

        def project(columns):
            return jnp.concatenate(
                [
                    jnp.dot(columns, weight, preferred_element_type=jnp.float32)
                    for weight in (key_weight, value_weight)
                ],
                axis=1,
            )

        own_columns = lax.dynamic_slice_in_dim(after(tokens, *sent), shard * depth, depth, 1)
        own_product = project(own_columns)

        start = context * group_rows
        first = start + shard * rows
        own_cosine, own_sine = tables(first + jnp.arange(rows, dtype=jnp.int32), head_size)
        by_head = queries.astype(jnp.float32).reshape(rows, heads, head_size).transpose(1, 0, 2)
        query_flat = (
            rotate(by_head, own_cosine[None], own_sine[None])
            .astype(jnp.bfloat16)
            .reshape(heads * rows, head_size)
        )
        top_unit = min(stages[0])
        top_count = contexts // top_unit
        level = context // top_unit
        upper = (2 * level >= top_count).astype(jnp.int32)
        span = jnp.stack([start, first, upper]).astype(jnp.int32)
        for part in parts:
            part.tables = tables(start + places_of(part.top, part.rows), head_size)
        own_product, early.tables, late.tables, query_flat, span = lax.optimization_barrier(
            (own_product, early.tables, late.tables, query_flat, span)
        )

        def exchange(part, gate):
            arrived = []
            for number in range(part.first, part.end):
                chunk, gate = lax.optimization_barrier((flying[number], gate))
                gate = [project(columns) for columns in chunk]
                arrived.append(gate)
            products = [own_product[part.top : part.top + part.rows]] + [
                jnp.concatenate([chunk[step] for chunk in arrived], axis=0)
                for step in range(shards - 1)
            ]
            if shards == 2:
                sums = jnp.concatenate(
                    [
                        jnp.where(shard == 0, products[0], products[1]),
                        jnp.where(shard == 0, products[1], products[0]),
                    ],
                    axis=0,
                )
            else:
                sums = jnp.zeros((shards * part.rows, 2 * head_size), jnp.float32)
                for step in range(shards):
                    source = lax.rem(shard + shards - step, shards)
                    sums = lax.dynamic_update_slice_in_dim(
                        sums, products[step], source * part.rows, 0
                    )
            part.sums = after(sums)
            part.other = jnp.zeros_like(sums)
            reach = 1
            while reach < shards:
                if reach > 1:
                    part.sums = part.sums + part.other
                part.other = lax.ppermute(
                    part.sums, "fsdp", [(i, i ^ reach) for i in range(shards)]
                )
                reach *= 2

        def combine(part, *gate):
            own, other = lax.optimization_barrier((part.sums, part.other, *gate))[:2]
            sums = own + other
            keys_rot = rotate(sums[:, :head_size], *part.tables).astype(jnp.bfloat16)
            block = after(
                jnp.concatenate([keys_rot, sums[:, head_size:].astype(jnp.bfloat16)], axis=1)
            )
            part.cache = lax.dynamic_slice_in_dim(block, shard * part.rows, part.rows, 0)
            part.known, part.fresh, part.masks = block, [], [(0, 0)]

        def advance(part, *gate):
            fresh = lax.optimization_barrier((part.known, part.fresh, *gate))
            part.known = after(jnp.concatenate([fresh[0]] + list(fresh[1]), axis=0))
            part.fresh = []
            if part.stage == 0:
                climbs = range(1, top_count)
                part.fresh = [
                    lax.ppermute(
                        part.known,
                        "ctx",
                        [(i, i + top_unit * up) for i in range(contexts - top_unit * up)],
                    )
                    for up in climbs
                ]
                part.masks = [(0, up) for up in range(top_count)]
                part.group = top_count * part.known.shape[0]
            elif part.stage < len(stages):
                moves = [0]
                for bit in stages[part.stage]:
                    moves = moves + [move ^ bit for move in moves]
                part.fresh = [
                    lax.ppermute(part.known, "ctx", [(i, i ^ move) for i in range(contexts)])
                    for move in moves[1:]
                ]
                part.known_masks = part.masks
                part.masks = [(mask ^ move, up) for move in moves for mask, up in part.masks]
            part.stage += 1

        def absorb(part, pieces, masks, own, state, last, *gate):
            local_pos = places_of(part.top, part.rows)
            turns, climbs = [], []
            for half in range(2):
                for index, (mask, up) in enumerate(masks):
                    if (2 * up >= top_count) == (half == 1):
                        turns.append(mask)
                        climbs.append(up)
            climbs = jnp.array(climbs, jnp.int32)
            sources = (context ^ jnp.array(turns, jnp.int32)) - climbs * top_unit
            place = sources[:, None] * group_rows + local_pos[None, :]
            place = jnp.where((climbs <= level)[:, None], place, contexts * group_rows)
            query = after(query_flat, *gate)
            groups = tuple(min(part.group, piece.shape[0]) for piece in pieces)
            return attend(
                span, place.reshape(1, -1), query, pieces, groups, own, state, last, rows
            )

        exchange(early, own_product)
        for chunk in chunks[early.end + 1 :]:
            flying.append(send_rows(chunk, early.sums)[0])
        combine(early, *flying[early.end])
        advance(early)
        exchange(late, early.known)
        for stage in range(len(stages)):
            if early.stage < len(stages):
                advance(early, late.sums if stage == 0 else late.known)
            if stage == 0:
                combine(late, early.known)
                advance(late)
            elif stage < len(stages) - 1:
                advance(late, early.known)
        state = absorb(
            early,
            [early.known] + list(early.fresh),
            early.masks,
            shards * early.rows,
            None,
            False,
            late.known,
        )
        advance(late, *state)
        state = absorb(
            late, [late.known], late.known_masks, shards * late.rows, state, False
        )
        fresh_masks = late.masks[len(late.known_masks) :]
        attended = absorb(late, list(late.fresh), fresh_masks, 0, state, True)
        kv_cache = jnp.concatenate([part.cache for part in parts], axis=0)
        return (kv_cache, attended)

    return local


def solution(mesh):
    placed = (P(("ctx", "fsdp"), None), P(("ctx", "fsdp"), None), P("fsdp", None), P("fsdp", None))
    return jax.shard_map(
        make_local(mesh.shape["ctx"], mesh.shape["fsdp"], ((1, 4), (2, 1))),
        mesh=mesh,
        in_specs=placed,
        out_specs=(P(("ctx", "fsdp"), None), P(("ctx", "fsdp"), None)),
        check_vma=False,
    )
```

```python
from functools import partial
import math

import jax
import jax.numpy as jnp
from jax import lax
from jax.experimental import pallas as pl
from jax.experimental.pallas import tpu as pltpu
from jax.sharding import PartitionSpec as P

rope_base = 500000.0
floor_value = -1e30


def rotate(vectors, cosine, sine_table):
    middle = vectors.shape[-1] // 2
    leading = vectors[..., :middle]
    back_half = vectors[..., middle:]
    return jnp.concatenate(
        [leading * cosine - back_half * sine_table, back_half * cosine + leading * sine_table],
        axis=-1,
    )


def tables(positions, head_size):
    middle = head_size // 2
    frequency = rope_base ** (-jnp.arange(middle, dtype=jnp.float32) * 2.0 / head_size)
    angles = positions.astype(jnp.float32)[:, None] * frequency[None, :]
    return (jnp.cos(angles), jnp.sin(angles))


def attention_kernel(
    span_ref, place_ref, query_ref, *refs, count, order, carry, final, rows, own, head_size, stride
):
    pieces, refs = refs[:count], refs[count:]
    if carry:
        old_peak, old_total, old_sum = refs[:3]
        refs = refs[3:]
    start = span_ref[0]
    first = span_ref[1]
    factor = head_size ** (-0.5) * math.log2(math.e)
    flat = query_ref.shape[0]
    blocks = []
    size = sum(piece.shape[0] for piece in pieces) // len(order)
    for piece in pieces:
        blocks.extend(piece[top : top + size, :] for top in range(0, piece.shape[0], size))
    ordered = [blocks[index] for index in order]
    everything = jnp.concatenate(ordered, axis=0)

    def run(width):
        keys = everything[:width, :head_size]
        values = everything[:width, head_size:]
        edge = min(width, -(-own // 128) * 128)
        if edge:
            query_pos = first + lax.rem(
                lax.broadcasted_iota(jnp.int32, (stride, edge), 0), jnp.int32(rows)
            )
            diagonal = place_ref[:, :edge] <= query_pos
        bias = jnp.where(place_ref[:, :width] < start, 0.0, floor_value).astype(jnp.float32)

        def one(part):
            place = pl.ds(pl.multiple_of(part * stride, stride), stride)
            scores = (
                lax.dot_general(
                    query_ref[place, :],
                    keys,
                    (((1,), (1,)), ((), ())),
                    preferred_element_type=jnp.float32,
                )
                * factor
            )
            masked = []
            if edge:
                masked.append(jnp.where(diagonal, scores[:, :edge], floor_value))
            if edge < width:
                masked.append(scores[:, edge:] + bias[:, edge:])
            masked = jnp.concatenate(masked, axis=1) if len(masked) > 1 else masked[0]
            peak = jnp.max(masked, axis=1, keepdims=True)
            if carry:
                peak = jnp.maximum(peak, old_peak[place, :])
            weights = jnp.exp2(masked - peak)
            total = jnp.sum(weights, axis=1, keepdims=True)
            numerator = jnp.dot(
                weights.astype(jnp.bfloat16), values, preferred_element_type=jnp.float32
            )
            if carry:
                shrink = jnp.exp2(old_peak[place, :] - peak)
                total = total + shrink * old_total[place, :]
                numerator = numerator + shrink * old_sum[place, :]
            if final:
                out_ref, scratch = refs
                scratch[place, :] = (numerator / total).astype(jnp.bfloat16)
            else:
                peak_ref, total_ref, sum_ref = refs
                peak_ref[place, :] = peak
                total_ref[place, :] = total
                sum_ref[place, :] = numerator

        @pl.loop(0, flat // stride)
        def each(part):
            one(part)

    upper = span_ref[2]

    @pl.when(upper == 1)
    def all_keys():
        run(everything.shape[0])

    @pl.when(upper == 0)
    def lower_keys():
        run(everything.shape[0] // 2)

    if final:
        out_ref, scratch = refs
        for head in range(flat // rows):
            out_ref[:, head * head_size : (head + 1) * head_size] = scratch[
                head * rows : (head + 1) * rows, :
            ]


def attend(span, place, query_flat, pieces, order, own, state, final, rows):
    flat, head_size = query_flat.shape
    width = sum(piece.shape[0] for piece in pieces)
    stride = math.gcd(flat, 256 if width <= 2048 else rows)
    whole = pl.BlockSpec(memory_space=pltpu.VMEM)
    if final:
        shapes = jax.ShapeDtypeStruct((rows, flat // rows * head_size), jnp.bfloat16)
        out_specs, scratch = whole, [pltpu.VMEM((flat, head_size), jnp.bfloat16)]
    else:
        shapes = [
            jax.ShapeDtypeStruct((flat, 1), jnp.float32),
            jax.ShapeDtypeStruct((flat, 1), jnp.float32),
            jax.ShapeDtypeStruct((flat, head_size), jnp.float32),
        ]
        out_specs, scratch = [whole] * 3, []
    return pl.pallas_call(
        partial(
            attention_kernel,
            count=len(pieces),
            order=order,
            carry=state is not None,
            final=final,
            rows=rows,
            own=own,
            head_size=head_size,
            stride=stride,
        ),
        out_shape=shapes,
        in_specs=[pl.BlockSpec(memory_space=pltpu.SMEM)]
        + [whole] * (2 + len(pieces) + (0 if state is None else 3)),
        out_specs=out_specs,
        scratch_shapes=scratch,
        compiler_params=pltpu.CompilerParams(vmem_limit_bytes=32 * 1024 * 1024),
        cost_estimate=pl.CostEstimate(
            flops=4 * flat * width * head_size,
            bytes_accessed=4 * flat * head_size + 4 * width * head_size,
            transcendentals=flat * width,
        ),
        name="attend_last" if final else "attend_part",
    )(span, place, query_flat, *pieces, *(() if state is None else state))


def stages_of(contexts):
    bits = []
    bit = contexts // 2
    while bit >= 1:
        bits.append(bit)
        bit //= 2
    return bits


def after(value, *earlier):
    return lax.optimization_barrier((value, *earlier))[0]


def make_local(contexts, shards, plan):
    def local(tokens, queries, key_weight, value_weight):
        rows = tokens.shape[0]
        depth, head_size = key_weight.shape
        heads = queries.shape[1] // head_size
        group_rows = shards * rows
        context = lax.axis_index("ctx")
        shard = lax.axis_index("fsdp")
        unit = rows // sum(sum(part) for part in plan)
        stages = stages_of(contexts)

        def send_rows(chunk, *earlier):
            top, count = chunk
            source = after(tokens, *earlier) if earlier else tokens
            arrived, sent = [], []
            for step in range(1, shards):
                target = lax.rem(shard + step, shards)
                columns = lax.dynamic_slice(
                    source, (jnp.int32(top), target * depth), (count, depth)
                )
                sent.append(columns)
                arrived.append(
                    lax.ppermute(
                        columns, "fsdp", [(i, (i + step) % shards) for i in range(shards)]
                    )
                )
            return arrived, sent

        def places_of(top, count):
            turns = jnp.arange(shards, dtype=jnp.int32) * rows + top
            return (turns[:, None] + jnp.arange(count, dtype=jnp.int32)[None, :]).reshape(-1)

        class Part:
            pass

        parts = []
        chunks = []
        top = 0
        for sizes in plan:
            part = Part()
            part.top = top
            part.rows = sum(sizes) * unit
            part.first = len(chunks)
            for size in sizes:
                chunks.append((top, size * unit))
                top += size * unit
            part.end = len(chunks)
            part.stage = 0
            parts.append(part)
        early, late = parts

        flying = []
        sent = ()
        for chunk in chunks[: early.end + 1]:
            arrived, sent = send_rows(chunk, *sent)
            flying.append(arrived)

        def project(columns):
            return jnp.concatenate(
                [
                    jnp.dot(columns, weight, preferred_element_type=jnp.float32)
                    for weight in (key_weight, value_weight)
                ],
                axis=1,
            )

        own_columns = lax.dynamic_slice_in_dim(after(tokens, *sent), shard * depth, depth, 1)
        own_product = project(own_columns)

        start = context * group_rows
        first = start + shard * rows
        own_cosine, own_sine = tables(first + jnp.arange(rows, dtype=jnp.int32), head_size)
        by_head = queries.astype(jnp.float32).reshape(rows, heads, head_size).transpose(1, 0, 2)
        query_flat = (
            rotate(by_head, own_cosine[None], own_sine[None])
            .astype(jnp.bfloat16)
            .reshape(heads * rows, head_size)
        )
        top_bit = stages[0]
        upper = ((context & top_bit) != 0).astype(jnp.int32)
        span = jnp.stack([start, first, upper]).astype(jnp.int32)
        for part in parts:
            part.tables = tables(start + places_of(part.top, part.rows), head_size)
        own_product, early.tables, late.tables, query_flat, span = lax.optimization_barrier(
            (own_product, early.tables, late.tables, query_flat, span)
        )

        def exchange(part, gate):
            arrived = []
            for number in range(part.first, part.end):
                chunk, gate = lax.optimization_barrier((flying[number], gate))
                gate = [project(columns) for columns in chunk]
                arrived.append(gate)
            products = [own_product[part.top : part.top + part.rows]] + [
                jnp.concatenate([chunk[step] for chunk in arrived], axis=0)
                for step in range(shards - 1)
            ]
            if shards == 2:
                sums = jnp.concatenate(
                    [
                        jnp.where(shard == 0, products[0], products[1]),
                        jnp.where(shard == 0, products[1], products[0]),
                    ],
                    axis=0,
                )
            else:
                sums = jnp.zeros((shards * part.rows, 2 * head_size), jnp.float32)
                for step in range(shards):
                    source = lax.rem(shard + shards - step, shards)
                    sums = lax.dynamic_update_slice_in_dim(
                        sums, products[step], source * part.rows, 0
                    )
            part.sums = after(sums)
            part.other = jnp.zeros_like(sums)
            reach = 1
            while reach < shards:
                if reach > 1:
                    part.sums = part.sums + part.other
                part.other = lax.ppermute(
                    part.sums, "fsdp", [(i, i ^ reach) for i in range(shards)]
                )
                reach *= 2

        def combine(part, *gate):
            own, other = lax.optimization_barrier((part.sums, part.other, *gate))[:2]
            sums = own + other
            keys_rot = rotate(sums[:, :head_size], *part.tables).astype(jnp.bfloat16)
            block = after(
                jnp.concatenate([keys_rot, sums[:, head_size:].astype(jnp.bfloat16)], axis=1)
            )
            part.cache = lax.dynamic_slice_in_dim(block, shard * part.rows, part.rows, 0)
            part.known, part.fresh, part.masks = block, [], [0]

        def advance(part, *gate):
            fresh = lax.optimization_barrier((part.known, part.fresh, *gate))
            part.known = after(jnp.concatenate([fresh[0]] + list(fresh[1]), axis=0))
            part.fresh = []
            if part.stage < len(stages):
                bit = stages[part.stage]
                pairs = [(i, i ^ bit) for i in range(contexts)]
                part.fresh = [lax.ppermute(part.known, "ctx", pairs)]
                part.masks = part.masks + [mask ^ bit for mask in part.masks]
            part.stage += 1

        def absorb(part, pieces, masks, own, state, last, *gate):
            local_pos = places_of(part.top, part.rows)
            order = sorted(range(len(masks)), key=lambda index: masks[index] & top_bit)
            turns = jnp.array([masks[index] for index in order], jnp.int32)
            place = (context ^ turns)[:, None] * group_rows + local_pos[None, :]
            query = after(query_flat, *gate)
            return attend(
                span, place.reshape(1, -1), query, pieces, tuple(order), own, state, last, rows
            )

        exchange(early, own_product)
        for chunk in chunks[early.end + 1 :]:
            flying.append(send_rows(chunk, early.sums)[0])
        combine(early, *flying[early.end])
        advance(early)
        exchange(late, early.known)
        advance(early, late.sums)
        combine(late, early.known)
        advance(late)
        for stage in range(2, len(stages)):
            advance(early, late.known)
            advance(late, early.known)
        state = absorb(
            early,
            [early.known] + early.fresh,
            early.masks,
            shards * early.rows,
            None,
            False,
            late.known,
        )
        advance(late, *state)
        attended = absorb(
            late, [late.known] + late.fresh, late.masks, shards * late.rows, state, True
        )
        kv_cache = jnp.concatenate([part.cache for part in parts], axis=0)
        return (kv_cache, attended)

    return local


def solution(mesh):
    placed = (P(("ctx", "fsdp"), None), P(("ctx", "fsdp"), None), P("fsdp", None), P("fsdp", None))
    return jax.shard_map(
        make_local(mesh.shape["ctx"], mesh.shape["fsdp"], ((1, 4), (2, 1))),
        mesh=mesh,
        in_specs=placed,
        out_specs=(P(("ctx", "fsdp"), None), P(("ctx", "fsdp"), None)),
        check_vma=False,
    )
```

```python
from functools import partial
import math

import jax
import jax.numpy as jnp
from jax import lax
from jax.experimental import pallas as pl
from jax.experimental.pallas import tpu as pltpu
from jax.sharding import PartitionSpec as P

rope_base = 500000.0
floor_value = -1e30


def rotate(vectors, cosine, sine_table):
    middle = vectors.shape[-1] // 2
    leading = vectors[..., :middle]
    back_half = vectors[..., middle:]
    return jnp.concatenate(
        [leading * cosine - back_half * sine_table, back_half * cosine + leading * sine_table],
        axis=-1,
    )


def tables(positions, head_size):
    middle = head_size // 2
    frequency = rope_base ** (-jnp.arange(middle, dtype=jnp.float32) * 2.0 / head_size)
    angles = positions.astype(jnp.float32)[:, None] * frequency[None, :]
    return (jnp.cos(angles), jnp.sin(angles))


def attention_kernel(
    span_ref, place_ref, query_ref, *refs, count, slots, carry, final, rows, own, head_size, stride
):
    pieces, refs = refs[:count], refs[count:]
    if carry:
        old_peak, old_total, old_sum = refs[:3]
        refs = refs[3:]
    start = span_ref[0]
    first = span_ref[1]
    factor = head_size ** (-0.5) * math.log2(math.e)
    flat = query_ref.shape[0]
    size = sum(piece.shape[0] for piece in pieces) // (2 * slots * count)
    ordered = []
    for half in range(2):
        for index, piece in enumerate(pieces):
            for slot in range(slots):
                number = span_ref[3 + (index * 2 + half) * slots + slot]
                ordered.append(piece[pl.ds(pl.multiple_of(number * size, size), size), :])
    everything = jnp.concatenate(ordered, axis=0)

    def run(width):
        keys = everything[:width, :head_size]
        values = everything[:width, head_size:]
        edge = min(width, -(-own // 128) * 128)
        if edge:
            query_pos = first + lax.rem(
                lax.broadcasted_iota(jnp.int32, (stride, edge), 0), jnp.int32(rows)
            )
            diagonal = place_ref[:, :edge] <= query_pos
        bias = jnp.where(place_ref[:, :width] < start, 0.0, floor_value).astype(jnp.float32)

        def one(part):
            place = pl.ds(pl.multiple_of(part * stride, stride), stride)
            scores = (
                lax.dot_general(
                    query_ref[place, :],
                    keys,
                    (((1,), (1,)), ((), ())),
                    preferred_element_type=jnp.float32,
                )
                * factor
            )
            masked = []
            if edge:
                masked.append(jnp.where(diagonal, scores[:, :edge], floor_value))
            if edge < width:
                masked.append(scores[:, edge:] + bias[:, edge:])
            masked = jnp.concatenate(masked, axis=1) if len(masked) > 1 else masked[0]
            peak = jnp.max(masked, axis=1, keepdims=True)
            if carry:
                peak = jnp.maximum(peak, old_peak[place, :])
            weights = jnp.exp2(masked - peak)
            total = jnp.sum(weights, axis=1, keepdims=True)
            numerator = jnp.dot(
                weights.astype(jnp.bfloat16), values, preferred_element_type=jnp.float32
            )
            if carry:
                shrink = jnp.exp2(old_peak[place, :] - peak)
                total = total + shrink * old_total[place, :]
                numerator = numerator + shrink * old_sum[place, :]
            if final:
                out_ref, scratch = refs
                scratch[place, :] = (numerator / total).astype(jnp.bfloat16)
            else:
                peak_ref, total_ref, sum_ref = refs
                peak_ref[place, :] = peak
                total_ref[place, :] = total
                sum_ref[place, :] = numerator

        if flat // stride <= 8:
            for part in range(flat // stride):
                one(part)
        else:

            @pl.loop(0, flat // stride)
            def each(part):
                one(part)

    upper = span_ref[2]

    @pl.when(upper == 1)
    def all_keys():
        run(everything.shape[0])

    @pl.when(upper == 0)
    def lower_keys():
        run(everything.shape[0] // 2)

    if final:
        out_ref, scratch = refs
        for head in range(flat // rows):
            out_ref[:, head * head_size : (head + 1) * head_size] = scratch[
                head * rows : (head + 1) * rows, :
            ]


def attend(span, place, query_flat, pieces, slots, own, state, final, rows):
    flat, head_size = query_flat.shape
    width = sum(piece.shape[0] for piece in pieces)
    stride = math.gcd(flat, 256 if width <= 2048 else rows)
    whole = pl.BlockSpec(memory_space=pltpu.VMEM)
    if final:
        shapes = jax.ShapeDtypeStruct((rows, flat // rows * head_size), jnp.bfloat16)
        out_specs, scratch = whole, [pltpu.VMEM((flat, head_size), jnp.bfloat16)]
    else:
        shapes = [
            jax.ShapeDtypeStruct((flat, 1), jnp.float32),
            jax.ShapeDtypeStruct((flat, 1), jnp.float32),
            jax.ShapeDtypeStruct((flat, head_size), jnp.float32),
        ]
        out_specs, scratch = [whole] * 3, []
    return pl.pallas_call(
        partial(
            attention_kernel,
            count=len(pieces),
            slots=slots,
            carry=state is not None,
            final=final,
            rows=rows,
            own=own,
            head_size=head_size,
            stride=stride,
        ),
        out_shape=shapes,
        in_specs=[pl.BlockSpec(memory_space=pltpu.SMEM)]
        + [whole] * (2 + len(pieces) + (0 if state is None else 3)),
        out_specs=out_specs,
        scratch_shapes=scratch,
        compiler_params=pltpu.CompilerParams(vmem_limit_bytes=32 * 1024 * 1024),
        cost_estimate=pl.CostEstimate(
            flops=4 * flat * width * head_size,
            bytes_accessed=4 * flat * head_size + 4 * width * head_size,
            transcendentals=flat * width,
        ),
        name="attend_last" if final else "attend_part",
    )(span, place, query_flat, *pieces, *(() if state is None else state))


def stages_of(contexts):
    bits = []
    bit = contexts // 2
    while bit >= 1:
        bits.append(bit)
        bit //= 2
    inner = bits[:-1]
    turn = len(inner) // 2 if len(inner) > 3 else len(inner) - 1
    paths = (inner + bits[-1:], inner[turn:] + inner[:turn] + bits[-1:])
    masks = ([0], [0])
    for first, second in zip(*paths):
        masks = (
            masks[0] + [mask ^ first for mask in masks[0 if first > 1 else 1]],
            masks[1] + [mask ^ second for mask in masks[1 if second > 1 else 0]],
        )
    return paths, masks


def after(value, *earlier):
    return lax.optimization_barrier((value, *earlier))[0]


def make_local(contexts, shards, plan):
    def local(tokens, queries, key_weight, value_weight):
        rows = tokens.shape[0]
        depth, head_size = key_weight.shape
        heads = queries.shape[1] // head_size
        group_rows = shards * rows
        context = lax.axis_index("ctx")
        shard = lax.axis_index("fsdp")
        unit = rows // sum(sum(part) for part in plan)
        paths, all_masks = stages_of(contexts)
        stages = paths[0]
        core = context & 1

        def send_rows(chunk, *earlier):
            top, count = chunk
            source = after(tokens, *earlier) if earlier else tokens
            arrived, sent = [], []
            for step in range(1, shards):
                target = lax.rem(shard + step, shards)
                columns = lax.dynamic_slice(
                    source, (jnp.int32(top), target * depth), (count, depth)
                )
                sent.append(columns)
                arrived.append(
                    lax.ppermute(
                        columns, "fsdp", [(i, (i + step) % shards) for i in range(shards)]
                    )
                )
            return arrived, sent

        def places_of(top, count):
            turns = jnp.arange(shards, dtype=jnp.int32) * rows + top
            return (turns[:, None] + jnp.arange(count, dtype=jnp.int32)[None, :]).reshape(-1)

        class Part:
            pass

        parts = []
        chunks = []
        top = 0
        for sizes in plan:
            part = Part()
            part.top = top
            part.rows = sum(sizes) * unit
            part.first = len(chunks)
            for size in sizes:
                chunks.append((top, size * unit))
                top += size * unit
            part.end = len(chunks)
            part.stage = 0
            parts.append(part)
        early, late = parts

        flying = []
        sent = ()
        for chunk in chunks[: early.end + 1]:
            arrived, sent = send_rows(chunk, *sent)
            flying.append(arrived)

        def project(columns):
            return jnp.concatenate(
                [
                    jnp.dot(columns, weight, preferred_element_type=jnp.float32)
                    for weight in (key_weight, value_weight)
                ],
                axis=1,
            )

        own_columns = lax.dynamic_slice_in_dim(after(tokens, *sent), shard * depth, depth, 1)
        own_product = project(own_columns)

        start = context * group_rows
        first = start + shard * rows
        own_cosine, own_sine = tables(first + jnp.arange(rows, dtype=jnp.int32), head_size)
        by_head = queries.astype(jnp.float32).reshape(rows, heads, head_size).transpose(1, 0, 2)
        query_flat = (
            rotate(by_head, own_cosine[None], own_sine[None])
            .astype(jnp.bfloat16)
            .reshape(heads * rows, head_size)
        )
        top_bit = stages[0]
        upper = ((context & top_bit) != 0).astype(jnp.int32)
        span = jnp.stack([start, first, upper]).astype(jnp.int32)
        for part in parts:
            part.tables = tables(start + places_of(part.top, part.rows), head_size)
        own_product, early.tables, late.tables, query_flat, span = lax.optimization_barrier(
            (own_product, early.tables, late.tables, query_flat, span)
        )

        def exchange(part, gate):
            arrived = []
            for number in range(part.first, part.end):
                chunk, gate = lax.optimization_barrier((flying[number], gate))
                gate = [project(columns) for columns in chunk]
                arrived.append(gate)
            products = [own_product[part.top : part.top + part.rows]] + [
                jnp.concatenate([chunk[step] for chunk in arrived], axis=0)
                for step in range(shards - 1)
            ]
            if shards == 2:
                sums = jnp.concatenate(
                    [
                        jnp.where(shard == 0, products[0], products[1]),
                        jnp.where(shard == 0, products[1], products[0]),
                    ],
                    axis=0,
                )
            else:
                sums = jnp.zeros((shards * part.rows, 2 * head_size), jnp.float32)
                for step in range(shards):
                    source = lax.rem(shard + shards - step, shards)
                    sums = lax.dynamic_update_slice_in_dim(
                        sums, products[step], source * part.rows, 0
                    )
            part.sums = after(sums)
            part.other = jnp.zeros_like(sums)
            reach = 1
            while reach < shards:
                if reach > 1:
                    part.sums = part.sums + part.other
                part.other = lax.ppermute(
                    part.sums, "fsdp", [(i, i ^ reach) for i in range(shards)]
                )
                reach *= 2

        def combine(part, *gate):
            own, other = lax.optimization_barrier((part.sums, part.other, *gate))[:2]
            sums = own + other
            keys_rot = rotate(sums[:, :head_size], *part.tables).astype(jnp.bfloat16)
            block = after(
                jnp.concatenate([keys_rot, sums[:, head_size:].astype(jnp.bfloat16)], axis=1)
            )
            part.cache = lax.dynamic_slice_in_dim(block, shard * part.rows, part.rows, 0)
            part.known, part.fresh = block, []

        def advance(part, *gate):
            fresh = lax.optimization_barrier((part.known, part.fresh, *gate))
            part.known = after(jnp.concatenate([fresh[0]] + list(fresh[1]), axis=0))
            part.fresh = []
            if part.stage < len(stages):
                pairs = [(i, i ^ paths[i & 1][part.stage]) for i in range(contexts)]
                part.fresh = [lax.ppermute(part.known, "ctx", pairs)]
            part.stage += 1

        slots = contexts // 4
        choices = []
        for masks in all_masks:
            order = []
            for index in range(2):
                held = range(index * 2 * slots, (index + 1) * 2 * slots)
                order.append(sorted(held, key=lambda slot: masks[slot] & top_bit))
            numbers = [slot - index * 2 * slots for index in range(2) for slot in order[index]]
            turns = [
                masks[slot]
                for half in range(2)
                for index in range(2)
                for slot in order[index][half * slots : (half + 1) * slots]
            ]
            choices.append((jnp.array(numbers, jnp.int32), jnp.array(turns, jnp.int32)))
        numbers = jnp.where(core == 0, choices[0][0], choices[1][0])
        sources = context ^ jnp.where(core == 0, choices[0][1], choices[1][1])
        span = jnp.concatenate([span, numbers])

        def absorb(part, pieces, own, state, last, *gate):
            local_pos = places_of(part.top, part.rows)
            place = sources[:, None] * group_rows + local_pos[None, :]
            query = after(query_flat, *gate)
            return attend(span, place.reshape(1, -1), query, pieces, slots, own, state, last, rows)

        exchange(early, own_product)
        for chunk in chunks[early.end + 1 :]:
            flying.append(send_rows(chunk, early.sums)[0])
        combine(early, *flying[early.end])
        advance(early)
        exchange(late, early.known)
        advance(early, late.sums)
        combine(late, early.known)
        advance(late)
        for stage in range(2, len(stages)):
            advance(early, late.known)
            advance(late, early.known)
        state = absorb(
            early,
            [early.known] + early.fresh,
            shards * early.rows,
            None,
            False,
            late.known,
        )
        advance(late, *state)
        attended = absorb(
            late, [late.known] + late.fresh, shards * late.rows, state, True
        )
        kv_cache = jnp.concatenate([part.cache for part in parts], axis=0)
        return (kv_cache, attended)

    return local


def solution(mesh):
    placed = (P(("ctx", "fsdp"), None), P(("ctx", "fsdp"), None), P("fsdp", None), P("fsdp", None))
    return jax.shard_map(
        make_local(mesh.shape["ctx"], mesh.shape["fsdp"], ((1, 4), (2, 1))),
        mesh=mesh,
        in_specs=placed,
        out_specs=(P(("ctx", "fsdp"), None), P(("ctx", "fsdp"), None)),
        check_vma=False,
    )
```

```python
from functools import partial
import math

import jax
import jax.numpy as jnp
from jax import lax
from jax.experimental import pallas as pl
from jax.experimental.pallas import tpu as pltpu
from jax.sharding import PartitionSpec as P

rope_base = 500000.0
floor_value = -1e30


def rotate(vectors, cosine, sine_table):
    middle = vectors.shape[-1] // 2
    leading = vectors[..., :middle]
    back_half = vectors[..., middle:]
    return jnp.concatenate(
        [leading * cosine - back_half * sine_table, back_half * cosine + leading * sine_table],
        axis=-1,
    )


def tables(positions, head_size):
    middle = head_size // 2
    frequency = rope_base ** (-jnp.arange(middle, dtype=jnp.float32) * 2.0 / head_size)
    angles = positions.astype(jnp.float32)[:, None] * frequency[None, :]
    return (jnp.cos(angles), jnp.sin(angles))


def attention_kernel(
    span_ref, place_ref, query_ref, *refs, count, order, carry, final, rows, own, head_size, stride
):
    pieces, refs = refs[:count], refs[count:]
    if carry:
        old_peak, old_total, old_sum = refs[:3]
        refs = refs[3:]
    start = span_ref[0]
    first = span_ref[1]
    factor = head_size ** (-0.5) * math.log2(math.e)
    flat = query_ref.shape[0]
    blocks = []
    size = sum(piece.shape[0] for piece in pieces) // len(order)
    for piece in pieces:
        blocks.extend(piece[top : top + size, :] for top in range(0, piece.shape[0], size))
    ordered = [blocks[index] for index in order]
    everything = jnp.concatenate(ordered, axis=0)

    def run(width):
        keys = everything[:width, :head_size]
        values = everything[:width, head_size:]
        edge = min(width, -(-own // 128) * 128)
        if edge:
            query_pos = first + lax.rem(
                lax.broadcasted_iota(jnp.int32, (stride, edge), 0), jnp.int32(rows)
            )
            diagonal = place_ref[:, :edge] <= query_pos
        bias = jnp.where(place_ref[:, :width] < start, 0.0, floor_value).astype(jnp.float32)

        def one(part):
            place = pl.ds(pl.multiple_of(part * stride, stride), stride)
            scores = (
                lax.dot_general(
                    query_ref[place, :],
                    keys,
                    (((1,), (1,)), ((), ())),
                    preferred_element_type=jnp.float32,
                )
                * factor
            )
            masked = []
            if edge:
                masked.append(jnp.where(diagonal, scores[:, :edge], floor_value))
            if edge < width:
                masked.append(scores[:, edge:] + bias[:, edge:])
            masked = jnp.concatenate(masked, axis=1) if len(masked) > 1 else masked[0]
            peak = jnp.max(masked, axis=1, keepdims=True)
            if carry:
                peak = jnp.maximum(peak, old_peak[place, :])
            weights = jnp.exp2(masked - peak)
            total = jnp.sum(weights, axis=1, keepdims=True)
            numerator = jnp.dot(
                weights.astype(jnp.bfloat16), values, preferred_element_type=jnp.float32
            )
            if carry:
                shrink = jnp.exp2(old_peak[place, :] - peak)
                total = total + shrink * old_total[place, :]
                numerator = numerator + shrink * old_sum[place, :]
            if final:
                out_ref, scratch = refs
                scratch[place, :] = (numerator / total).astype(jnp.bfloat16)
            else:
                peak_ref, total_ref, sum_ref = refs
                peak_ref[place, :] = peak
                total_ref[place, :] = total
                sum_ref[place, :] = numerator

        if flat // stride <= 8:
            for part in range(flat // stride):
                one(part)
        else:

            @pl.loop(0, flat // stride)
            def each(part):
                one(part)

    upper = span_ref[2]

    @pl.when(upper == 1)
    def all_keys():
        run(everything.shape[0])

    @pl.when(upper == 0)
    def lower_keys():
        run(everything.shape[0] // 2)

    if final:
        out_ref, scratch = refs
        for head in range(flat // rows):
            out_ref[:, head * head_size : (head + 1) * head_size] = scratch[
                head * rows : (head + 1) * rows, :
            ]


def attend(span, place, query_flat, pieces, order, own, state, final, rows):
    flat, head_size = query_flat.shape
    width = sum(piece.shape[0] for piece in pieces)
    stride = math.gcd(flat, 256 if width <= 2048 else rows)
    whole = pl.BlockSpec(memory_space=pltpu.VMEM)
    if final:
        shapes = jax.ShapeDtypeStruct((rows, flat // rows * head_size), jnp.bfloat16)
        out_specs, scratch = whole, [pltpu.VMEM((flat, head_size), jnp.bfloat16)]
    else:
        shapes = [
            jax.ShapeDtypeStruct((flat, 1), jnp.float32),
            jax.ShapeDtypeStruct((flat, 1), jnp.float32),
            jax.ShapeDtypeStruct((flat, head_size), jnp.float32),
        ]
        out_specs, scratch = [whole] * 3, []
    return pl.pallas_call(
        partial(
            attention_kernel,
            count=len(pieces),
            order=order,
            carry=state is not None,
            final=final,
            rows=rows,
            own=own,
            head_size=head_size,
            stride=stride,
        ),
        out_shape=shapes,
        in_specs=[pl.BlockSpec(memory_space=pltpu.SMEM)]
        + [whole] * (2 + len(pieces) + (0 if state is None else 3)),
        out_specs=out_specs,
        scratch_shapes=scratch,
        compiler_params=pltpu.CompilerParams(vmem_limit_bytes=32 * 1024 * 1024),
        cost_estimate=pl.CostEstimate(
            flops=4 * flat * width * head_size,
            bytes_accessed=4 * flat * head_size + 4 * width * head_size,
            transcendentals=flat * width,
        ),
        name="attend_last" if final else "attend_part",
    )(span, place, query_flat, *pieces, *(() if state is None else state))


def stages_of(contexts):
    bits = []
    bit = contexts // 2
    while bit >= 1:
        bits.append(bit)
        bit //= 2
    return bits


def after(value, *earlier):
    return lax.optimization_barrier((value, *earlier))[0]


def make_local(contexts, shards, plan):
    def local(tokens, queries, key_weight, value_weight):
        rows = tokens.shape[0]
        depth, head_size = key_weight.shape
        heads = queries.shape[1] // head_size
        group_rows = shards * rows
        context = lax.axis_index("ctx")
        shard = lax.axis_index("fsdp")
        unit = rows // sum(sum(part) for part in plan)
        stages = stages_of(contexts)

        def cut(chunk, *earlier):
            top, count = chunk
            source = after(tokens, *earlier) if earlier else tokens
            return [
                lax.dynamic_slice(
                    source,
                    (jnp.int32(top), lax.rem(shard + step, shards) * depth),
                    (count, depth),
                )
                for step in range(1, shards)
            ]

        def send(columns, *earlier):
            return [
                lax.ppermute(
                    after(columns[step - 1], *earlier) if earlier else columns[step - 1],
                    "fsdp",
                    [(i, (i + step) % shards) for i in range(shards)],
                )
                for step in range(1, shards)
            ]

        def places_of(top, count):
            turns = jnp.arange(shards, dtype=jnp.int32) * rows + top
            return (turns[:, None] + jnp.arange(count, dtype=jnp.int32)[None, :]).reshape(-1)

        class Part:
            pass

        parts = []
        chunks = []
        top = 0
        for sizes in plan:
            part = Part()
            part.top = top
            part.rows = sum(sizes) * unit
            part.first = len(chunks)
            for size in sizes:
                chunks.append((top, size * unit))
                top += size * unit
            part.end = len(chunks)
            part.stage = 0
            parts.append(part)
        early, late = parts

        flying = []
        sent = ()
        for chunk in chunks[: early.end + 1]:
            sent = cut(chunk, *sent)
            flying.append(send(sent))
        kept = []
        for chunk in chunks[early.end + 1 :]:
            sent = cut(chunk, *sent)
            kept.append(sent)

        def project(columns):
            return jnp.concatenate(
                [
                    jnp.dot(columns, weight, preferred_element_type=jnp.float32)
                    for weight in (key_weight, value_weight)
                ],
                axis=1,
            )

        own_columns = lax.dynamic_slice_in_dim(after(tokens, *sent), shard * depth, depth, 1)
        own_product = project(own_columns)

        start = context * group_rows
        first = start + shard * rows
        early.tables = tables(start + places_of(early.top, early.rows), head_size)
        own_product, early.tables, kept = lax.optimization_barrier(
            (own_product, early.tables, kept)
        )

        def exchange(part, gate):
            arrived = []
            for number in range(part.first, part.end):
                chunk, gate = lax.optimization_barrier((flying[number], gate))
                gate = [project(columns) for columns in chunk]
                arrived.append(gate)
            products = [own_product[part.top : part.top + part.rows]] + [
                jnp.concatenate([chunk[step] for chunk in arrived], axis=0)
                for step in range(shards - 1)
            ]
            if shards == 2:
                sums = jnp.concatenate(
                    [
                        jnp.where(shard == 0, products[0], products[1]),
                        jnp.where(shard == 0, products[1], products[0]),
                    ],
                    axis=0,
                )
            else:
                sums = jnp.zeros((shards * part.rows, 2 * head_size), jnp.float32)
                for step in range(shards):
                    source = lax.rem(shard + shards - step, shards)
                    sums = lax.dynamic_update_slice_in_dim(
                        sums, products[step], source * part.rows, 0
                    )
            part.sums = after(sums)
            part.other = jnp.zeros_like(sums)
            reach = 1
            while reach < shards:
                if reach > 1:
                    part.sums = part.sums + part.other
                part.other = lax.ppermute(
                    part.sums, "fsdp", [(i, i ^ reach) for i in range(shards)]
                )
                reach *= 2

        def combine(part, *gate):
            own, other = lax.optimization_barrier((part.sums, part.other, *gate))[:2]
            sums = own + other
            keys_rot = rotate(sums[:, :head_size], *part.tables).astype(jnp.bfloat16)
            block = after(
                jnp.concatenate([keys_rot, sums[:, head_size:].astype(jnp.bfloat16)], axis=1)
            )
            part.cache = lax.dynamic_slice_in_dim(block, shard * part.rows, part.rows, 0)
            part.known, part.fresh, part.masks = block, [], [0]

        def advance(part, *gate):
            fresh = lax.optimization_barrier((part.known, part.fresh, *gate))
            part.known = after(jnp.concatenate([fresh[0]] + list(fresh[1]), axis=0))
            part.fresh = []
            if part.stage < len(stages):
                bit = stages[part.stage]
                pairs = [(i, i ^ bit) for i in range(contexts)]
                part.fresh = [lax.ppermute(part.known, "ctx", pairs)]
                part.masks = part.masks + [mask ^ bit for mask in part.masks]
            part.stage += 1

        def absorb(part, pieces, masks, own, state, last, *gate):
            local_pos = places_of(part.top, part.rows)
            order = sorted(range(len(masks)), key=lambda index: masks[index] & top_bit)
            turns = jnp.array([masks[index] for index in order], jnp.int32)
            place = (context ^ turns)[:, None] * group_rows + local_pos[None, :]
            query = after(query_flat, *gate)
            return attend(
                span, place.reshape(1, -1), query, pieces, tuple(order), own, state, last, rows
            )

        exchange(early, own_product)
        for columns in kept:
            flying.append(send(columns, early.sums))
        raw_queries, first = lax.optimization_barrier((queries, first, early.sums))[:2]
        own_cosine, own_sine = tables(first + jnp.arange(rows, dtype=jnp.int32), head_size)
        by_head = raw_queries.astype(jnp.float32).reshape(rows, heads, head_size)
        query_flat = (
            rotate(by_head.transpose(1, 0, 2), own_cosine[None], own_sine[None])
            .astype(jnp.bfloat16)
            .reshape(heads * rows, head_size)
        )
        base = first - shard * rows
        late.tables = tables(base + places_of(late.top, late.rows), head_size)
        top_bit = stages[0]
        upper = ((context & top_bit) != 0).astype(jnp.int32)
        span = jnp.stack([base, first, upper]).astype(jnp.int32)
        query_flat, late.tables, span = lax.optimization_barrier((query_flat, late.tables, span))
        combine(early, query_flat, *late.tables, *flying[early.end])
        advance(early)
        exchange(late, early.known)
        advance(early, late.sums)
        combine(late, early.known)
        advance(late)
        for stage in range(2, len(stages)):
            advance(early, late.known)
            advance(late, early.known)
        state = absorb(
            early,
            [early.known] + early.fresh,
            early.masks,
            shards * early.rows,
            None,
            False,
            late.known,
        )
        advance(late, *state)
        attended = absorb(
            late, [late.known] + late.fresh, late.masks, shards * late.rows, state, True
        )
        kv_cache = jnp.concatenate([part.cache for part in parts], axis=0)
        return (kv_cache, attended)

    return local


def solution(mesh):
    placed = (P(("ctx", "fsdp"), None), P(("ctx", "fsdp"), None), P("fsdp", None), P("fsdp", None))
    return jax.shard_map(
        make_local(mesh.shape["ctx"], mesh.shape["fsdp"], ((1, 4), (2, 1))),
        mesh=mesh,
        in_specs=placed,
        out_specs=(P(("ctx", "fsdp"), None), P(("ctx", "fsdp"), None)),
        check_vma=False,
    )
```

```python
from functools import partial
import math

import jax
import jax.numpy as jnp
from jax import lax
from jax.experimental import pallas as pl
from jax.experimental.pallas import tpu as pltpu
from jax.sharding import PartitionSpec as P

rope_base = 500000.0
floor_value = -1e30


def rotate(vectors, cosine, sine_table):
    middle = vectors.shape[-1] // 2
    leading = vectors[..., :middle]
    back_half = vectors[..., middle:]
    return jnp.concatenate(
        [leading * cosine - back_half * sine_table, back_half * cosine + leading * sine_table],
        axis=-1,
    )


def tables(positions, head_size):
    middle = head_size // 2
    frequency = rope_base ** (-jnp.arange(middle, dtype=jnp.float32) * 2.0 / head_size)
    angles = positions.astype(jnp.float32)[:, None] * frequency[None, :]
    return (jnp.cos(angles), jnp.sin(angles))


def attention_kernel(
    span_ref, place_ref, query_ref, *refs, count, order, carry, final, rows, own, head_size, stride
):
    pieces, refs = refs[:count], refs[count:]
    if carry:
        old_peak, old_total, old_sum = refs[:3]
        refs = refs[3:]
    start = span_ref[0]
    first = span_ref[1]
    factor = head_size ** (-0.5) * math.log2(math.e)
    flat = query_ref.shape[0]
    blocks = []
    size = sum(piece.shape[0] for piece in pieces) // len(order)
    for piece in pieces:
        blocks.extend(piece[top : top + size, :] for top in range(0, piece.shape[0], size))
    ordered = [blocks[index] for index in order]
    everything = jnp.concatenate(ordered, axis=0)

    def run(width):
        keys = everything[:width, :head_size]
        values = everything[:width, head_size:]
        edge = min(width, -(-own // 128) * 128)
        if edge:
            query_pos = first + lax.rem(
                lax.broadcasted_iota(jnp.int32, (stride, edge), 0), jnp.int32(rows)
            )
            diagonal = place_ref[:, :edge] <= query_pos
        bias = jnp.where(place_ref[:, :width] < start, 0.0, floor_value).astype(jnp.float32)

        def one(part):
            place = pl.ds(pl.multiple_of(part * stride, stride), stride)
            scores = (
                lax.dot_general(
                    query_ref[place, :],
                    keys,
                    (((1,), (1,)), ((), ())),
                    preferred_element_type=jnp.float32,
                )
                * factor
            )
            masked = []
            if edge:
                masked.append(jnp.where(diagonal, scores[:, :edge], floor_value))
            if edge < width:
                masked.append(scores[:, edge:] + bias[:, edge:])
            masked = jnp.concatenate(masked, axis=1) if len(masked) > 1 else masked[0]
            peak = jnp.max(masked, axis=1, keepdims=True)
            if carry:
                peak = jnp.maximum(peak, old_peak[place, :])
            weights = jnp.exp2(masked - peak)
            total = jnp.sum(weights, axis=1, keepdims=True)
            numerator = jnp.dot(
                weights.astype(jnp.bfloat16), values, preferred_element_type=jnp.float32
            )
            if carry:
                shrink = jnp.exp2(old_peak[place, :] - peak)
                total = total + shrink * old_total[place, :]
                numerator = numerator + shrink * old_sum[place, :]
            if final:
                out_ref, scratch = refs
                scratch[place, :] = (numerator / total).astype(jnp.bfloat16)
            else:
                peak_ref, total_ref, sum_ref = refs
                peak_ref[place, :] = peak
                total_ref[place, :] = total
                sum_ref[place, :] = numerator

        if flat // stride <= 8:
            for part in range(flat // stride):
                one(part)
        else:

            @pl.loop(0, flat // stride)
            def each(part):
                one(part)

    upper = span_ref[2]

    @pl.when(upper == 1)
    def all_keys():
        run(everything.shape[0])

    @pl.when(upper == 0)
    def lower_keys():
        run(everything.shape[0] // 2)

    if final:
        out_ref, scratch = refs
        for head in range(flat // rows):
            out_ref[:, head * head_size : (head + 1) * head_size] = scratch[
                head * rows : (head + 1) * rows, :
            ]


def attend(span, place, query_flat, pieces, order, own, state, final, rows):
    flat, head_size = query_flat.shape
    width = sum(piece.shape[0] for piece in pieces)
    stride = math.gcd(flat, 256 if width <= 2048 else rows)
    whole = pl.BlockSpec(memory_space=pltpu.VMEM)
    if final:
        shapes = jax.ShapeDtypeStruct((rows, flat // rows * head_size), jnp.bfloat16)
        out_specs, scratch = whole, [pltpu.VMEM((flat, head_size), jnp.bfloat16)]
    else:
        shapes = [
            jax.ShapeDtypeStruct((flat, 1), jnp.float32),
            jax.ShapeDtypeStruct((flat, 1), jnp.float32),
            jax.ShapeDtypeStruct((flat, head_size), jnp.float32),
        ]
        out_specs, scratch = [whole] * 3, []
    return pl.pallas_call(
        partial(
            attention_kernel,
            count=len(pieces),
            order=order,
            carry=state is not None,
            final=final,
            rows=rows,
            own=own,
            head_size=head_size,
            stride=stride,
        ),
        out_shape=shapes,
        in_specs=[pl.BlockSpec(memory_space=pltpu.SMEM)]
        + [whole] * (2 + len(pieces) + (0 if state is None else 3)),
        out_specs=out_specs,
        scratch_shapes=scratch,
        compiler_params=pltpu.CompilerParams(vmem_limit_bytes=32 * 1024 * 1024),
        cost_estimate=pl.CostEstimate(
            flops=4 * flat * width * head_size,
            bytes_accessed=4 * flat * head_size + 4 * width * head_size,
            transcendentals=flat * width,
        ),
        name="attend_last" if final else "attend_part",
    )(span, place, query_flat, *pieces, *(() if state is None else state))


def stages_of(contexts):
    bits = []
    bit = contexts // 2
    while bit >= 1:
        bits.append(bit)
        bit //= 2
    return bits


def after(value, *earlier):
    return lax.optimization_barrier((value, *earlier))[0]


def make_local(contexts, shards, plan):
    def local(tokens, queries, key_weight, value_weight):
        rows = tokens.shape[0]
        depth, head_size = key_weight.shape
        heads = queries.shape[1] // head_size
        group_rows = shards * rows
        context = lax.axis_index("ctx")
        shard = lax.axis_index("fsdp")
        unit = rows // sum(sum(part) for part in plan)
        stages = stages_of(contexts)

        def cut(chunk, *earlier):
            top, count = chunk
            source = after(tokens, *earlier) if earlier else tokens
            return [
                lax.dynamic_slice(
                    source,
                    (jnp.int32(top), lax.rem(shard + step, shards) * depth),
                    (count, depth),
                )
                for step in range(1, shards)
            ]

        def send(columns, *earlier):
            return [
                lax.ppermute(
                    after(columns[step - 1], *earlier) if earlier else columns[step - 1],
                    "fsdp",
                    [(i, (i + step) % shards) for i in range(shards)],
                )
                for step in range(1, shards)
            ]

        def places_of(top, count):
            turns = jnp.arange(shards, dtype=jnp.int32) * rows + top
            return (turns[:, None] + jnp.arange(count, dtype=jnp.int32)[None, :]).reshape(-1)

        class Part:
            pass

        parts = []
        chunks = []
        top = 0
        for sizes in plan:
            part = Part()
            part.top = top
            part.rows = sum(sizes) * unit
            part.first = len(chunks)
            for size in sizes:
                chunks.append((top, size * unit))
                top += size * unit
            part.end = len(chunks)
            part.stage = 0
            parts.append(part)
        early, late = parts

        flying = []
        sent = ()
        for chunk in chunks[: early.end + 1]:
            sent = cut(chunk, *sent)
            flying.append(send(sent))
        kept = []
        for chunk in chunks[early.end + 1 :]:
            sent = cut(chunk, *sent)
            kept.append(sent)

        def project(columns):
            return jnp.concatenate(
                [
                    jnp.dot(columns, weight, preferred_element_type=jnp.float32)
                    for weight in (key_weight, value_weight)
                ],
                axis=1,
            )

        own_columns = lax.dynamic_slice_in_dim(after(tokens, *sent), shard * depth, depth, 1)
        own_product = project(own_columns)

        start = context * group_rows
        first = start + shard * rows
        early.tables = tables(start + places_of(early.top, early.rows), head_size)
        own_product, early.tables, kept = lax.optimization_barrier(
            (own_product, early.tables, kept)
        )

        def exchange(part, gate):
            arrived = []
            for number in range(part.first, part.end):
                chunk, gate = lax.optimization_barrier((flying[number], gate))
                gate = [project(columns) for columns in chunk]
                arrived.append(gate)
            products = [own_product[part.top : part.top + part.rows]] + [
                jnp.concatenate([chunk[step] for chunk in arrived], axis=0)
                for step in range(shards - 1)
            ]
            if shards == 2:
                sums = jnp.concatenate(
                    [
                        jnp.where(shard == 0, products[0], products[1]),
                        jnp.where(shard == 0, products[1], products[0]),
                    ],
                    axis=0,
                )
            else:
                sums = jnp.zeros((shards * part.rows, 2 * head_size), jnp.float32)
                for step in range(shards):
                    source = lax.rem(shard + shards - step, shards)
                    sums = lax.dynamic_update_slice_in_dim(
                        sums, products[step], source * part.rows, 0
                    )
            part.sums = after(sums)
            part.other = jnp.zeros_like(sums)
            reach = 1
            while reach < shards:
                if reach > 1:
                    part.sums = part.sums + part.other
                part.other = lax.ppermute(
                    part.sums, "fsdp", [(i, i ^ reach) for i in range(shards)]
                )
                reach *= 2

        def combine(part, *gate):
            own, other = lax.optimization_barrier((part.sums, part.other, *gate))[:2]
            sums = own + other
            keys_rot = rotate(sums[:, :head_size], *part.tables).astype(jnp.bfloat16)
            block = after(
                jnp.concatenate([keys_rot, sums[:, head_size:].astype(jnp.bfloat16)], axis=1)
            )
            part.cache = lax.dynamic_slice_in_dim(block, shard * part.rows, part.rows, 0)
            part.known, part.fresh, part.masks = block, [], [0]

        def advance(part, *gate):
            fresh = lax.optimization_barrier((part.known, part.fresh, *gate))
            part.known = after(jnp.concatenate([fresh[0]] + list(fresh[1]), axis=0))
            part.fresh = []
            if part.stage < len(stages):
                bit = stages[part.stage]
                pairs = [(i, i ^ bit) for i in range(contexts)]
                part.fresh = [lax.ppermute(part.known, "ctx", pairs)]
                part.masks = part.masks + [mask ^ bit for mask in part.masks]
            part.stage += 1

        def absorb(part, pieces, masks, own, state, last, *gate):
            local_pos = places_of(part.top, part.rows)
            order = sorted(range(len(masks)), key=lambda index: masks[index] & top_bit)
            turns = jnp.array([masks[index] for index in order], jnp.int32)
            place = (context ^ turns)[:, None] * group_rows + local_pos[None, :]
            query = after(query_flat, *gate)
            return attend(
                span, place.reshape(1, -1), query, pieces, tuple(order), own, state, last, rows
            )

        exchange(early, own_product)
        for columns in kept:
            flying.append(send(columns, early.sums))
        raw_queries, first = lax.optimization_barrier((queries, first, early.sums))[:2]
        own_cosine, own_sine = tables(first + jnp.arange(rows, dtype=jnp.int32), head_size)
        by_head = raw_queries.astype(jnp.float32).reshape(rows, heads, head_size)
        query_flat = (
            rotate(by_head.transpose(1, 0, 2), own_cosine[None], own_sine[None])
            .astype(jnp.bfloat16)
            .reshape(heads * rows, head_size)
        )
        base = first - shard * rows
        late.tables = tables(base + places_of(late.top, late.rows), head_size)
        top_bit = stages[0]
        upper = ((context & top_bit) != 0).astype(jnp.int32)
        span = jnp.stack([base, first, upper]).astype(jnp.int32)
        query_flat, late.tables, span = lax.optimization_barrier((query_flat, late.tables, span))
        combine(early, query_flat, *late.tables, *flying[early.end])
        advance(early)
        advance(early, *[piece for chunk in flying[early.end + 1 : -1] for piece in chunk])
        exchange(late, early.known)
        advance(early, late.sums)
        combine(late, early.known)
        advance(late)
        for stage in range(3, len(stages)):
            advance(early, late.known)
            advance(late, early.known)
        state = absorb(
            early,
            [early.known] + early.fresh,
            early.masks,
            shards * early.rows,
            None,
            False,
            late.known,
        )
        advance(late, *state)
        while late.stage < len(stages):
            advance(late)
        attended = absorb(
            late, [late.known] + late.fresh, late.masks, shards * late.rows, state, True
        )
        kv_cache = jnp.concatenate([part.cache for part in parts], axis=0)
        return (kv_cache, attended)

    return local


def solution(mesh):
    placed = (P(("ctx", "fsdp"), None), P(("ctx", "fsdp"), None), P("fsdp", None), P("fsdp", None))
    return jax.shard_map(
        make_local(mesh.shape["ctx"], mesh.shape["fsdp"], ((1, 2), (2, 1, 2))),
        mesh=mesh,
        in_specs=placed,
        out_specs=(P(("ctx", "fsdp"), None), P(("ctx", "fsdp"), None)),
        check_vma=False,
    )
```

```python
from functools import partial
import math

import jax
import jax.numpy as jnp
from jax import lax
from jax.experimental import pallas as pl
from jax.experimental.pallas import tpu as pltpu
from jax.sharding import PartitionSpec as P

rope_base = 500000.0
floor_value = -1e30


def rotate(vectors, cosine, sine_table):
    middle = vectors.shape[-1] // 2
    leading = vectors[..., :middle]
    back_half = vectors[..., middle:]
    return jnp.concatenate(
        [leading * cosine - back_half * sine_table, back_half * cosine + leading * sine_table],
        axis=-1,
    )


def tables(positions, head_size):
    middle = head_size // 2
    frequency = rope_base ** (-jnp.arange(middle, dtype=jnp.float32) * 2.0 / head_size)
    angles = positions.astype(jnp.float32)[:, None] * frequency[None, :]
    return (jnp.cos(angles), jnp.sin(angles))


def attention_kernel(
    span_ref, place_ref, query_ref, *refs, count, order, carry, final, rows, own, head_size, stride
):
    pieces, refs = refs[:count], refs[count:]
    if carry:
        old_peak, old_total, old_sum = refs[:3]
        refs = refs[3:]
    start = span_ref[0]
    first = span_ref[1]
    factor = head_size ** (-0.5) * math.log2(math.e)
    flat = query_ref.shape[0]
    ordered = []
    for index, slot in order:
        size = pieces[index].shape[0] * len(pieces) // len(order)
        ordered.append(pieces[index][slot * size : (slot + 1) * size, :])
    everything = jnp.concatenate(ordered, axis=0)

    def run(width):
        keys = everything[:width, :head_size]
        values = everything[:width, head_size:]
        edge = min(width, -(-own // 128) * 128)
        if edge:
            query_pos = first + lax.rem(
                lax.broadcasted_iota(jnp.int32, (stride, edge), 0), jnp.int32(rows)
            )
            diagonal = place_ref[:, :edge] <= query_pos
        bias = jnp.where(place_ref[:, :width] < start, 0.0, floor_value).astype(jnp.float32)

        def one(part):
            place = pl.ds(pl.multiple_of(part * stride, stride), stride)
            scores = (
                lax.dot_general(
                    query_ref[place, :],
                    keys,
                    (((1,), (1,)), ((), ())),
                    preferred_element_type=jnp.float32,
                )
                * factor
            )
            masked = []
            if edge:
                masked.append(jnp.where(diagonal, scores[:, :edge], floor_value))
            if edge < width:
                masked.append(scores[:, edge:] + bias[:, edge:])
            masked = jnp.concatenate(masked, axis=1) if len(masked) > 1 else masked[0]
            peak = jnp.max(masked, axis=1, keepdims=True)
            if carry:
                peak = jnp.maximum(peak, old_peak[place, :])
            weights = jnp.exp2(masked - peak)
            total = jnp.sum(weights, axis=1, keepdims=True)
            numerator = jnp.dot(
                weights.astype(jnp.bfloat16), values, preferred_element_type=jnp.float32
            )
            if carry:
                shrink = jnp.exp2(old_peak[place, :] - peak)
                total = total + shrink * old_total[place, :]
                numerator = numerator + shrink * old_sum[place, :]
            if final:
                out_ref, scratch = refs
                scratch[place, :] = (numerator / total).astype(jnp.bfloat16)
            else:
                peak_ref, total_ref, sum_ref = refs
                peak_ref[place, :] = peak
                total_ref[place, :] = total
                sum_ref[place, :] = numerator

        if flat // stride <= 8:
            for part in range(flat // stride):
                one(part)
        else:

            @pl.loop(0, flat // stride)
            def each(part):
                one(part)

    upper = span_ref[2]

    @pl.when(upper == 1)
    def all_keys():
        run(everything.shape[0])

    @pl.when(upper == 0)
    def lower_keys():
        run(everything.shape[0] // 2)

    if final:
        out_ref, scratch = refs
        for head in range(flat // rows):
            out_ref[:, head * head_size : (head + 1) * head_size] = scratch[
                head * rows : (head + 1) * rows, :
            ]


def attend(span, place, query_flat, pieces, order, own, state, final, rows):
    flat, head_size = query_flat.shape
    width = sum(piece.shape[0] for piece in pieces)
    stride = math.gcd(flat, 256 if width <= 2048 else rows)
    whole = pl.BlockSpec(memory_space=pltpu.VMEM)
    if final:
        shapes = jax.ShapeDtypeStruct((rows, flat // rows * head_size), jnp.bfloat16)
        out_specs, scratch = whole, [pltpu.VMEM((flat, head_size), jnp.bfloat16)]
    else:
        shapes = [
            jax.ShapeDtypeStruct((flat, 1), jnp.float32),
            jax.ShapeDtypeStruct((flat, 1), jnp.float32),
            jax.ShapeDtypeStruct((flat, head_size), jnp.float32),
        ]
        out_specs, scratch = [whole] * 3, []
    return pl.pallas_call(
        partial(
            attention_kernel,
            count=len(pieces),
            order=order,
            carry=state is not None,
            final=final,
            rows=rows,
            own=own,
            head_size=head_size,
            stride=stride,
        ),
        out_shape=shapes,
        in_specs=[pl.BlockSpec(memory_space=pltpu.SMEM)]
        + [whole] * (2 + len(pieces) + (0 if state is None else 3)),
        out_specs=out_specs,
        scratch_shapes=scratch,
        compiler_params=pltpu.CompilerParams(vmem_limit_bytes=24 * 1024 * 1024),
        cost_estimate=pl.CostEstimate(
            flops=4 * flat * width * head_size,
            bytes_accessed=4 * flat * head_size + 4 * width * head_size,
            transcendentals=flat * width,
        ),
        name="attend_last" if final else "attend_part",
    )(span, place, query_flat, *pieces, *(() if state is None else state))


def stages_of(contexts):
    bits = []
    bit = contexts // 2
    while bit >= 1:
        bits.append(bit)
        bit //= 2
    return bits


def after(value, *earlier):
    return lax.optimization_barrier((value, *earlier))[0]


def make_local(contexts, shards, plan):
    def local(tokens, queries, key_weight, value_weight):
        rows = tokens.shape[0]
        depth, head_size = key_weight.shape
        heads = queries.shape[1] // head_size
        group_rows = shards * rows
        context = lax.axis_index("ctx")
        shard = lax.axis_index("fsdp")
        unit = rows // sum(sum(part) for part in plan)
        stages = stages_of(contexts)

        def cut(chunk, *earlier):
            top, count = chunk
            source = after(tokens, *earlier) if earlier else tokens
            return [
                lax.dynamic_slice(
                    source,
                    (jnp.int32(top), lax.rem(shard + step, shards) * depth),
                    (count, depth),
                )
                for step in range(1, shards)
            ]

        def send(columns, *earlier):
            return [
                lax.ppermute(
                    after(columns[step - 1], *earlier) if earlier else columns[step - 1],
                    "fsdp",
                    [(i, (i + step) % shards) for i in range(shards)],
                )
                for step in range(1, shards)
            ]

        def places_of(top, count):
            turns = jnp.arange(shards, dtype=jnp.int32) * rows + top
            return (turns[:, None] + jnp.arange(count, dtype=jnp.int32)[None, :]).reshape(-1)

        class Part:
            pass

        parts = []
        chunks = []
        top = 0
        for sizes in plan:
            part = Part()
            part.top = top
            part.rows = sum(sizes) * unit
            part.first = len(chunks)
            for size in sizes:
                chunks.append((top, size * unit))
                top += size * unit
            part.end = len(chunks)
            part.stage = 0
            parts.append(part)
        early, late = parts

        flying = []
        sent = ()
        for chunk in chunks[: early.end + 1]:
            sent = cut(chunk, *sent)
            flying.append(send(sent))
        kept = []
        for chunk in chunks[early.end + 1 :]:
            sent = cut(chunk, *sent)
            kept.append(sent)

        def project(columns):
            return jnp.concatenate(
                [
                    jnp.dot(columns, weight, preferred_element_type=jnp.float32)
                    for weight in (key_weight, value_weight)
                ],
                axis=1,
            )

        own_columns = lax.dynamic_slice_in_dim(after(tokens, *sent), shard * depth, depth, 1)
        own_product = project(own_columns)

        start = context * group_rows
        first = start + shard * rows
        early.tables = tables(start + places_of(early.top, early.rows), head_size)
        own_product, early.tables, kept = lax.optimization_barrier(
            (own_product, early.tables, kept)
        )

        def exchange(part, gate):
            arrived = []
            for number in range(part.first, part.end):
                chunk, gate = lax.optimization_barrier((flying[number], gate))
                gate = [project(columns) for columns in chunk]
                arrived.append(gate)
            products = [own_product[part.top : part.top + part.rows]] + [
                jnp.concatenate([chunk[step] for chunk in arrived], axis=0)
                for step in range(shards - 1)
            ]
            if shards == 2:
                sums = jnp.concatenate(
                    [
                        jnp.where(shard == 0, products[0], products[1]),
                        jnp.where(shard == 0, products[1], products[0]),
                    ],
                    axis=0,
                )
            else:
                sums = jnp.zeros((shards * part.rows, 2 * head_size), jnp.float32)
                for step in range(shards):
                    source = lax.rem(shard + shards - step, shards)
                    sums = lax.dynamic_update_slice_in_dim(
                        sums, products[step], source * part.rows, 0
                    )
            part.sums = after(sums)
            part.other = jnp.zeros_like(sums)
            reach = 1
            while reach < shards:
                if reach > 1:
                    part.sums = part.sums + part.other
                part.other = lax.ppermute(
                    part.sums, "fsdp", [(i, i ^ reach) for i in range(shards)]
                )
                reach *= 2

        def combine(part, *gate):
            own, other = lax.optimization_barrier((part.sums, part.other, *gate))[:2]
            sums = own + other
            keys_rot = rotate(sums[:, :head_size], *part.tables).astype(jnp.bfloat16)
            block = after(
                jnp.concatenate([keys_rot, sums[:, head_size:].astype(jnp.bfloat16)], axis=1)
            )
            part.cache = lax.dynamic_slice_in_dim(block, shard * part.rows, part.rows, 0)
            part.known, part.fresh, part.masks = block, [], [0]

        def advance(part, *gate):
            fresh = lax.optimization_barrier((part.known, part.fresh, *gate))
            part.known = after(jnp.concatenate([fresh[0]] + list(fresh[1]), axis=0))
            part.fresh = []
            if part.stage < len(stages):
                bit = stages[part.stage]
                pairs = [(i, i ^ bit) for i in range(contexts)]
                part.fresh = [lax.ppermute(part.known, "ctx", pairs)]
                part.masks = part.masks + [mask ^ bit for mask in part.masks]
            part.stage += 1

        exchange(early, own_product)
        for columns in kept:
            flying.append(send(columns, early.sums))
        raw_queries, first = lax.optimization_barrier((queries, first, early.sums))[:2]
        own_cosine, own_sine = tables(first + jnp.arange(rows, dtype=jnp.int32), head_size)
        by_head = raw_queries.astype(jnp.float32).reshape(rows, heads, head_size)
        query_flat = (
            rotate(by_head.transpose(1, 0, 2), own_cosine[None], own_sine[None])
            .astype(jnp.bfloat16)
            .reshape(heads * rows, head_size)
        )
        base = first - shard * rows
        late.tables = tables(base + places_of(late.top, late.rows), head_size)
        top_bit = stages[0]
        upper = ((context & top_bit) != 0).astype(jnp.int32)
        span = jnp.stack([base, first, upper]).astype(jnp.int32)
        def halves(masks):
            return sorted(range(len(masks)), key=lambda slot: masks[slot] & top_bit)

        all_masks = [0]
        for bit in stages:
            all_masks = all_masks + [mask ^ bit for mask in all_masks]
        sorted_slots = halves(all_masks)
        middle = len(all_masks) // 2
        turns = jnp.array([all_masks[slot] for slot in sorted_slots], jnp.int32)
        sources = (context ^ turns)[:, None] * group_rows
        spots = [
            (sources + places_of(part.top, part.rows)[None, :]).reshape(-1) for part in parts
        ]
        cuts = [(0, 1), (1, middle), (middle, 2 * middle)]
        place = jnp.concatenate(
            [
                spot[low * shards * part.rows : high * shards * part.rows]
                for low, high in cuts
                for spot, part in zip(spots, parts)
            ]
        ).reshape(1, -1)
        order = tuple(
            (2 * number + slot // middle, slot % middle)
            for low, high in cuts
            for number in range(len(parts))
            for slot in sorted_slots[low:high]
        )
        query_flat, late.tables, span, place = lax.optimization_barrier(
            (query_flat, late.tables, span, place)
        )
        exchange(late, query_flat)
        combine(early, late.sums)
        advance(early)
        combine(late, early.known)
        advance(late)
        for stage in range(1, len(stages)):
            advance(early, late.known)
            advance(late, early.known)
        pieces = [early.known] + early.fresh + [late.known] + late.fresh
        attended = attend(
            span, place, query_flat, pieces, order, shards * rows, None, True, rows
        )
        kv_cache = jnp.concatenate([part.cache for part in parts], axis=0)
        return (kv_cache, attended)

    return local


def solution(mesh):
    placed = (P(("ctx", "fsdp"), None), P(("ctx", "fsdp"), None), P("fsdp", None), P("fsdp", None))
    return jax.shard_map(
        make_local(mesh.shape["ctx"], mesh.shape["fsdp"], ((1, 4), (3,))),
        mesh=mesh,
        in_specs=placed,
        out_specs=(P(("ctx", "fsdp"), None), P(("ctx", "fsdp"), None)),
        check_vma=False,
    )
```

```python
from functools import partial
import math

import jax
import jax.numpy as jnp
from jax import lax
from jax.experimental import pallas as pl
from jax.experimental.pallas import tpu as pltpu
from jax.sharding import PartitionSpec as P

rope_base = 500000.0
floor_value = -1e30


def rotate(vectors, cosine, sine_table):
    middle = vectors.shape[-1] // 2
    leading = vectors[..., :middle]
    back_half = vectors[..., middle:]
    return jnp.concatenate(
        [leading * cosine - back_half * sine_table, back_half * cosine + leading * sine_table],
        axis=-1,
    )


def tables(positions, head_size):
    middle = head_size // 2
    frequency = rope_base ** (-jnp.arange(middle, dtype=jnp.float32) * 2.0 / head_size)
    angles = positions.astype(jnp.float32)[:, None] * frequency[None, :]
    return (jnp.cos(angles), jnp.sin(angles))


def attention_kernel(
    span_ref, query_ref, *refs, count, slots, owns, rows, head_size, stride
):
    places, refs = refs[:count], refs[count:]
    pieces, (out_ref, scratch) = refs[: 2 * count], refs[2 * count :]
    start = span_ref[0]
    first = span_ref[1]
    factor = head_size ** (-0.5) * math.log2(math.e)
    flat = query_ref.shape[0]
    middle = len(slots) // 2
    sorted_parts = []
    for number in range(count):
        size = pieces[2 * number].shape[0] // middle
        blocks = []
        for slot in slots:
            top = (slot % middle) * size
            blocks.append(pieces[2 * number + slot // middle][top : top + size, :])
        sorted_parts.append(jnp.concatenate(blocks, axis=0))

    def run(share):
        chosen = [part[: part.shape[0] // share, :] for part in sorted_parts]
        everything = jnp.concatenate(chosen, axis=0)
        keys = everything[:, :head_size]
        values = everything[:, head_size:]
        segments = []
        top = 0
        for part, place_ref, own in zip(chosen, places, owns):
            width = part.shape[0]
            edge = min(width, -(-own // 128) * 128)
            query_pos = first + lax.rem(
                lax.broadcasted_iota(jnp.int32, (stride, edge), 0), jnp.int32(rows)
            )
            diagonal = place_ref[:, :edge] <= query_pos
            bias = jnp.where(place_ref[:, edge:width] < start, 0.0, floor_value)
            segments.append((top, edge, width, diagonal, bias.astype(jnp.float32)))
            top += width

        def one(turn):
            place = pl.ds(pl.multiple_of(turn * stride, stride), stride)
            scores = (
                lax.dot_general(
                    query_ref[place, :],
                    keys,
                    (((1,), (1,)), ((), ())),
                    preferred_element_type=jnp.float32,
                )
                * factor
            )
            masked = []
            for top, edge, width, diagonal, bias in segments:
                masked.append(jnp.where(diagonal, scores[:, top : top + edge], floor_value))
                if edge < width:
                    masked.append(scores[:, top + edge : top + width] + bias)
            masked = jnp.concatenate(masked, axis=1)
            peak = jnp.max(masked, axis=1, keepdims=True)
            weights = jnp.exp2(masked - peak)
            total = jnp.sum(weights, axis=1, keepdims=True)
            numerator = jnp.dot(
                weights.astype(jnp.bfloat16), values, preferred_element_type=jnp.float32
            )
            scratch[place, :] = (numerator / total).astype(jnp.bfloat16)

        if flat // stride <= 8:
            for turn in range(flat // stride):
                one(turn)
        else:

            @pl.loop(0, flat // stride)
            def each(turn):
                one(turn)

    upper = span_ref[2]

    @pl.when(upper == 1)
    def all_keys():
        run(1)

    @pl.when(upper == 0)
    def lower_keys():
        run(2)

    for head in range(flat // rows):
        out_ref[:, head * head_size : (head + 1) * head_size] = scratch[
            head * rows : (head + 1) * rows, :
        ]


def attend(span, places, query_flat, pieces, slots, owns, rows):
    flat, head_size = query_flat.shape
    width = sum(piece.shape[0] for piece in pieces)
    stride = math.gcd(flat, 256 if width <= 2048 else rows)
    whole = pl.BlockSpec(memory_space=pltpu.VMEM)
    return pl.pallas_call(
        partial(
            attention_kernel,
            count=len(places),
            slots=slots,
            owns=owns,
            rows=rows,
            head_size=head_size,
            stride=stride,
        ),
        out_shape=jax.ShapeDtypeStruct((rows, flat // rows * head_size), jnp.bfloat16),
        in_specs=[pl.BlockSpec(memory_space=pltpu.SMEM)]
        + [whole] * (1 + len(places) + len(pieces)),
        out_specs=whole,
        scratch_shapes=[pltpu.VMEM((flat, head_size), jnp.bfloat16)],
        compiler_params=pltpu.CompilerParams(vmem_limit_bytes=24 * 1024 * 1024),
        cost_estimate=pl.CostEstimate(
            flops=4 * flat * width * head_size,
            bytes_accessed=4 * flat * head_size + 4 * width * head_size,
            transcendentals=flat * width,
        ),
        name="attend",
    )(span, query_flat, *places, *pieces)


def stages_of(contexts):
    bits = []
    bit = contexts // 2
    while bit >= 1:
        bits.append(bit)
        bit //= 2
    return bits


def after(value, *earlier):
    return lax.optimization_barrier((value, *earlier))[0]


def make_local(contexts, shards, plan):
    def local(tokens, queries, key_weight, value_weight):
        rows = tokens.shape[0]
        depth, head_size = key_weight.shape
        heads = queries.shape[1] // head_size
        group_rows = shards * rows
        context = lax.axis_index("ctx")
        shard = lax.axis_index("fsdp")
        unit = rows // sum(sum(part) for part in plan)
        stages = stages_of(contexts)

        def cut(chunk, *earlier):
            top, count = chunk
            source = after(tokens, *earlier) if earlier else tokens
            return [
                lax.dynamic_slice(
                    source,
                    (jnp.int32(top), lax.rem(shard + step, shards) * depth),
                    (count, depth),
                )
                for step in range(1, shards)
            ]

        def send(columns, *earlier):
            return [
                lax.ppermute(
                    after(columns[step - 1], *earlier) if earlier else columns[step - 1],
                    "fsdp",
                    [(i, (i + step) % shards) for i in range(shards)],
                )
                for step in range(1, shards)
            ]

        def places_of(top, count):
            turns = jnp.arange(shards, dtype=jnp.int32) * rows + top
            return (turns[:, None] + jnp.arange(count, dtype=jnp.int32)[None, :]).reshape(-1)

        class Part:
            pass

        parts = []
        chunks = []
        top = 0
        for sizes in plan:
            part = Part()
            part.top = top
            part.rows = sum(sizes) * unit
            part.first = len(chunks)
            for size in sizes:
                chunks.append((top, size * unit))
                top += size * unit
            part.end = len(chunks)
            part.stage = 0
            parts.append(part)
        early, late = parts

        flying = []
        sent = ()
        for chunk in chunks[: early.end + 1]:
            sent = cut(chunk, *sent)
            flying.append(send(sent))
        kept = []
        for chunk in chunks[early.end + 1 :]:
            sent = cut(chunk, *sent)
            kept.append(sent)

        def project(columns):
            return jnp.concatenate(
                [
                    jnp.dot(columns, weight, preferred_element_type=jnp.float32)
                    for weight in (key_weight, value_weight)
                ],
                axis=1,
            )

        own_columns = lax.dynamic_slice_in_dim(after(tokens, *sent), shard * depth, depth, 1)
        own_product = project(own_columns)

        start = context * group_rows
        first = start + shard * rows
        early.tables = tables(start + places_of(early.top, early.rows), head_size)
        own_product, early.tables, kept = lax.optimization_barrier(
            (own_product, early.tables, kept)
        )

        def exchange(part, gate):
            arrived = []
            for number in range(part.first, part.end):
                chunk, gate = lax.optimization_barrier((flying[number], gate))
                gate = [project(columns) for columns in chunk]
                arrived.append(gate)
            products = [own_product[part.top : part.top + part.rows]] + [
                jnp.concatenate([chunk[step] for chunk in arrived], axis=0)
                for step in range(shards - 1)
            ]
            if shards == 2:
                sums = jnp.concatenate(
                    [
                        jnp.where(shard == 0, products[0], products[1]),
                        jnp.where(shard == 0, products[1], products[0]),
                    ],
                    axis=0,
                )
            else:
                sums = jnp.zeros((shards * part.rows, 2 * head_size), jnp.float32)
                for step in range(shards):
                    source = lax.rem(shard + shards - step, shards)
                    sums = lax.dynamic_update_slice_in_dim(
                        sums, products[step], source * part.rows, 0
                    )
            part.sums = after(sums)
            part.other = jnp.zeros_like(sums)
            reach = 1
            while reach < shards:
                if reach > 1:
                    part.sums = part.sums + part.other
                part.other = lax.ppermute(
                    part.sums, "fsdp", [(i, i ^ reach) for i in range(shards)]
                )
                reach *= 2

        def combine(part, *gate):
            own, other = lax.optimization_barrier((part.sums, part.other, *gate))[:2]
            sums = own + other
            keys_rot = rotate(sums[:, :head_size], *part.tables).astype(jnp.bfloat16)
            block = after(
                jnp.concatenate([keys_rot, sums[:, head_size:].astype(jnp.bfloat16)], axis=1)
            )
            part.cache = lax.dynamic_slice_in_dim(block, shard * part.rows, part.rows, 0)
            part.known, part.fresh, part.masks = block, [], [0]

        def advance(part, *gate):
            fresh = lax.optimization_barrier((part.known, part.fresh, *gate))
            part.known = after(jnp.concatenate([fresh[0]] + list(fresh[1]), axis=0))
            part.fresh = []
            if part.stage < len(stages):
                bit = stages[part.stage]
                pairs = [(i, i ^ bit) for i in range(contexts)]
                part.fresh = [lax.ppermute(part.known, "ctx", pairs)]
                part.masks = part.masks + [mask ^ bit for mask in part.masks]
            part.stage += 1

        exchange(early, own_product)
        for columns in kept:
            flying.append(send(columns, early.sums))
        raw_queries, first = lax.optimization_barrier((queries, first, early.sums))[:2]
        own_cosine, own_sine = tables(first + jnp.arange(rows, dtype=jnp.int32), head_size)
        by_head = raw_queries.astype(jnp.float32).reshape(rows, heads, head_size)
        query_flat = (
            rotate(by_head.transpose(1, 0, 2), own_cosine[None], own_sine[None])
            .astype(jnp.bfloat16)
            .reshape(heads * rows, head_size)
        )
        base = first - shard * rows
        late.tables = tables(base + places_of(late.top, late.rows), head_size)
        top_bit = stages[0]
        upper = ((context & top_bit) != 0).astype(jnp.int32)
        span = jnp.stack([base, first, upper]).astype(jnp.int32)
        all_masks = [0]
        for bit in stages:
            all_masks = all_masks + [mask ^ bit for mask in all_masks]
        slots = tuple(sorted(range(contexts), key=lambda slot: all_masks[slot] & top_bit))
        turns = jnp.array([all_masks[slot] for slot in slots], jnp.int32)
        sources = (context ^ turns)[:, None] * group_rows
        query_flat, late.tables, span = lax.optimization_barrier((query_flat, late.tables, span))
        exchange(late, query_flat)
        combine(early, late.sums)
        advance(early)
        combine(late, early.known)
        advance(late)
        for stage in range(1, len(stages)):
            advance(early, late.known)
            advance(late, early.known)
        places = [
            (sources + places_of(part.top, part.rows)[None, :]).reshape(1, -1) for part in parts
        ]
        pieces = [early.known] + early.fresh + [late.known] + late.fresh
        owns = tuple(shards * part.rows for part in parts)
        attended = attend(span, places, query_flat, pieces, slots, owns, rows)
        kv_cache = jnp.concatenate([part.cache for part in parts], axis=0)
        return (kv_cache, attended)

    return local


def solution(mesh):
    placed = (P(("ctx", "fsdp"), None), P(("ctx", "fsdp"), None), P("fsdp", None), P("fsdp", None))
    return jax.shard_map(
        make_local(mesh.shape["ctx"], mesh.shape["fsdp"], ((1, 4), (2, 1))),
        mesh=mesh,
        in_specs=placed,
        out_specs=(P(("ctx", "fsdp"), None), P(("ctx", "fsdp"), None)),
        check_vma=False,
    )
```

```python
from functools import partial
import math

import jax
import jax.numpy as jnp
from jax import lax
from jax.experimental import pallas as pl
from jax.experimental.pallas import tpu as pltpu
from jax.sharding import PartitionSpec as P

rope_base = 500000.0
floor_value = -1e30


def rotate(vectors, cosine, sine_table):
    middle = vectors.shape[-1] // 2
    leading = vectors[..., :middle]
    back_half = vectors[..., middle:]
    return jnp.concatenate(
        [leading * cosine - back_half * sine_table, back_half * cosine + leading * sine_table],
        axis=-1,
    )


def tables(positions, head_size):
    middle = head_size // 2
    frequency = rope_base ** (-jnp.arange(middle, dtype=jnp.float32) * 2.0 / head_size)
    angles = positions.astype(jnp.float32)[:, None] * frequency[None, :]
    return (jnp.cos(angles), jnp.sin(angles))


def attention_kernel(
    span_ref, query_ref, *refs, count, slots, owns, rows, head_size, stride
):
    places, refs = refs[:count], refs[count:]
    pieces, (out_ref, scratch) = refs[: 2 * count], refs[2 * count :]
    start = span_ref[0]
    first = span_ref[1]
    factor = head_size ** (-0.5) * math.log2(math.e)
    flat = query_ref.shape[0]
    middle = len(slots) // 2
    sorted_parts = []
    for number in range(count):
        size = pieces[2 * number].shape[0] // middle
        blocks = []
        for slot in slots:
            top = (slot % middle) * size
            blocks.append(pieces[2 * number + slot // middle][top : top + size, :])
        sorted_parts.append(jnp.concatenate(blocks, axis=0))

    def run(share):
        chosen = [part[: part.shape[0] // share, :] for part in sorted_parts]
        everything = jnp.concatenate(chosen, axis=0)
        keys = everything[:, :head_size]
        values = everything[:, head_size:]
        segments = []
        top = 0
        for part, place_ref, own in zip(chosen, places, owns):
            width = part.shape[0]
            edge = min(width, -(-own // 128) * 128)
            query_pos = first + lax.rem(
                lax.broadcasted_iota(jnp.int32, (stride, edge), 0), jnp.int32(rows)
            )
            diagonal = place_ref[:, :edge] <= query_pos
            bias = jnp.where(place_ref[:, edge:width] < start, 0.0, floor_value)
            segments.append((top, edge, width, diagonal, bias.astype(jnp.float32)))
            top += width

        def one(turn):
            place = pl.ds(pl.multiple_of(turn * stride, stride), stride)
            scores = (
                lax.dot_general(
                    query_ref[place, :],
                    keys,
                    (((1,), (1,)), ((), ())),
                    preferred_element_type=jnp.float32,
                )
                * factor
            )
            masked = []
            for top, edge, width, diagonal, bias in segments:
                masked.append(jnp.where(diagonal, scores[:, top : top + edge], floor_value))
                if edge < width:
                    masked.append(scores[:, top + edge : top + width] + bias)
            masked = jnp.concatenate(masked, axis=1)
            peak = jnp.max(masked, axis=1, keepdims=True)
            weights = jnp.exp2(masked - peak)
            total = jnp.sum(weights, axis=1, keepdims=True)
            numerator = jnp.dot(
                weights.astype(jnp.bfloat16), values, preferred_element_type=jnp.float32
            )
            scratch[place, :] = (numerator / total).astype(jnp.bfloat16)

        if flat // stride <= 8:
            for turn in range(flat // stride):
                one(turn)
        else:

            @pl.loop(0, flat // stride)
            def each(turn):
                one(turn)

    upper = span_ref[2]

    @pl.when(upper == 1)
    def all_keys():
        run(1)

    @pl.when(upper == 0)
    def lower_keys():
        run(2)

    for head in range(flat // rows):
        out_ref[:, head * head_size : (head + 1) * head_size] = scratch[
            head * rows : (head + 1) * rows, :
        ]


def attend(span, places, query_flat, pieces, slots, owns, rows):
    flat, head_size = query_flat.shape
    width = sum(piece.shape[0] for piece in pieces)
    stride = math.gcd(flat, 256 if width <= 2048 else rows)
    whole = pl.BlockSpec(memory_space=pltpu.VMEM)
    return pl.pallas_call(
        partial(
            attention_kernel,
            count=len(places),
            slots=slots,
            owns=owns,
            rows=rows,
            head_size=head_size,
            stride=stride,
        ),
        out_shape=jax.ShapeDtypeStruct((rows, flat // rows * head_size), jnp.bfloat16),
        in_specs=[pl.BlockSpec(memory_space=pltpu.SMEM)]
        + [whole] * (1 + len(places) + len(pieces)),
        out_specs=whole,
        scratch_shapes=[pltpu.VMEM((flat, head_size), jnp.bfloat16)],
        compiler_params=pltpu.CompilerParams(vmem_limit_bytes=24 * 1024 * 1024),
        cost_estimate=pl.CostEstimate(
            flops=4 * flat * width * head_size,
            bytes_accessed=4 * flat * head_size + 4 * width * head_size,
            transcendentals=flat * width,
        ),
        name="attend",
    )(span, query_flat, *places, *pieces)


def stages_of(contexts):
    bits = []
    bit = contexts // 2
    while bit >= 1:
        bits.append(bit)
        bit //= 2
    return bits


def after(value, *earlier):
    return lax.optimization_barrier((value, *earlier))[0]


def make_local(contexts, shards, plan):
    def local(tokens, queries, key_weight, value_weight):
        rows = tokens.shape[0]
        depth, head_size = key_weight.shape
        heads = queries.shape[1] // head_size
        group_rows = shards * rows
        context = lax.axis_index("ctx")
        shard = lax.axis_index("fsdp")
        unit = rows // sum(sum(part) for part in plan)
        stages = stages_of(contexts)

        def cut(chunk, *earlier):
            top, count = chunk
            source = after(tokens, *earlier) if earlier else tokens
            return [
                lax.dynamic_slice(
                    source,
                    (jnp.int32(top), lax.rem(shard + step, shards) * depth),
                    (count, depth),
                )
                for step in range(1, shards)
            ]

        def send(columns, *earlier):
            return [
                lax.ppermute(
                    after(columns[step - 1], *earlier) if earlier else columns[step - 1],
                    "fsdp",
                    [(i, (i + step) % shards) for i in range(shards)],
                )
                for step in range(1, shards)
            ]

        def places_of(top, count):
            turns = jnp.arange(shards, dtype=jnp.int32) * rows + top
            return (turns[:, None] + jnp.arange(count, dtype=jnp.int32)[None, :]).reshape(-1)

        class Part:
            pass

        parts = []
        chunks = []
        top = 0
        for sizes in plan:
            part = Part()
            part.top = top
            part.rows = sum(sizes) * unit
            part.first = len(chunks)
            for size in sizes:
                chunks.append((top, size * unit))
                top += size * unit
            part.end = len(chunks)
            part.stage = 0
            parts.append(part)
        early, late = parts

        flying = []
        sent = ()
        for chunk in chunks[: early.end + 1]:
            sent = cut(chunk, *sent)
            flying.append(send(sent))
        kept = []
        for chunk in chunks[early.end + 1 :]:
            sent = cut(chunk, *sent)
            kept.append(sent)

        def project(columns):
            return jnp.concatenate(
                [
                    jnp.dot(columns, weight, preferred_element_type=jnp.float32)
                    for weight in (key_weight, value_weight)
                ],
                axis=1,
            )

        own_columns = lax.dynamic_slice_in_dim(after(tokens, *sent), shard * depth, depth, 1)
        own_product = project(own_columns)

        start = context * group_rows
        first = start + shard * rows
        own_product, kept = lax.optimization_barrier((own_product, kept))

        def exchange(part, gate):
            arrived = []
            for number in range(part.first, part.end):
                chunk, gate = lax.optimization_barrier((flying[number], gate))
                gate = [project(columns) for columns in chunk]
                arrived.append(gate)
            products = [own_product[part.top : part.top + part.rows]] + [
                jnp.concatenate([chunk[step] for chunk in arrived], axis=0)
                for step in range(shards - 1)
            ]
            if shards == 2:
                sums = jnp.concatenate(
                    [
                        jnp.where(shard == 0, products[0], products[1]),
                        jnp.where(shard == 0, products[1], products[0]),
                    ],
                    axis=0,
                )
            else:
                sums = jnp.zeros((shards * part.rows, 2 * head_size), jnp.float32)
                for step in range(shards):
                    source = lax.rem(shard + shards - step, shards)
                    sums = lax.dynamic_update_slice_in_dim(
                        sums, products[step], source * part.rows, 0
                    )
            part.sums = after(sums)
            part.other = jnp.zeros_like(sums)
            reach = 1
            while reach < shards:
                if reach > 1:
                    part.sums = part.sums + part.other
                part.other = lax.ppermute(
                    part.sums, "fsdp", [(i, i ^ reach) for i in range(shards)]
                )
                reach *= 2

        def combine(part, *gate):
            own, other = lax.optimization_barrier((part.sums, part.other, *gate))[:2]
            sums = own + other
            keys_rot = rotate(sums[:, :head_size], *part.tables).astype(jnp.bfloat16)
            block = after(
                jnp.concatenate([keys_rot, sums[:, head_size:].astype(jnp.bfloat16)], axis=1)
            )
            part.cache = lax.dynamic_slice_in_dim(block, shard * part.rows, part.rows, 0)
            part.known, part.fresh, part.masks = block, [], [0]

        def advance(part, *gate):
            fresh = lax.optimization_barrier((part.known, part.fresh, *gate))
            part.known = after(jnp.concatenate([fresh[0]] + list(fresh[1]), axis=0))
            part.fresh = []
            if part.stage < len(stages):
                bit = stages[part.stage]
                pairs = [(i, i ^ bit) for i in range(contexts)]
                part.fresh = [lax.ppermute(part.known, "ctx", pairs)]
                part.masks = part.masks + [mask ^ bit for mask in part.masks]
            part.stage += 1

        exchange(early, own_product)
        for columns in kept:
            flying.append(send(columns, early.sums))
        raw_queries, first = lax.optimization_barrier((queries, first, early.sums))[:2]
        own_cosine, own_sine = tables(first + jnp.arange(rows, dtype=jnp.int32), head_size)
        by_head = raw_queries.astype(jnp.float32).reshape(rows, heads, head_size)
        query_flat = (
            rotate(by_head.transpose(1, 0, 2), own_cosine[None], own_sine[None])
            .astype(jnp.bfloat16)
            .reshape(heads * rows, head_size)
        )
        base = first - shard * rows
        early.tables = tables(base + places_of(early.top, early.rows), head_size)
        late.tables = tables(base + places_of(late.top, late.rows), head_size)
        top_bit = stages[0]
        upper = ((context & top_bit) != 0).astype(jnp.int32)
        span = jnp.stack([base, first, upper]).astype(jnp.int32)
        all_masks = [0]
        for bit in stages:
            all_masks = all_masks + [mask ^ bit for mask in all_masks]
        slots = tuple(sorted(range(contexts), key=lambda slot: all_masks[slot] & top_bit))
        turns = jnp.array([all_masks[slot] for slot in slots], jnp.int32)
        query_flat, early.tables, late.tables, span = lax.optimization_barrier(
            (query_flat, early.tables, late.tables, span)
        )
        combine(early, query_flat, *flying[early.end])
        exchange(late, early.known)
        advance(early, late.sums)
        combine(late, early.known)
        advance(late)
        for stage in range(1, len(stages)):
            advance(early, late.known)
            advance(late, early.known)
        sources = (after(context, late.known) ^ turns)[:, None] * group_rows
        places = [
            (sources + places_of(part.top, part.rows)[None, :]).reshape(1, -1) for part in parts
        ]
        pieces = [early.known] + early.fresh + [late.known] + late.fresh
        owns = tuple(shards * part.rows for part in parts)
        attended = attend(span, places, query_flat, pieces, slots, owns, rows)
        kv_cache = jnp.concatenate([part.cache for part in parts], axis=0)
        return (kv_cache, attended)

    return local


def solution(mesh):
    placed = (P(("ctx", "fsdp"), None), P(("ctx", "fsdp"), None), P("fsdp", None), P("fsdp", None))
    return jax.shard_map(
        make_local(mesh.shape["ctx"], mesh.shape["fsdp"], ((1, 4), (2, 1))),
        mesh=mesh,
        in_specs=placed,
        out_specs=(P(("ctx", "fsdp"), None), P(("ctx", "fsdp"), None)),
        check_vma=False,
    )
```

```python
from functools import partial
import math

import jax
import jax.numpy as jnp
from jax import lax
from jax.experimental import pallas as pl
from jax.experimental.pallas import tpu as pltpu
from jax.sharding import PartitionSpec as P

rope_base = 500000.0
floor_value = -1e30


def rotate(vectors, cosine, sine_table):
    middle = vectors.shape[-1] // 2
    leading = vectors[..., :middle]
    back_half = vectors[..., middle:]
    return jnp.concatenate(
        [leading * cosine - back_half * sine_table, back_half * cosine + leading * sine_table],
        axis=-1,
    )


def tables(positions, head_size):
    middle = head_size // 2
    frequency = rope_base ** (-jnp.arange(middle, dtype=jnp.float32) * 2.0 / head_size)
    angles = positions.astype(jnp.float32)[:, None] * frequency[None, :]
    return (jnp.cos(angles), jnp.sin(angles))


def attention_kernel(
    span_ref, query_ref, *refs, count, slots, owns, rows, head_size, stride
):
    places, refs = refs[:count], refs[count:]
    pieces, (out_ref, scratch) = refs[: 2 * count], refs[2 * count :]
    start = span_ref[0]
    first = span_ref[1]
    factor = head_size ** (-0.5) * math.log2(math.e)
    flat = query_ref.shape[0]
    middle = len(slots) // 2
    sorted_parts = []
    for number in range(count):
        size = pieces[2 * number].shape[0] // middle
        blocks = []
        for slot in slots:
            top = (slot % middle) * size
            blocks.append(pieces[2 * number + slot // middle][top : top + size, :])
        sorted_parts.append(jnp.concatenate(blocks, axis=0))

    def run(share):
        chosen = [part[: part.shape[0] // share, :] for part in sorted_parts]
        everything = jnp.concatenate(chosen, axis=0)
        keys = everything[:, :head_size]
        values = everything[:, head_size:]
        segments = []
        top = 0
        for part, place_ref, own in zip(chosen, places, owns):
            width = part.shape[0]
            edge = min(width, -(-own // 128) * 128)
            query_pos = first + lax.rem(
                lax.broadcasted_iota(jnp.int32, (stride, edge), 0), jnp.int32(rows)
            )
            diagonal = place_ref[:, :edge] <= query_pos
            bias = jnp.where(place_ref[:, edge:width] < start, 0.0, floor_value)
            segments.append((top, edge, width, diagonal, bias.astype(jnp.float32)))
            top += width

        def one(turn):
            place = pl.ds(pl.multiple_of(turn * stride, stride), stride)
            scores = (
                lax.dot_general(
                    query_ref[place, :],
                    keys,
                    (((1,), (1,)), ((), ())),
                    preferred_element_type=jnp.float32,
                )
                * factor
            )
            masked = []
            for top, edge, width, diagonal, bias in segments:
                masked.append(jnp.where(diagonal, scores[:, top : top + edge], floor_value))
                if edge < width:
                    masked.append(scores[:, top + edge : top + width] + bias)
            masked = jnp.concatenate(masked, axis=1)
            peak = jnp.max(masked, axis=1, keepdims=True)
            weights = jnp.exp2(masked - peak)
            total = jnp.sum(weights, axis=1, keepdims=True)
            numerator = jnp.dot(
                weights.astype(jnp.bfloat16), values, preferred_element_type=jnp.float32
            )
            scratch[place, :] = (numerator / total).astype(jnp.bfloat16)

        if flat // stride <= 8:
            for turn in range(flat // stride):
                one(turn)
        else:

            @pl.loop(0, flat // stride)
            def each(turn):
                one(turn)

    upper = span_ref[2]

    @pl.when(upper == 1)
    def all_keys():
        run(1)

    @pl.when(upper == 0)
    def lower_keys():
        run(2)

    for head in range(flat // rows):
        out_ref[:, head * head_size : (head + 1) * head_size] = scratch[
            head * rows : (head + 1) * rows, :
        ]


def attend(span, places, query_flat, pieces, slots, owns, rows):
    flat, head_size = query_flat.shape
    width = sum(piece.shape[0] for piece in pieces)
    stride = math.gcd(flat, 256 if width <= 2048 else rows)
    whole = pl.BlockSpec(memory_space=pltpu.VMEM)
    return pl.pallas_call(
        partial(
            attention_kernel,
            count=len(places),
            slots=slots,
            owns=owns,
            rows=rows,
            head_size=head_size,
            stride=stride,
        ),
        out_shape=jax.ShapeDtypeStruct((rows, flat // rows * head_size), jnp.bfloat16),
        in_specs=[pl.BlockSpec(memory_space=pltpu.SMEM)]
        + [whole] * (1 + len(places) + len(pieces)),
        out_specs=whole,
        scratch_shapes=[pltpu.VMEM((flat, head_size), jnp.bfloat16)],
        compiler_params=pltpu.CompilerParams(vmem_limit_bytes=24 * 1024 * 1024),
        cost_estimate=pl.CostEstimate(
            flops=4 * flat * width * head_size,
            bytes_accessed=4 * flat * head_size + 4 * width * head_size,
            transcendentals=flat * width,
        ),
        name="attend",
    )(span, query_flat, *places, *pieces)


def stages_of(contexts):
    bits = []
    bit = contexts // 2
    while bit >= 1:
        bits.append(bit)
        bit //= 2
    return bits


def after(value, *earlier):
    return lax.optimization_barrier((value, *earlier))[0]


def make_local(contexts, shards, plan):
    def local(tokens, queries, key_weight, value_weight):
        rows = tokens.shape[0]
        depth, head_size = key_weight.shape
        heads = queries.shape[1] // head_size
        group_rows = shards * rows
        context = lax.axis_index("ctx")
        shard = lax.axis_index("fsdp")
        unit = rows // sum(sum(part) for part in plan)
        stages = stages_of(contexts)

        def cut(chunk, *earlier):
            top, count = chunk
            source = after(tokens, *earlier) if earlier else tokens
            return [
                lax.dynamic_slice(
                    source,
                    (jnp.int32(top), lax.rem(shard + step, shards) * depth),
                    (count, depth),
                )
                for step in range(1, shards)
            ]

        def send(columns, *earlier):
            return [
                lax.ppermute(
                    after(columns[step - 1], *earlier) if earlier else columns[step - 1],
                    "fsdp",
                    [(i, (i + step) % shards) for i in range(shards)],
                )
                for step in range(1, shards)
            ]

        def places_of(top, count):
            turns = jnp.arange(shards, dtype=jnp.int32) * rows + top
            return (turns[:, None] + jnp.arange(count, dtype=jnp.int32)[None, :]).reshape(-1)

        class Part:
            pass

        parts = []
        chunks = []
        top = 0
        for sizes in plan:
            part = Part()
            part.top = top
            part.rows = sum(sizes) * unit
            part.first = len(chunks)
            for size in sizes:
                chunks.append((top, size * unit))
                top += size * unit
            part.end = len(chunks)
            part.stage = 0
            parts.append(part)
        early, late = parts

        flying = []
        sent = ()
        for chunk in chunks[: early.end + 1]:
            sent = cut(chunk, *sent)
            flying.append(send(sent))
        kept = []
        for chunk in chunks[early.end + 1 :]:
            sent = cut(chunk, *sent)
            kept.append(sent)

        def project(columns):
            return jnp.concatenate(
                [
                    jnp.dot(columns, weight, preferred_element_type=jnp.float32)
                    for weight in (key_weight, value_weight)
                ],
                axis=1,
            )

        own_columns = lax.dynamic_slice_in_dim(after(tokens, *sent), shard * depth, depth, 1)
        own_product = project(own_columns)

        start = context * group_rows
        first = start + shard * rows
        own_product, kept = lax.optimization_barrier((own_product, kept))

        def exchange(part, own, arrived, gate):
            for number in range(part.first + len(arrived), part.end):
                chunk, gate = lax.optimization_barrier((flying[number], gate))
                gate = [project(columns) for columns in chunk]
                arrived.append(gate)
            products = [own] + [
                jnp.concatenate([chunk[step] for chunk in arrived], axis=0)
                for step in range(shards - 1)
            ]
            if shards == 2:
                sums = jnp.concatenate(
                    [
                        jnp.where(shard == 0, products[0], products[1]),
                        jnp.where(shard == 0, products[1], products[0]),
                    ],
                    axis=0,
                )
            else:
                sums = jnp.zeros((shards * part.rows, 2 * head_size), jnp.float32)
                for step in range(shards):
                    source = lax.rem(shard + shards - step, shards)
                    sums = lax.dynamic_update_slice_in_dim(
                        sums, products[step], source * part.rows, 0
                    )
            part.sums = after(sums)
            part.other = jnp.zeros_like(sums)
            reach = 1
            while reach < shards:
                if reach > 1:
                    part.sums = part.sums + part.other
                part.other = lax.ppermute(
                    part.sums, "fsdp", [(i, i ^ reach) for i in range(shards)]
                )
                reach *= 2

        def combine(part, *gate):
            own, other = lax.optimization_barrier((part.sums, part.other, *gate))[:2]
            sums = own + other
            keys_rot = rotate(sums[:, :head_size], *part.tables).astype(jnp.bfloat16)
            block = after(
                jnp.concatenate([keys_rot, sums[:, head_size:].astype(jnp.bfloat16)], axis=1)
            )
            part.cache = lax.dynamic_slice_in_dim(block, shard * part.rows, part.rows, 0)
            part.known, part.fresh, part.masks = block, [], [0]

        def advance(part, *gate):
            fresh = lax.optimization_barrier((part.known, part.fresh, *gate))
            part.known = after(jnp.concatenate([fresh[0]] + list(fresh[1]), axis=0))
            part.fresh = []
            if part.stage < len(stages):
                bit = stages[part.stage]
                pairs = [(i, i ^ bit) for i in range(contexts)]
                part.fresh = [lax.ppermute(part.known, "ctx", pairs)]
                part.masks = part.masks + [mask ^ bit for mask in part.masks]
            part.stage += 1

        early_own, late_own = own_product[: late.top], own_product[late.top :]
        exchange(early, early_own, [], own_product)
        for columns in kept:
            flying.append(send(columns, early.sums))
        raw_queries, first = lax.optimization_barrier((queries, first, early.sums))[:2]
        own_cosine, own_sine = tables(first + jnp.arange(rows, dtype=jnp.int32), head_size)
        by_head = raw_queries.astype(jnp.float32).reshape(rows, heads, head_size)
        query_flat = (
            rotate(by_head.transpose(1, 0, 2), own_cosine[None], own_sine[None])
            .astype(jnp.bfloat16)
            .reshape(heads * rows, head_size)
        )
        base = first - shard * rows
        early.tables = tables(base + places_of(early.top, early.rows), head_size)
        late.tables = tables(base + places_of(late.top, late.rows), head_size)
        top_bit = stages[0]
        upper = ((context & top_bit) != 0).astype(jnp.int32)
        span = jnp.stack([base, first, upper]).astype(jnp.int32)
        all_masks = [0]
        for bit in stages:
            all_masks = all_masks + [mask ^ bit for mask in all_masks]
        slots = tuple(sorted(range(contexts), key=lambda slot: all_masks[slot] & top_bit))
        turns = jnp.array([all_masks[slot] for slot in slots], jnp.int32)
        late_own = after(late_own, early.sums)
        query_flat, early.tables, late.tables, span, late_own = lax.optimization_barrier(
            (query_flat, early.tables, late.tables, span, late_own)
        )
        combine(early, query_flat, *flying[early.end])
        exchange(late, late_own, [], early.known)
        advance(early, late.sums)
        combine(late, early.known)
        advance(late)
        for stage in range(1, len(stages)):
            advance(early, late.known)
            advance(late, early.known)
        sources = (after(context, late.known) ^ turns)[:, None] * group_rows
        places = [
            (sources + places_of(part.top, part.rows)[None, :]).reshape(1, -1) for part in parts
        ]
        pieces = [early.known] + early.fresh + [late.known] + late.fresh
        owns = tuple(shards * part.rows for part in parts)
        attended = attend(span, places, query_flat, pieces, slots, owns, rows)
        kv_cache = jnp.concatenate([part.cache for part in parts], axis=0)
        return (kv_cache, attended)

    return local


def solution(mesh):
    placed = (P(("ctx", "fsdp"), None), P(("ctx", "fsdp"), None), P("fsdp", None), P("fsdp", None))
    return jax.shard_map(
        make_local(mesh.shape["ctx"], mesh.shape["fsdp"], ((1, 4), (2, 1))),
        mesh=mesh,
        in_specs=placed,
        out_specs=(P(("ctx", "fsdp"), None), P(("ctx", "fsdp"), None)),
        check_vma=False,
    )
```

```python
from functools import partial
import math

import jax
import jax.numpy as jnp
from jax import lax
from jax.experimental import pallas as pl
from jax.experimental.pallas import tpu as pltpu
from jax.sharding import PartitionSpec as P

rope_base = 500000.0
floor_value = -1e30


def rotate(vectors, cosine, sine_table):
    middle = vectors.shape[-1] // 2
    leading = vectors[..., :middle]
    back_half = vectors[..., middle:]
    return jnp.concatenate(
        [leading * cosine - back_half * sine_table, back_half * cosine + leading * sine_table],
        axis=-1,
    )


def tables(positions, head_size):
    middle = head_size // 2
    frequency = rope_base ** (-jnp.arange(middle, dtype=jnp.float32) * 2.0 / head_size)
    angles = positions.astype(jnp.float32)[:, None] * frequency[None, :]
    return (jnp.cos(angles), jnp.sin(angles))


def attention_kernel(
    span_ref, query_ref, *refs, count, slots, owns, rows, head_size, stride
):
    places, refs = refs[:count], refs[count:]
    pieces, out_ref = refs[: 2 * count], refs[2 * count]
    start = span_ref[0]
    first = span_ref[1]
    factor = head_size ** (-0.5) * math.log2(math.e)
    flat = query_ref.shape[0]
    middle = len(slots) // 2
    sorted_parts = []
    for number in range(count):
        size = pieces[2 * number].shape[0] // middle
        blocks = []
        for slot in slots:
            top = (slot % middle) * size
            blocks.append(pieces[2 * number + slot // middle][top : top + size, :])
        sorted_parts.append(jnp.concatenate(blocks, axis=0))

    def run(share):
        chosen = [part[: part.shape[0] // share, :] for part in sorted_parts]
        everything = jnp.concatenate(chosen, axis=0)
        keys = everything[:, :head_size]
        values = everything[:, head_size:]
        segments = []
        top = 0
        for part, place_ref, own in zip(chosen, places, owns):
            width = part.shape[0]
            edge = min(width, -(-own // 128) * 128)
            query_pos = first + lax.rem(
                lax.broadcasted_iota(jnp.int32, (stride, edge), 0), jnp.int32(rows)
            )
            diagonal = place_ref[:, :edge] <= query_pos
            bias = jnp.where(place_ref[:, edge:width] < start, 0.0, floor_value)
            segments.append((top, edge, width, diagonal, bias.astype(jnp.float32)))
            top += width

        def one(turn):
            place = pl.ds(pl.multiple_of(turn * stride, stride), stride)
            scores = (
                lax.dot_general(
                    query_ref[place, :],
                    keys,
                    (((1,), (1,)), ((), ())),
                    preferred_element_type=jnp.float32,
                )
                * factor
            )
            masked = []
            for top, edge, width, diagonal, bias in segments:
                masked.append(jnp.where(diagonal, scores[:, top : top + edge], floor_value))
                if edge < width:
                    masked.append(scores[:, top + edge : top + width] + bias)
            masked = jnp.concatenate(masked, axis=1)
            peak = jnp.max(masked, axis=1, keepdims=True)
            weights = jnp.exp2(masked - peak)
            total = jnp.sum(weights, axis=1, keepdims=True)
            numerator = jnp.dot(
                weights.astype(jnp.bfloat16), values, preferred_element_type=jnp.float32
            )
            result = (numerator * (1.0 / total)).astype(out_ref.dtype)
            for head in range(stride // rows):
                column = (turn * (stride // rows) + head) * head_size
                out_ref[:, pl.ds(pl.multiple_of(column, head_size), head_size)] = result[
                    head * rows : (head + 1) * rows, :
                ]

        if flat // stride <= 8:
            for turn in range(flat // stride):
                one(turn)
        else:

            @pl.loop(0, flat // stride)
            def each(turn):
                one(turn)

    upper = span_ref[2]

    @pl.when(upper == 1)
    def all_keys():
        run(1)

    @pl.when(upper == 0)
    def lower_keys():
        run(2)


def attend(span, places, query_flat, pieces, slots, owns, rows):
    flat, head_size = query_flat.shape
    width = sum(piece.shape[0] for piece in pieces)
    stride = math.gcd(flat, 256 if width <= 2048 else rows)
    whole = pl.BlockSpec(memory_space=pltpu.VMEM)
    return pl.pallas_call(
        partial(
            attention_kernel,
            count=len(places),
            slots=slots,
            owns=owns,
            rows=rows,
            head_size=head_size,
            stride=stride,
        ),
        out_shape=jax.ShapeDtypeStruct((rows, flat // rows * head_size), jnp.bfloat16),
        in_specs=[pl.BlockSpec(memory_space=pltpu.SMEM)]
        + [whole] * (1 + len(places) + len(pieces)),
        out_specs=whole,
        compiler_params=pltpu.CompilerParams(vmem_limit_bytes=24 * 1024 * 1024),
        cost_estimate=pl.CostEstimate(
            flops=4 * flat * width * head_size,
            bytes_accessed=4 * flat * head_size + 4 * width * head_size,
            transcendentals=flat * width,
        ),
        name="attend",
    )(span, query_flat, *places, *pieces)


def stages_of(contexts):
    bits = []
    bit = contexts // 2
    while bit >= 1:
        bits.append(bit)
        bit //= 2
    return bits


def after(value, *earlier):
    return lax.optimization_barrier((value, *earlier))[0]


def make_local(contexts, shards, plan):
    def local(tokens, queries, key_weight, value_weight):
        rows = tokens.shape[0]
        depth, head_size = key_weight.shape
        heads = queries.shape[1] // head_size
        group_rows = shards * rows
        context = lax.axis_index("ctx")
        shard = lax.axis_index("fsdp")
        unit = rows // sum(sum(part) for part in plan)
        stages = stages_of(contexts)

        def cut(chunk, *earlier):
            top, count = chunk
            source = after(tokens, *earlier) if earlier else tokens
            return [
                lax.dynamic_slice(
                    source,
                    (jnp.int32(top), lax.rem(shard + step, shards) * depth),
                    (count, depth),
                )
                for step in range(1, shards)
            ]

        def send(columns, *earlier):
            return [
                lax.ppermute(
                    after(columns[step - 1], *earlier) if earlier else columns[step - 1],
                    "fsdp",
                    [(i, (i + step) % shards) for i in range(shards)],
                )
                for step in range(1, shards)
            ]

        def places_of(top, count):
            turns = jnp.arange(shards, dtype=jnp.int32) * rows + top
            return (turns[:, None] + jnp.arange(count, dtype=jnp.int32)[None, :]).reshape(-1)

        class Part:
            pass

        parts = []
        chunks = []
        top = 0
        for sizes in plan:
            part = Part()
            part.top = top
            part.rows = sum(sizes) * unit
            part.first = len(chunks)
            for size in sizes:
                chunks.append((top, size * unit))
                top += size * unit
            part.end = len(chunks)
            part.stage = 0
            parts.append(part)
        early, late = parts

        flying = []
        sent = ()
        for chunk in chunks[: early.end + 1]:
            sent = cut(chunk, *sent)
            flying.append(send(sent))
        kept = []
        for chunk in chunks[early.end + 1 :]:
            sent = cut(chunk, *sent)
            kept.append(sent)

        def project(columns):
            return jnp.concatenate(
                [
                    jnp.dot(columns, weight, preferred_element_type=jnp.float32)
                    for weight in (key_weight, value_weight)
                ],
                axis=1,
            )

        own_columns = lax.dynamic_slice_in_dim(after(tokens, *sent), shard * depth, depth, 1)
        own_product = project(own_columns)

        start = context * group_rows
        first = start + shard * rows
        own_product, kept = lax.optimization_barrier((own_product, kept))

        def exchange(part, own, arrived, gate):
            for number in range(part.first + len(arrived), part.end):
                chunk, gate = lax.optimization_barrier((flying[number], gate))
                gate = [project(columns) for columns in chunk]
                arrived.append(gate)
            products = [own] + [
                jnp.concatenate([chunk[step] for chunk in arrived], axis=0)
                for step in range(shards - 1)
            ]
            if shards == 2:
                sums = jnp.concatenate(
                    [
                        jnp.where(shard == 0, products[0], products[1]),
                        jnp.where(shard == 0, products[1], products[0]),
                    ],
                    axis=0,
                )
            else:
                sums = jnp.zeros((shards * part.rows, 2 * head_size), jnp.float32)
                for step in range(shards):
                    source = lax.rem(shard + shards - step, shards)
                    sums = lax.dynamic_update_slice_in_dim(
                        sums, products[step], source * part.rows, 0
                    )
            part.sums = after(sums)
            part.other = jnp.zeros_like(sums)
            reach = 1
            while reach < shards:
                if reach > 1:
                    part.sums = part.sums + part.other
                part.other = lax.ppermute(
                    part.sums, "fsdp", [(i, i ^ reach) for i in range(shards)]
                )
                reach *= 2

        def combine(part, *gate):
            own, other = lax.optimization_barrier((part.sums, part.other, *gate))[:2]
            sums = own + other
            keys_rot = rotate(sums[:, :head_size], *part.tables).astype(jnp.bfloat16)
            block = after(
                jnp.concatenate([keys_rot, sums[:, head_size:].astype(jnp.bfloat16)], axis=1)
            )
            part.cache = lax.dynamic_slice_in_dim(block, shard * part.rows, part.rows, 0)
            part.known, part.fresh, part.masks = block, [], [0]

        def advance(part, *gate):
            fresh = lax.optimization_barrier((part.known, part.fresh, *gate))
            part.known = after(jnp.concatenate([fresh[0]] + list(fresh[1]), axis=0))
            part.fresh = []
            if part.stage < len(stages):
                bit = stages[part.stage]
                pairs = [(i, i ^ bit) for i in range(contexts)]
                part.fresh = [lax.ppermute(part.known, "ctx", pairs)]
                part.masks = part.masks + [mask ^ bit for mask in part.masks]
            part.stage += 1

        early_own, late_own = own_product[: late.top], own_product[late.top :]
        exchange(early, early_own, [], own_product)
        for columns in kept:
            flying.append(send(columns, early.sums))
        raw_queries, first = lax.optimization_barrier((queries, first, early.sums))[:2]
        own_cosine, own_sine = tables(first + jnp.arange(rows, dtype=jnp.int32), head_size)
        by_head = raw_queries.astype(jnp.float32).reshape(rows, heads, head_size)
        query_flat = (
            rotate(by_head.transpose(1, 0, 2), own_cosine[None], own_sine[None])
            .astype(jnp.bfloat16)
            .reshape(heads * rows, head_size)
        )
        base = first - shard * rows
        early.tables = tables(base + places_of(early.top, early.rows), head_size)
        late.tables = tables(base + places_of(late.top, late.rows), head_size)
        top_bit = stages[0]
        upper = ((context & top_bit) != 0).astype(jnp.int32)
        span = jnp.stack([base, first, upper]).astype(jnp.int32)
        all_masks = [0]
        for bit in stages:
            all_masks = all_masks + [mask ^ bit for mask in all_masks]
        slots = tuple(sorted(range(contexts), key=lambda slot: all_masks[slot] & top_bit))
        turns = jnp.array([all_masks[slot] for slot in slots], jnp.int32)
        late_own = after(late_own, early.sums)
        query_flat, early.tables, late.tables, span, late_own = lax.optimization_barrier(
            (query_flat, early.tables, late.tables, span, late_own)
        )
        combine(early, query_flat, *flying[early.end])
        exchange(late, late_own, [], early.known)
        advance(early, late.sums)
        combine(late, early.known)
        advance(late)
        for stage in range(1, len(stages)):
            advance(early, late.known)
            advance(late, early.known)
        sources = (after(context, late.known) ^ turns)[:, None] * group_rows
        places = [
            (sources + places_of(part.top, part.rows)[None, :]).reshape(1, -1) for part in parts
        ]
        pieces = [early.known] + early.fresh + [late.known] + late.fresh
        owns = tuple(shards * part.rows for part in parts)
        attended = attend(span, places, query_flat, pieces, slots, owns, rows)
        kv_cache = jnp.concatenate([part.cache for part in parts], axis=0)
        return (kv_cache, attended)

    return local


def solution(mesh):
    placed = (P(("ctx", "fsdp"), None), P(("ctx", "fsdp"), None), P("fsdp", None), P("fsdp", None))
    return jax.shard_map(
        make_local(mesh.shape["ctx"], mesh.shape["fsdp"], ((1, 4), (2, 1))),
        mesh=mesh,
        in_specs=placed,
        out_specs=(P(("ctx", "fsdp"), None), P(("ctx", "fsdp"), None)),
        check_vma=False,
    )
```
